32 devices in a mesh: section: 2 (over x), tensor: 2 (over y), dp: 8 (over z, core).
Axes of the slice: x: 2, y: 2, z: 4, core: 2. Of those that a mesh axis runs over, the one named last changes fastest.
Arguments:
- embedded: float32 [2, 8, 2, 197, 768], P(None, 'dp', 'tensor'), may hold values from -6 to 6
- image_counts: int32 [8], P('dp'), may hold values from 2 to 4, as said below
- cotangent: float32 [2, 8, 2, 197, 768], P(None, 'dp', 'tensor'), may hold values from -6 to 6
- qkv_weight: float32 [2, 768, 3, 768], P('section', 'dp', None, 'tensor'), may hold values from -0.21875 to 0.21875
- qv_bias: float32 [2, 2, 768], P('section', None, ('tensor', 'dp')), may hold values from -1.2 to 1.2
- out_weight: float32 [2, 768, 768], P('section', 'tensor', 'dp'), may hold values from -1 to 1
- up_weight: float32 [2, 768, 3072], P('section', 'dp', 'tensor'), may hold values from -0.21875 to 0.21875
- up_bias: float32 [2, 3072], P('section', ('tensor', 'dp')), may hold values from -3 to 3
- down_weight: float32 [2, 3072, 768], P('section', 'tensor', 'dp'), may hold values from -0.109375 to 0.109375
- norm_gains: float32 [2, 2, 768], P('section', None, ('tensor', 'dp')), may hold values from 0.1 to 1.9
- shift_terms: float32 [2, 4, 768], P('section', None, ('tensor', 'dp')), may hold values from -3 to 3
Outputs:
- layer_outputs: float32 [2, 2, 8, 2, 197, 768], P('section', None, 'dp', 'tensor')
- input_grads: float32 [2, 2, 8, 2, 197, 768], P('section', None, 'dp', 'tensor')
- grad_qkv: float32 [2, 768, 3, 768], P('section', 'dp', None, 'tensor')
- grad_qv_bias: float32 [2, 2, 768], P('section', None, ('tensor', 'dp'))
- grad_out_weight: float32 [2, 768, 768], P('section', 'tensor', 'dp')
- grad_up_weight: float32 [2, 768, 3072], P('section', 'dp', 'tensor')
- grad_up_bias: float32 [2, 3072], P('section', ('tensor', 'dp'))
- grad_down_weight: float32 [2, 3072, 768], P('section', 'tensor', 'dp')
- grad_gains: float32 [2, 2, 768], P('section', None, ('tensor', 'dp'))
- grad_shifts: float32 [2, 4, 768], P('section', None, ('tensor', 'dp'))
The draws below stay inside these ranges and needn't reach their ends.
Inputs may be any that keep to these rules, and one draw needn't show every extreme that they name: image_counts[g] counts the live image slots of group g, taken in order micro-batch by micro-batch; some group is full and some group holds exactly the least count.
All inputs are finite; a program needn't handle non-finite values.
Results may differ from the reference program's by a relative error of at most 0.0003.
Values sent between devices are 32-bit elements; how exact they have to be, the bound alone decides.
A program may use at most 192 MiB of HBM per device.

```python
import jax
import jax.numpy as jnp
from jax import lax

D = 768
H = 12
HD = 64
FF = 3072
SEQ = 197
MB = 2
IMG_MB = 2
LAYERS = 2
GROUPS = 8


def draw_image_counts(key, part):
    key = jax.random.fold_in(key, 11)
    fullest = MB * IMG_MB
    fewest = max(1, fullest // 2)
    first_key, second_key = jax.random.split(key)
    counted = jax.random.randint(first_key, (GROUPS,), fewest, fullest + 1)
    shuffled = jax.random.permutation(second_key, GROUPS)
    counted = counted.at[shuffled[0]].set(fullest).at[shuffled[1]].set(fewest)
    return counted.astype(jnp.int32)


def spiked(array, rng, source, target, parts, factor):
    owner, partner = [(jnp.arange(array.shape[dim]) // (array.shape[dim] // parts)).reshape([-1 if axis == dim else 1 for axis in range(array.ndim)]) for dim in (source, target)]
    chosen = jax.random.permutation(rng, parts)[partner]
    strong = (owner == chosen) | (owner == (partner + parts // 2) % parts)
    return jnp.where(strong, factor * array, array)


def steps_of(key, extent, cuts, smallest, high):
    factor_of = 1.0
    for position, parts in cuts:
        draws = jax.random.uniform(jax.random.fold_in(jax.random.fold_in(key, 6), position), (parts,), jnp.float32, smallest / len(cuts), high / len(cuts))
        factor_of = factor_of * jnp.repeat(jnp.exp(draws), extent[position] // parts).reshape((-1,) + (1,) * (len(extent) - 1 - position))
    return factor_of


def normal_values(key, extent, deviation, reach, pieces=(), held_as=jnp.bfloat16):
    result = jax.random.normal(key, extent, jnp.float32) * deviation
    if len(pieces) > 0:
        result = steps_of(key, extent, pieces, -0.22, 0.18) * result
    return jnp.clip(result, min=-reach, max=reach).astype(held_as)


def heavy_noise(stream_key, shape, spread, limit, shards, heavy, held_as=jnp.bfloat16):
    drawn = spread * jax.random.normal(stream_key, shape, jnp.float32)
    if shards:
        drawn = drawn * steps_of(stream_key, shape, shards, -0.22, 0.18)
    return jnp.clip(spiked(drawn, jax.random.fold_in(stream_key, 3), *heavy), -limit, limit).astype(held_as)


def setup_inputs(seed: int = 0) -> dict:
    key_of = jax.random.split(jax.random.key(seed), 12)
    return {
        "embedded": normal_values(key_of[0], (MB, GROUPS, IMG_MB, SEQ, D), 1.0, 6.0, ((1, 8), (2, 2)), jnp.float32),
        "image_counts": draw_image_counts(jax.random.fold_in(key_of[11], 71), 0),
        "cotangent": heavy_noise(key_of[2], (MB, GROUPS, IMG_MB, SEQ, D), 1.0, 6.0, ((1, 8), (2, 2)), (1, 4, 8, 2.0), jnp.float32),
        "qkv_weight": normal_values(key_of[3], (LAYERS, D, 3, D), D ** -0.5, 0.21875, ((0, 2), (1, 8), (3, 2)), jnp.float32),
        "qv_bias": normal_values(key_of[4], (LAYERS, 2, D), 0.2, 1.2, ((0, 2), (2, 16)), jnp.float32),
        "out_weight": normal_values(key_of[5], (LAYERS, D, D), (D * 8 // SEQ) ** -0.5, 1.0, ((0, 2), (1, 2), (2, 8)), jnp.float32),
        "up_weight": normal_values(key_of[6], (LAYERS, D, FF), D ** -0.5, 0.21875, ((0, 2), (1, 8), (2, 2)), jnp.float32),
        "up_bias": normal_values(key_of[7], (LAYERS, FF), 0.5, 3.0, ((0, 2), (1, 16)), jnp.float32),
        "down_weight": normal_values(key_of[8], (LAYERS, FF, D), FF ** -0.5, 0.109375, ((0, 2), (1, 2), (2, 8)), jnp.float32),
        "norm_gains": jnp.clip(1.0 + 0.18 * jax.random.normal(key_of[9], (LAYERS, 2, D), jnp.float32), 0.1, 1.9),
        "shift_terms": normal_values(key_of[10], (LAYERS, 4, D), 0.5, 3.0, ((0, 2), (2, 16)), jnp.float32),
    }


epsilon = 1e-06
highest = lax.Precision.HIGHEST

@jax.custom_vjp
def low(v):
    return lax.optimization_barrier(v.astype(jnp.bfloat16)).astype(jnp.float32)

@jax.custom_vjp
def low_back(v):
    return v

def low_keep(v):
    return (low(v), None)

def low_pass(kept, grad):
    return (grad,)

def back_keep(v):
    return (v, None)

def back_low(kept, grad):
    return (low(grad),)
low.defvjp(low_keep, low_pass)
low_back.defvjp(back_keep, back_low)

def layer_norm(value, gain, shift):
    centred = value - lax.optimization_barrier(jnp.mean(value, -1, keepdims=True))
    variance = lax.optimization_barrier(jnp.mean(centred * centred, -1, keepdims=True))
    return centred * lax.rsqrt(variance + epsilon) * gain + shift

def attend_block(block):
    query, keys, values = block
    scores = jnp.einsum('nqhd,nkhd->nhqk', query, keys, precision=highest) * HD ** (-0.5)
    weights = jax.nn.softmax(scores, -1)
    return jnp.einsum('nhqk,nkhd->nqhd', weights, values, precision=highest)

def encoder_layer(value, qkv_w, qv_b, out_w, up_w, up_b, down_w, gains, shifts):
    number = value.shape[0]
    normed = layer_norm(value, gains[0], shifts[0])
    joined = jnp.einsum('nsd,dce->nsce', normed, qkv_w, precision=highest)
    joined = joined + jnp.stack([qv_b[0], jnp.zeros_like(qv_b[0]), qv_b[1]])
    split = joined.reshape(number // IMG_MB, IMG_MB, SEQ, 3, H, HD)
    mixed = lax.map(jax.checkpoint(attend_block), (split[:, :, :, 0], split[:, :, :, 1], split[:, :, :, 2]))
    mixed = mixed.reshape(number, SEQ, D)
    middle = value + jnp.einsum('nse,ed->nsd', mixed, out_w, precision=highest) + shifts[2]
    second = layer_norm(middle, gains[1], shifts[1])
    pre = jnp.einsum('nsd,df->nsf', second, up_w, precision=highest) + up_b
    hidden = jax.nn.gelu(pre, approximate=False)
    return middle + jnp.einsum('nsf,fd->nsd', hidden, down_w, precision=highest) + shifts[3]

def reference(embedded, image_counts, cotangent, qkv_weight, qv_bias, out_weight, up_weight, up_bias, down_weight, norm_gains, shift_terms):
    slot = jnp.arange(MB, dtype=jnp.int32)[:, None, None] * IMG_MB + jnp.arange(IMG_MB, dtype=jnp.int32)[None, None, :]
    live = (slot < image_counts[None, :, None]).astype(jnp.float32)[..., None, None]
    shape = embedded.shape

    def forward(start, offsets, params):
        value = start
        outputs = []
        for level in range(LAYERS):
            flat = (value + offsets[level]).reshape(-1, SEQ, D)
            layer_params = [param[level] for param in params]
            value = encoder_layer(flat, *layer_params).reshape(shape) * live
            outputs.append(value)
        return jnp.stack(outputs)
    params = (qkv_weight, qv_bias, out_weight, up_weight, up_bias, down_weight, norm_gains, shift_terms)
    offsets = jnp.zeros((LAYERS,) + shape, jnp.float32)
    outputs, backward = jax.vjp(forward, embedded, offsets, params)
    upstream = jnp.zeros_like(outputs).at[LAYERS - 1].set(cotangent)
    grad_start, grad_offsets, grads = backward(upstream)
    return (outputs, grad_offsets, grads[0], grads[1], grads[2], grads[3], grads[4], grads[5], grads[6], grads[7])
```

```python
import functools

import jax
import jax.numpy as jnp
from jax import lax
from jax.experimental import pallas as pl
from jax.experimental.pallas import tpu as pltpu
from jax.sharding import PartitionSpec as P

HD = 64
SCALE = HD ** (-0.5)
EPS = 1e-06
HIGH = lax.Precision.HIGH
MESH = pl.DeviceIdType.MESH
VMEM_BYTES = 63 * 2**20
F32 = jnp.float32


def dot(left, right, left_dim, right_dim):
    return lax.dot_general(
        left,
        right,
        (((left_dim,), (right_dim,)), ((), ())),
        precision=HIGH,
        preferred_element_type=F32,
    )


def up_to(count, step):
    return -(-count // step) * step


def normalize(value):
    centred = value - jnp.mean(value, -1, keepdims=True)
    inverse = lax.rsqrt(jnp.mean(centred * centred, -1, keepdims=True) + EPS)
    return centred * inverse, inverse


def normalize_back(grad_unit, unit, inverse):
    return inverse * (
        grad_unit
        - jnp.mean(grad_unit, -1, keepdims=True)
        - unit * jnp.mean(grad_unit * unit, -1, keepdims=True)
    )


class Place:
    def __init__(self, chips):
        self.s = lax.axis_index("section")
        self.t = lax.axis_index("tensor")
        d = lax.axis_index("dp")
        self.chips = chips
        self.z = d // 2
        self.c = d % 2
        self.x_peer = (1 - self.s, self.t, d)
        self.y_peer = (self.s, 1 - self.t, d)
        self.core_peer = (self.s, self.t, self.z * 2 + 1 - self.c)

    def z_at(self, step):
        return (self.z + step) % self.chips

    def z_peer(self, step):
        return (self.s, self.t, self.z_at(step) * 2 + self.c)

    def greet(self):
        barrier = pltpu.get_barrier_semaphore()
        peers = [self.x_peer, self.y_peer, self.core_peer]
        peers += [self.z_peer(step) for step in range(1, self.chips)]
        for peer in peers:
            pl.semaphore_signal(barrier, inc=1, device_id=peer, device_id_type=MESH)
        pl.semaphore_wait(barrier, len(peers))


def remote(src, dst, send, recv, peer):
    return pltpu.make_async_remote_copy(
        src_ref=src,
        dst_ref=dst,
        send_sem=send,
        recv_sem=recv,
        device_id=peer,
        device_id_type=MESH,
    )


def key_mask(rows, seq):
    return lax.broadcasted_iota(jnp.int32, (rows, rows), 1) < seq


def head_lanes(which):
    return lax.broadcasted_iota(jnp.int32, (1, 2 * HD), 1) // HD == which


def attend(joined, mixed, seq):
    rows, width = mixed.shape
    keep = key_mask(rows, seq)
    for pair in range(width // (2 * HD)):
        lanes = slice(pair * 2 * HD, (pair + 1) * 2 * HD)
        query = joined[:, lanes] * SCALE
        keys = joined[:, width + lanes.start : width + lanes.stop]
        values = joined[:, 2 * width + lanes.start : 2 * width + lanes.stop]
        total = None
        for which in range(2):
            own = head_lanes(which)
            scores = dot(query, jnp.where(own, keys, 0.0), 1, 1)
            scores = jnp.where(keep, scores, -3e38)
            weights = jnp.exp(scores - jnp.max(scores, -1, keepdims=True))
            probs = weights / jnp.sum(weights, -1, keepdims=True)
            part = dot(probs, jnp.where(own, values, 0.0), 1, 0)
            total = part if total is None else total + part
        mixed[:, lanes] = total


def attend_back(joined, mixed, grad_mixed, grad_joined, seq):
    rows, width = mixed.shape
    keep = key_mask(rows, seq)
    for pair in range(width // (2 * HD)):
        lanes = slice(pair * 2 * HD, (pair + 1) * 2 * HD)
        query = joined[:, lanes] * SCALE
        keys = joined[:, width + lanes.start : width + lanes.stop]
        values = joined[:, 2 * width + lanes.start : 2 * width + lanes.stop]
        grad = grad_mixed[:, lanes]
        product = grad * mixed[:, lanes]
        grads = [None, None, None]
        for which in range(2):
            own = head_lanes(which)
            own_keys = jnp.where(own, keys, 0.0)
            scores = dot(query, own_keys, 1, 1)
            scores = jnp.where(keep, scores, -3e38)
            weights = jnp.exp(scores - jnp.max(scores, -1, keepdims=True))
            probs = weights / jnp.sum(weights, -1, keepdims=True)
            own_grad = jnp.where(own, grad, 0.0)
            row_dot = jnp.sum(jnp.where(own, product, 0.0), -1, keepdims=True)
            grad_probs = dot(grad, jnp.where(own, values, 0.0), 1, 1)
            grad_scores = probs * (grad_probs - row_dot)
            parts = (
                dot(grad_scores, own_keys, 1, 0) * SCALE,
                dot(grad_scores, jnp.where(own, query, 0.0), 0, 0),
                dot(probs, own_grad, 0, 0),
            )
            grads = [b if a is None else a + b for a, b in zip(grads, parts)]
        for number, part in enumerate(grads):
            start = number * width + lanes.start
            grad_joined[:, start : start + 2 * HD] = part


def phi_big(value):
    return 0.5 * (1.0 + lax.erf(value * 0.7071067811865476))


def phi_small(value):
    return jnp.exp(-0.5 * value * value) * 0.3989422804014327


class Vectors:
    def __init__(self, ref, width, hidden):
        self.ref, self.width, self.hidden = ref, width, hidden

    def gain(self, which):
        return self.ref[which : which + 1, :]

    def shift(self, which):
        return self.ref[2 + which : 3 + which, :]

    def query(self):
        return self.ref[8:9, 0 : self.width]

    def value(self):
        return self.ref[8:9, self.width : 2 * self.width]

    def up(self, row):
        return self.ref[9 + row : 10 + row, :]


def add_rows(target, sources, step):
    rows = target.shape[0]

    @pl.loop(0, rows // step)
    def _(index):
        here = pl.ds(pl.multiple_of(index * step, 8), step)
        total = target[here, :]
        for source in sources:
            total = total + source[here, :]
        target[here, :] = total


def forward_kernel(
    chips,
    seq,
    sent_rows,
    x_in,
    live,
    vec_in,
    wq,
    wo,
    wu,
    wd,
    out_all,
    out_x,
    vec,
    hs,
    mid,
    gq_out,
    go_out,
    gu_out,
    gd_out,
    n1_out,
    n2_out,
    joined_out,
    mixed_out,
    pre_out,
    gq,
    go,
    gu,
    gd,
    n1,
    n2,
    joined,
    mixed,
    pre,
    hidden,
    received,
    sending,
    vs,
    vy,
    vc,
    vz,
    y_send,
    y_recv,
    v_send,
    v_recv,
    zs,
    zr,
    xs,
    xr,
    cs,
    cr,
    local,
    save,
):
    here = Place(chips)
    s, c, z = here.s, here.c, here.z
    shards = (wq, wo, wu, wd)
    whole = (gq, go, gu, gd)
    block = wq.shape[0]
    rows, depth = x_in.shape
    width = go.shape[2]
    tail = rows - sent_rows
    for buffer in (n1, n2):
        for layer in range(2):
            buffer[layer, 1, sent_rows:rows, :] = jnp.zeros((tail, depth), F32)
    for index in range(received.shape[0]):
        received[index, sent_rows:rows, :] = jnp.zeros((tail, depth), F32)
    vs[...] = vec_in[...]
    here.greet()

    def rows_of(matrix, layer, step, core):
        start = pl.multiple_of((here.z_at(step) * 2 + core) * block, 8)
        return whole[matrix].at[layer, pl.ds(start, block), :]

    departing = []

    def launch(copy):
        copy.start()
        departing.append(copy)
        return copy

    def departed(copy):
        copy.wait_send()
        departing[:] = [item for item in departing if item is not copy]

    def z_copy(matrix, step):
        return remote(
            shards[matrix],
            rows_of(matrix, s, 0, c),
            zs.at[matrix, step - 1],
            zr.at[matrix, step - 1],
            here.z_peer(step),
        )

    def x_copy(matrix, step, src=None):
        spot = rows_of(matrix, s, chips - step, c)
        return remote(
            spot if src is None else src,
            spot,
            xs.at[matrix, step],
            xr.at[matrix, step],
            here.x_peer,
        )

    def c_copy(kind, matrix, step, src=None):
        spot = rows_of(matrix, s if kind == 0 else 1 - s, chips - step, c)
        return remote(
            spot if src is None else src,
            spot,
            cs.at[kind, matrix, step],
            cr.at[kind, matrix, step],
            here.core_peer,
        )

    def z_arrived(matrix, step):
        spot = rows_of(matrix, s, chips - step, c)
        pltpu.make_async_copy(spot, spot, zr.at[matrix, step - 1]).wait()

    def x_arrived(matrix, step):
        spot = rows_of(matrix, 1 - s, chips - step, c)
        pltpu.make_async_copy(spot, spot, xr.at[matrix, step]).wait()

    def c_arrived(kind, matrix, step):
        spot = rows_of(matrix, s if kind == 0 else 1 - s, chips - step, 1 - c)
        pltpu.make_async_copy(spot, spot, cr.at[kind, matrix, step]).wait()

    own_copies = []
    for matrix in range(4):
        for step in range(1, chips):
            launch(z_copy(matrix, step))
        launch(x_copy(matrix, 0, shards[matrix]))
        launch(c_copy(0, matrix, 0, shards[matrix]))
        copy = pltpu.make_async_copy(
            shards[matrix], rows_of(matrix, s, 0, c), local.at[matrix]
        )
        copy.start()
        own_copies.append(copy)

    def exchange_vectors():
        copy = remote(
            vs.at[pl.ds(0, 8)], vy, v_send.at[0], v_recv.at[0], here.y_peer
        )
        copy.start()
        copy.wait()
        vs[0:8, :] = vs[0:8, :] + vy[...]
        copy = remote(vs, vc, v_send.at[1], v_recv.at[1], here.core_peer)
        copy.start()
        copy.wait()
        vs[...] = vs[...] + vc[...]
        copies = []
        for step in range(1, chips):
            copy = remote(
                vs,
                vz.at[step - 1],
                v_send.at[1 + step],
                v_recv.at[1 + step],
                here.z_peer(step),
            )
            copy.start()
            copies.append(copy)
        for copy in copies:
            copy.wait()
        total = vs[...]
        for step in range(1, chips):
            total = total + vz[step - 1]
        vec[s] = total
        copy = remote(
            vec.at[s], vec.at[s], v_send.at[chips + 1], v_recv.at[chips + 1], here.x_peer
        )
        copy.start()
        copy.wait_send()
        spot = vec.at[1 - s]
        pltpu.make_async_copy(spot, spot, v_recv.at[chips + 1]).wait()

    exchange_vectors()

    saves = {}

    def keep(name, src, dst, sem):
        copy = pltpu.make_async_copy(src, dst, save.at[sem])
        copy.start()
        saves[name] = copy

    def before_write(name):
        if name in saves:
            saves.pop(name).wait()

    def own_service(matrix):
        for step in range(1, chips):
            z_arrived(matrix, step)
            launch(x_copy(matrix, step))
            launch(c_copy(0, matrix, step))

    def other_service(matrix):
        for step in range(chips):
            x_arrived(matrix, step)
            launch(c_copy(1, matrix, step))

    def finish(matrix):
        own_copies[matrix].wait()
        for kind in range(2):
            for step in range(chips):
                c_arrived(kind, matrix, step)
        keep(
            "whole%d" % matrix,
            whole[matrix],
            (gq_out, go_out, gu_out, gd_out)[matrix],
            matrix,
        )

    for matrix in range(4):
        own_service(matrix)
    for matrix in range(4):
        other_service(matrix)
    for matrix in range(4):
        finish(matrix)

    hs[0] = x_in[...]

    def y_copy(src, dst, index):
        return launch(
            remote(
                src.at[pl.ds(0, sent_rows)],
                dst.at[pl.ds(0, sent_rows)],
                y_send.at[index],
                y_recv.at[index],
                here.y_peer,
            )
        )

    send_of = None
    for layer in range(2):
        vectors = Vectors(vec.at[layer], width, None)
        unit, _ = normalize(hs[layer])
        n1[layer, 0] = unit * vectors.gain(0) + vectors.shift(0)
        arrive = y_copy(n1.at[layer, 0], n1.at[layer, 1], 4 * layer)
        before_write("joined")
        before_write("mixed")
        for image in range(2):
            if image == 1:
                arrive.wait_recv()
            source = n1.at[layer, image]
            for part in range(3):
                lanes = slice(part * width, (part + 1) * width)
                value = dot(source[...], gq[layer, :, lanes], 1, 0)
                if part == 0:
                    value = value + vectors.query()
                if part == 2:
                    value = value + vectors.value()
                joined[image, :, lanes] = value
            attend(joined.at[image], mixed.at[image], seq)
        if send_of is not None:
            departed(send_of)
        sending[...] = dot(mixed[1], go[layer], 1, 1)
        send_of = y_copy(sending, received.at[2 * layer], 4 * layer + 1)
        middle = hs[layer] + dot(mixed[0], go[layer], 1, 1) + vectors.shift(2)
        keep("n1", n1.at[layer], n1_out.at[layer], 4 + layer)
        keep("joined", joined, joined_out.at[layer], 6 + layer)
        keep("mixed", mixed, mixed_out.at[layer], 8 + layer)
        saves["n1%d" % layer] = saves.pop("n1")
        send_of.wait_recv()
        middle = middle + received[2 * layer]
        mid[layer] = middle
        unit, _ = normalize(middle)
        n2[layer, 0] = unit * vectors.gain(1) + vectors.shift(1)
        arrive = y_copy(n2.at[layer, 0], n2.at[layer, 1], 4 * layer + 2)
        before_write("pre")
        for image in range(2):
            if image == 1:
                arrive.wait_recv()
            source = n2.at[layer, image]
            for part in range(pre.shape[2] // depth):
                lanes = slice(part * depth, (part + 1) * depth)
                value = dot(source[...], gu[layer, :, lanes], 1, 0) + vectors.up(part)
                pre[image, :, lanes] = value
                hidden[image, :, lanes] = value * phi_big(value)
        departed(send_of)
        sending[...] = dot(hidden[1], gd[layer], 1, 1)
        send_of = y_copy(sending, received.at[2 * layer + 1], 4 * layer + 3)
        keep("n2%d" % layer, n2.at[layer], n2_out.at[layer], 10 + layer)
        keep("pre", pre, pre_out.at[layer], 12 + layer)
        result = mid[layer] + dot(hidden[0], gd[layer], 1, 1) + vectors.shift(3)
        send_of.wait_recv()
        result = (result + received[2 * layer + 1]) * live[:, 0:1]
        out_all[layer] = result
        if layer == 0:
            hs[1] = result

    copy = remote(
        out_all.at[1 - s], out_x, v_send.at[chips + 2], v_recv.at[chips + 2], here.x_peer
    )
    copy.start()
    for saved in saves.values():
        saved.wait()
    for item in departing:
        item.wait_send()
    copy.wait()


def forward(chips, seq, x_in, live, vec_in, wq, wo, wu, wd):
    rows, depth = x_in.shape
    sent_rows = up_to(seq, 8)
    width = wo.shape[1]
    hidden = wu.shape[1]
    widths = (wq.shape[1], width, hidden, hidden)
    whole = [(2, depth, w) for w in widths]
    any_space = pl.BlockSpec(memory_space=pl.ANY)
    vmem = pl.BlockSpec(memory_space=pltpu.VMEM)
    outs = [
        ((2, rows, depth), vmem),
        ((rows, depth), vmem),
        ((2,) + vec_in.shape, vmem),
        ((2, rows, depth), vmem),
        ((2, rows, depth), vmem),
        *[(w, any_space) for w in whole],
        ((2, 2, rows, depth), any_space),
        ((2, 2, rows, depth), any_space),
        ((2, 2, rows, 3 * width), any_space),
        ((2, 2, rows, width), any_space),
        ((2, 2, rows, hidden), any_space),
    ]
    sems = pltpu.SemaphoreType.DMA
    scratch = [
        *[pltpu.VMEM(w, F32) for w in whole],
        pltpu.VMEM((2, 2, rows, depth), F32),
        pltpu.VMEM((2, 2, rows, depth), F32),
        pltpu.VMEM((2, rows, 3 * width), F32),
        pltpu.VMEM((2, rows, width), F32),
        pltpu.VMEM((2, rows, hidden), F32),
        pltpu.VMEM((2, rows, hidden), F32),
        pltpu.VMEM((4, rows, depth), F32),
        pltpu.VMEM((rows, depth), F32),
        pltpu.VMEM(vec_in.shape, F32),
        pltpu.VMEM((8, depth), F32),
        pltpu.VMEM(vec_in.shape, F32),
        pltpu.VMEM((chips - 1,) + vec_in.shape, F32),
        sems((8,)),
        sems((8,)),
        sems((chips + 3,)),
        sems((chips + 3,)),
        sems((4, chips - 1)),
        sems((4, chips - 1)),
        sems((4, chips)),
        sems((4, chips)),
        sems((2, 4, chips)),
        sems((2, 4, chips)),
        sems((4,)),
        sems((14,)),
    ]
    return pl.pallas_call(
        functools.partial(forward_kernel, chips, seq, sent_rows),
        out_shape=[jax.ShapeDtypeStruct(shape, F32) for shape, _ in outs],
        in_specs=[vmem] * 3 + [any_space] * 4,
        out_specs=[spec for _, spec in outs],
        scratch_shapes=scratch,
        compiler_params=pltpu.CompilerParams(
            collective_id=0, has_side_effects=True, vmem_limit_bytes=VMEM_BYTES
        ),
        name="forward_both",
    )(x_in, live, vec_in, wq, wo, wu, wd)


def backward_kernel(
    chips,
    seq,
    sent_rows,
    cot,
    live,
    vec,
    hs,
    mid,
    gq_in,
    go_in,
    gu_in,
    gd_in,
    n1_in,
    n2_in,
    joined_in,
    mixed_in,
    pre_in,
    gin,
    gin_x,
    gvec,
    pq,
    po,
    pu,
    pd,
    wq,
    wo,
    wu,
    wd,
    n1,
    n2,
    joined,
    mixed,
    pre,
    hidden,
    grad_all,
    mid_all,
    received,
    sending,
    own_part,
    grad_mixed,
    grad_joined,
    sq,
    so,
    su,
    sd,
    y_send,
    y_recv,
    x_send,
    x_recv,
    loads,
    stores,
):
    here = Place(chips)
    s = here.s
    rows, depth = cot.shape
    width = wo.shape[1]
    width_ff = wu.shape[1]
    tail = rows - sent_rows
    for buffer in (grad_all, mid_all):
        for layer in range(2):
            buffer[layer, 1, sent_rows:rows, :] = jnp.zeros((tail, depth), F32)
    for index in range(received.shape[0]):
        received[index, sent_rows:rows, :] = jnp.zeros((tail, depth), F32)
    gvec[...] = jnp.zeros(gvec.shape, F32)

    sources = dict(
        wd=(gd_in, wd),
        pre=(pre_in, pre),
        wu=(gu_in, wu),
        n2=(n2_in, n2),
        wo=(go_in, wo),
        joined=(joined_in, joined),
        mixed=(mixed_in, mixed),
        wq=(gq_in, wq),
        n1=(n1_in, n1),
    )
    order = list(sources)
    loading = {}

    def load(name, layer):
        src, dst = sources[name]
        copy = pltpu.make_async_copy(src.at[layer], dst, loads.at[order.index(name)])
        copy.start()
        loading[name] = copy

    def loaded(name):
        if name in loading:
            loading.pop(name).wait()

    for name in order:
        load(name, 1)
    here.greet()
    departing = []
    storing = {}

    def y_copy(src, dst, index):
        copy = remote(
            src.at[pl.ds(0, sent_rows)],
            dst.at[pl.ds(0, sent_rows)],
            y_send.at[index],
            y_recv.at[index],
            here.y_peer,
        )
        copy.start()
        departing.append(copy)
        return copy

    def departed(copy):
        copy.wait_send()
        departing[:] = [item for item in departing if item is not copy]

    def store(index, layer):
        copy = pltpu.make_async_copy(
            (sq, so, su, sd)[index], (pq, po, pu, pd)[index].at[layer], stores.at[index]
        )
        copy.start()
        storing[index] = copy

    def stored(index):
        if index in storing:
            storing.pop(index).wait()

    def flat(ref):
        return ref[...].reshape(2 * rows, ref.shape[-1])

    def product(target, left, right, tile):
        both = flat(left)
        for start in range(0, target.shape[1], tile):
            lanes = slice(start, start + tile)
            piece = right[:, :, lanes].reshape(2 * rows, tile)
            target[:, lanes] = dot(both, piece, 0, 0)

    def total(value):
        return jnp.sum(value, 0, keepdims=True)

    send_of = None
    for layer in (1, 0):
        vectors = Vectors(vec.at[layer], width, None)
        incoming = (cot[...] if layer == 1 else gin[1]) * live[:, 0:1]
        grad_all[layer, 0] = incoming
        base = 4 * (1 - layer)
        arrive = y_copy(grad_all.at[layer, 0], grad_all.at[layer, 1], base)
        gvec[layer, 5:6, :] = total(incoming)
        loaded("wd")
        loaded("pre")
        loaded("wu")
        for image in range(2):
            if image == 1:
                arrive.wait_recv()
            for part in range(width_ff // depth):
                lanes = slice(part * depth, (part + 1) * depth)
                grad_hidden = dot(grad_all[layer, image], wd[:, lanes], 1, 0)
                value = pre[image, :, lanes]
                upper = phi_big(value)
                hidden[image, :, lanes] = value * upper
                pre[image, :, lanes] = grad_hidden * (upper + value * phi_small(value))
            if image == 1:
                if send_of is not None:
                    departed(send_of)
                sending[...] = dot(pre[1], wu[...], 1, 1)
                send_of = y_copy(sending, received.at[2 * (1 - layer)], base + 1)
            else:
                own_part[...] = dot(pre[0], wu[...], 1, 1)
        if layer == 1:
            load("wd", 0)
            load("wu", 0)
        for part in range(width_ff // depth):
            lanes = slice(part * depth, (part + 1) * depth)
            gvec[layer, 9 + part : 10 + part, :] = total(pre[0, :, lanes]) + total(
                pre[1, :, lanes]
            )
        stored(3)
        product(sd, grad_all.at[layer], hidden, depth)
        store(3, layer)
        loaded("n2")
        stored(2)
        product(su, n2, pre, depth)
        store(2, layer)
        if layer == 1:
            load("pre", 0)
            load("n2", 0)
        unit, inverse = normalize(mid[layer])
        send_of.wait_recv()
        grad_second = own_part[...] + received[2 * (1 - layer)]
        gvec[layer, 1:2, :] = total(grad_second * unit)
        gvec[layer, 3:4, :] = total(grad_second)
        grad_middle = grad_all[layer, 0] + normalize_back(
            grad_second * vectors.gain(1), unit, inverse
        )
        mid_all[layer, 0] = grad_middle
        arrive = y_copy(mid_all.at[layer, 0], mid_all.at[layer, 1], base + 2)
        gvec[layer, 4:5, :] = total(grad_middle)
        loaded("wo")
        loaded("joined")
        loaded("mixed")
        loaded("wq")
        for image in range(2):
            if image == 1:
                arrive.wait_recv()
            grad_mixed[...] = dot(mid_all[layer, image], wo[...], 1, 0)
            attend_back(
                joined.at[image], mixed.at[image], grad_mixed, grad_joined.at[image], seq
            )
            if image == 1:
                departed(send_of)
                sending[...] = dot(grad_joined[1], wq[...], 1, 1)
                send_of = y_copy(sending, received.at[2 * (1 - layer) + 1], base + 3)
            else:
                own_part[...] = dot(grad_joined[0], wq[...], 1, 1)
        if layer == 1:
            load("wo", 0)
            load("wq", 0)
            load("joined", 0)
        stored(1)
        product(so, mid_all.at[layer], mixed, width)
        store(1, layer)
        loaded("n1")
        stored(0)
        product(sq, n1, grad_joined, width)
        store(0, layer)
        if layer == 1:
            load("mixed", 0)
            load("n1", 0)
        gvec[layer, 8:9, 0:width] = total(grad_joined[0, :, 0:width]) + total(
            grad_joined[1, :, 0:width]
        )
        gvec[layer, 8:9, width : 2 * width] = total(
            grad_joined[0, :, 2 * width : 3 * width]
        ) + total(grad_joined[1, :, 2 * width : 3 * width])
        unit, inverse = normalize(hs[layer])
        send_of.wait_recv()
        grad_first = own_part[...] + received[2 * (1 - layer) + 1]
        gvec[layer, 0:1, :] = total(grad_first * unit)
        gvec[layer, 2:3, :] = total(grad_first)
        gin[layer] = mid_all[layer, 0] + normalize_back(
            grad_first * vectors.gain(0), unit, inverse
        )
    copy = remote(gin.at[1 - s], gin_x, x_send, x_recv, here.x_peer)
    copy.start()
    for index in range(4):
        stored(index)
    for item in departing:
        item.wait_send()
    copy.wait()


def backward(chips, seq, cot, live, vec, hs, mid, whole, kept):
    rows, depth = cot.shape
    sent_rows = up_to(seq, 8)
    width, width_ff = whole[1].shape[2], whole[2].shape[2]
    widths = [w.shape[2] for w in whole]
    any_space = pl.BlockSpec(memory_space=pl.ANY)
    vmem = pl.BlockSpec(memory_space=pltpu.VMEM)
    outs = [
        ((2, rows, depth), vmem),
        ((rows, depth), vmem),
        (vec.shape, vmem),
        *[((2, depth, w), any_space) for w in widths],
    ]
    sems = pltpu.SemaphoreType.DMA
    scratch = [
        *[pltpu.VMEM((depth, w), F32) for w in widths],
        pltpu.VMEM((2, rows, depth), F32),
        pltpu.VMEM((2, rows, depth), F32),
        pltpu.VMEM((2, rows, 3 * width), F32),
        pltpu.VMEM((2, rows, width), F32),
        pltpu.VMEM((2, rows, width_ff), F32),
        pltpu.VMEM((2, rows, width_ff), F32),
        pltpu.VMEM((2, 2, rows, depth), F32),
        pltpu.VMEM((2, 2, rows, depth), F32),
        pltpu.VMEM((4, rows, depth), F32),
        pltpu.VMEM((rows, depth), F32),
        pltpu.VMEM((rows, depth), F32),
        pltpu.VMEM((rows, width), F32),
        pltpu.VMEM((2, rows, 3 * width), F32),
        *[pltpu.VMEM((depth, w), F32) for w in widths],
        sems((8,)),
        sems((8,)),
        sems,
        sems,
        sems((9,)),
        sems((4,)),
    ]
    return pl.pallas_call(
        functools.partial(backward_kernel, chips, seq, sent_rows),
        out_shape=[jax.ShapeDtypeStruct(shape, F32) for shape, _ in outs],
        in_specs=[vmem] * 5 + [any_space] * 9,
        out_specs=[spec for _, spec in outs],
        scratch_shapes=scratch,
        compiler_params=pltpu.CompilerParams(
            collective_id=1, has_side_effects=True, vmem_limit_bytes=VMEM_BYTES
        ),
        name="backward_both",
    )(cot, live, vec, hs, mid, *whole, *kept)


def sums_kernel(
    chips,
    gvec,
    pq,
    po,
    pu,
    pd,
    vec_out,
    outq,
    outo,
    outu,
    outd,
    aq,
    ao,
    au,
    ad,
    rcq,
    rco,
    rcu,
    rcd,
    rxq,
    rxo,
    rxu,
    rxd,
    rzq,
    rzo,
    rzu,
    rzd,
    vx,
    vc,
    vz,
    vy,
    cs,
    cr,
    xs,
    xr,
    zs,
    zr,
    local,
    v_send,
    v_recv,
):
    here = Place(chips)
    s, c, z = here.s, here.c, here.z
    partial = (pq, po, pu, pd)
    own = (aq, ao, au, ad)
    from_core = (rcq, rco, rcu, rcd)
    from_x = (rxq, rxo, rxu, rxd)
    from_z = (rzq, rzo, rzu, rzd)
    outs = (outq, outo, outu, outd)
    block = outq.shape[0]
    here.greet()
    departing = []

    def launch(copy):
        copy.start()
        departing.append(copy)
        return copy

    def rows_of(matrix, layer, step, core):
        start = pl.multiple_of((here.z_at(step) * 2 + core) * block, 8)
        return partial[matrix].at[layer, pl.ds(start, block), :]

    core_copies, own_copies = {}, {}
    for kind in (1, 0):
        layer = s if kind == 0 else 1 - s
        for matrix in (3, 2, 1, 0):
            for step in range(chips):
                core_copies[kind, matrix, step] = launch(
                    remote(
                        rows_of(matrix, layer, step, 1 - c),
                        from_core[matrix].at[kind, step],
                        cs.at[kind, matrix, step],
                        cr.at[kind, matrix, step],
                        here.core_peer,
                    )
                )
                copy = pltpu.make_async_copy(
                    rows_of(matrix, layer, step, c),
                    own[matrix].at[kind, step],
                    local.at[kind, matrix, step],
                )
                copy.start()
                own_copies[kind, matrix, step] = copy

    def sum_vectors():
        copy = remote(gvec.at[1 - s], vx, v_send.at[0], v_recv.at[0], here.x_peer)
        copy.start()
        copy.wait()
        vec_out[...] = gvec[s] + vx[...]
        copy = remote(vec_out, vc, v_send.at[1], v_recv.at[1], here.core_peer)
        copy.start()
        copy.wait()
        vec_out[...] = vec_out[...] + vc[...]
        copies = []
        for step in range(1, chips):
            copy = remote(
                vec_out,
                vz.at[step - 1],
                v_send.at[1 + step],
                v_recv.at[1 + step],
                here.z_peer(step),
            )
            copy.start()
            copies.append(copy)
        for copy in copies:
            copy.wait()
        total = vec_out[...]
        for step in range(1, chips):
            total = total + vz[step - 1]
        vec_out[...] = total
        copy = remote(
            vec_out.at[pl.ds(0, 8)],
            vy,
            v_send.at[chips + 1],
            v_recv.at[chips + 1],
            here.y_peer,
        )
        copy.start()
        copy.wait()
        vec_out[0:8, :] = vec_out[0:8, :] + vy[...]

    small = 24 if block % 24 == 0 else block

    def core_sum(kind, matrix, step):
        own_copies[kind, matrix, step].wait()
        core_copies[kind, matrix, step].wait_recv()
        add_rows(own[matrix].at[kind, step], [from_core[matrix].at[kind, step]], small)

    x_copies = {}
    for matrix in (3, 2, 1, 0):
        for step in range(chips):
            core_sum(1, matrix, step)
            x_copies[matrix, step] = launch(
                remote(
                    own[matrix].at[1, step],
                    from_x[matrix].at[step],
                    xs.at[matrix, step],
                    xr.at[matrix, step],
                    here.x_peer,
                )
            )
    sum_vectors()
    z_copies = {}
    for matrix in (3, 2, 1, 0):
        for step in list(range(1, chips)) + [0]:
            core_sum(0, matrix, step)
            x_copies[matrix, step].wait_recv()
            add_rows(own[matrix].at[0, step], [from_x[matrix].at[step]], small)
            if step:
                z_copies[matrix, step] = launch(
                    remote(
                        own[matrix].at[0, step],
                        from_z[matrix].at[step - 1],
                        zs.at[matrix, step - 1],
                        zr.at[matrix, step - 1],
                        here.z_peer(step),
                    )
                )
    for matrix in (3, 2, 1, 0):
        for step in range(1, chips):
            z_copies[matrix, step].wait_recv()
        outs[matrix][...] = own[matrix][0, 0]
        add_rows(
            outs[matrix], [from_z[matrix].at[step - 1] for step in range(1, chips)], small
        )
    for item in departing:
        item.wait_send()


def sums(chips, gvec, partial):
    widths = [p.shape[2] for p in partial]
    block = partial[0].shape[1] // (2 * chips)
    any_space = pl.BlockSpec(memory_space=pl.ANY)
    vmem = pl.BlockSpec(memory_space=pltpu.VMEM)
    packed = gvec.shape[1:]
    sems = pltpu.SemaphoreType.DMA
    scratch = [
        *[pltpu.VMEM((2, chips, block, w), F32) for w in widths],
        *[pltpu.VMEM((2, chips, block, w), F32) for w in widths],
        *[pltpu.VMEM((chips, block, w), F32) for w in widths],
        *[pltpu.VMEM((chips - 1, block, w), F32) for w in widths],
        pltpu.VMEM(packed, F32),
        pltpu.VMEM(packed, F32),
        pltpu.VMEM((chips - 1,) + packed, F32),
        pltpu.VMEM((8,) + packed[1:], F32),
        sems((2, 4, chips)),
        sems((2, 4, chips)),
        sems((4, chips)),
        sems((4, chips)),
        sems((4, chips - 1)),
        sems((4, chips - 1)),
        sems((2, 4, chips)),
        sems((chips + 2,)),
        sems((chips + 2,)),
    ]
    return pl.pallas_call(
        functools.partial(sums_kernel, chips),
        out_shape=[jax.ShapeDtypeStruct(packed, F32)]
        + [jax.ShapeDtypeStruct((block, w), F32) for w in widths],
        in_specs=[vmem] + [any_space] * 4,
        out_specs=[vmem] * 5,
        scratch_shapes=scratch,
        compiler_params=pltpu.CompilerParams(
            collective_id=2, has_side_effects=True, vmem_limit_bytes=VMEM_BYTES
        ),
        name="sum_all",
    )(gvec, *partial)


def body(
    embedded,
    image_counts,
    cotangent,
    qkv_weight,
    qv_bias,
    out_weight,
    up_weight,
    up_bias,
    down_weight,
    norm_gains,
    shift_terms,
):
    groups = lax.axis_size("dp")
    chips = groups // 2
    tensors = lax.axis_size("tensor")
    s = lax.axis_index("section")
    t = lax.axis_index("tensor")
    d = lax.axis_index("dp")
    seq, depth = embedded.shape[3:]
    rows = up_to(seq, 16)
    block = qkv_weight.shape[1]
    width = qkv_weight.shape[3]
    width_ff = up_weight.shape[2]

    def padded(value):
        chosen = lax.dynamic_index_in_dim(value[:, 0, 0], s, 0, keepdims=False)
        return jnp.pad(chosen, ((0, rows - seq), (0, 0)))

    slot = s * tensors + t
    alive = (slot < image_counts[0]).astype(F32)
    inside = lax.broadcasted_iota(jnp.int32, (rows, 128), 0) < seq
    live = jnp.where(inside, alive, 0.0)

    def spread(pieces, parts, part):
        count, piece = pieces.shape
        tiled = jnp.broadcast_to(pieces[:, None, :], (count, parts, piece))
        mine = lax.broadcasted_iota(jnp.int32, (count, parts, piece), 1) == part
        return jnp.where(mine, tiled, 0.0).reshape(count, parts * piece)

    wide = jnp.concatenate([norm_gains[0], shift_terms[0], jnp.zeros_like(norm_gains[0])])
    wide = spread(wide, tensors * groups, t * groups + d)
    biases = spread(qv_bias[0], groups, d).reshape(-1, depth)
    ups = spread(up_bias, groups, d).reshape(-1, depth)
    packed = jnp.concatenate([wide, biases, ups])
    packed = jnp.pad(packed, ((0, up_to(packed.shape[0], 8) - packed.shape[0]), (0, 0)))

    shards = (
        qkv_weight[0].reshape(block, 3 * width),
        out_weight[0].T,
        up_weight[0],
        down_weight[0].T,
    )
    (
        out_all,
        out_x,
        vec,
        hs,
        mid,
        gq,
        go,
        gu,
        gd,
        n1,
        n2,
        joined,
        mixed,
        pre,
    ) = forward(chips, seq, padded(embedded), live, packed, *shards)
    gin, gin_x, gvec, *partial = backward(
        chips,
        seq,
        padded(cotangent),
        live,
        vec,
        hs,
        mid,
        (gq, go, gu, gd),
        (n1, n2, joined, mixed, pre),
    )
    vec_sum, sum_q, sum_o, sum_u, sum_d = sums(chips, gvec, partial)

    def both(own, other):
        mine = lax.dynamic_index_in_dim(own, s, 0, keepdims=False)[:seq]
        other = other[:seq]
        first = jnp.where(s == 0, mine, other)
        second = jnp.where(s == 0, other, mine)
        return jnp.stack([first, second])[None, :, None, None]

    piece = depth // (tensors * groups)
    wide = lax.dynamic_slice_in_dim(vec_sum[0:6], (t * groups + d) * piece, piece, 1)
    biases = vec_sum[8].reshape(2, width)
    biases = lax.dynamic_slice_in_dim(biases, d * (width // groups), width // groups, 1)
    count = width_ff // depth
    ups = vec_sum[9 : 9 + count].reshape(width_ff)
    ups = lax.dynamic_slice_in_dim(ups, d * (width_ff // groups), width_ff // groups, 0)
    return (
        both(out_all, out_x),
        both(gin, gin_x),
        sum_q.reshape(1, block, 3, width),
        biases[None],
        sum_o.T[None],
        sum_u[None],
        ups[None],
        sum_d.T[None],
        wide[None, 0:2],
        wide[None, 2:6],
    )


def solution(mesh):
    placed = (
        P(None, "dp", "tensor", None, None),
        P("dp"),
        P(None, "dp", "tensor", None, None),
        P("section", "dp", None, "tensor"),
        P("section", None, ("tensor", "dp")),
        P("section", "tensor", "dp"),
        P("section", "dp", "tensor"),
        P("section", ("tensor", "dp")),
        P("section", "tensor", "dp"),
        P("section", None, ("tensor", "dp")),
        P("section", None, ("tensor", "dp")),
    )
    return jax.shard_map(
        body,
        mesh=mesh,
        in_specs=placed,
        out_specs=(
            P("section", None, "dp", "tensor", None, None),
            P("section", None, "dp", "tensor", None, None),
            P("section", "dp", None, "tensor"),
            P("section", None, ("tensor", "dp")),
            P("section", "tensor", "dp"),
            P("section", "dp", "tensor"),
            P("section", ("tensor", "dp")),
            P("section", "tensor", "dp"),
            P("section", None, ("tensor", "dp")),
            P("section", None, ("tensor", "dp")),
        ),
        check_vma=False,
    )
```

```python
import functools

import jax
import jax.numpy as jnp
from jax import lax
from jax.experimental import pallas as pl
from jax.experimental.pallas import tpu as pltpu
from jax.sharding import PartitionSpec as P

HD = 64
SCALE = HD ** (-0.5)
EPS = 1e-06
HIGH = lax.Precision.HIGH
MESH = pl.DeviceIdType.MESH
VMEM_BYTES = 63 * 2**20
F32 = jnp.float32


def dot(left, right, left_dim, right_dim):
    return lax.dot_general(
        left,
        right,
        (((left_dim,), (right_dim,)), ((), ())),
        precision=HIGH,
        preferred_element_type=F32,
    )


def up_to(count, step):
    return -(-count // step) * step


def normalize(value):
    centred = value - jnp.mean(value, -1, keepdims=True)
    inverse = lax.rsqrt(jnp.mean(centred * centred, -1, keepdims=True) + EPS)
    return centred * inverse, inverse


def normalize_back(grad_unit, unit, inverse):
    return inverse * (
        grad_unit
        - jnp.mean(grad_unit, -1, keepdims=True)
        - unit * jnp.mean(grad_unit * unit, -1, keepdims=True)
    )


class Place:
    def __init__(self, chips):
        self.s = lax.axis_index("section")
        self.t = lax.axis_index("tensor")
        d = lax.axis_index("dp")
        self.chips = chips
        self.z = d // 2
        self.c = d % 2
        self.x_peer = (1 - self.s, self.t, d)
        self.y_peer = (self.s, 1 - self.t, d)
        self.core_peer = (self.s, self.t, self.z * 2 + 1 - self.c)

    def z_at(self, step):
        return (self.z + step) % self.chips

    def z_peer(self, step):
        return (self.s, self.t, self.z_at(step) * 2 + self.c)

    def greet(self):
        barrier = pltpu.get_barrier_semaphore()
        peers = [self.x_peer, self.y_peer, self.core_peer]
        peers += [self.z_peer(step) for step in range(1, self.chips)]
        for peer in peers:
            pl.semaphore_signal(barrier, inc=1, device_id=peer, device_id_type=MESH)
        pl.semaphore_wait(barrier, len(peers))


def remote(src, dst, send, recv, peer):
    return pltpu.make_async_remote_copy(
        src_ref=src,
        dst_ref=dst,
        send_sem=send,
        recv_sem=recv,
        device_id=peer,
        device_id_type=MESH,
    )


def key_mask(rows, seq):
    return lax.broadcasted_iota(jnp.int32, (rows, rows), 1) < seq


def head_lanes(which):
    return lax.broadcasted_iota(jnp.int32, (1, 2 * HD), 1) // HD == which


def attend(joined, mixed, seq):
    rows, width = mixed.shape
    keep = key_mask(rows, seq)
    for pair in range(width // (2 * HD)):
        lanes = slice(pair * 2 * HD, (pair + 1) * 2 * HD)
        query = joined[:, lanes] * SCALE
        keys = joined[:, width + lanes.start : width + lanes.stop]
        values = joined[:, 2 * width + lanes.start : 2 * width + lanes.stop]
        total = None
        for which in range(2):
            own = head_lanes(which)
            scores = dot(query, jnp.where(own, keys, 0.0), 1, 1)
            scores = jnp.where(keep, scores, -3e38)
            weights = jnp.exp(scores - jnp.max(scores, -1, keepdims=True))
            probs = weights / jnp.sum(weights, -1, keepdims=True)
            part = dot(probs, jnp.where(own, values, 0.0), 1, 0)
            total = part if total is None else total + part
        mixed[:, lanes] = total


def attend_back(joined, mixed, grad_mixed, grad_joined, seq):
    rows, width = mixed.shape
    keep = key_mask(rows, seq)
    for pair in range(width // (2 * HD)):
        lanes = slice(pair * 2 * HD, (pair + 1) * 2 * HD)
        query = joined[:, lanes] * SCALE
        keys = joined[:, width + lanes.start : width + lanes.stop]
        values = joined[:, 2 * width + lanes.start : 2 * width + lanes.stop]
        grad = grad_mixed[:, lanes]
        product = grad * mixed[:, lanes]
        grads = [None, None, None]
        for which in range(2):
            own = head_lanes(which)
            own_keys = jnp.where(own, keys, 0.0)
            scores = dot(query, own_keys, 1, 1)
            scores = jnp.where(keep, scores, -3e38)
            weights = jnp.exp(scores - jnp.max(scores, -1, keepdims=True))
            probs = weights / jnp.sum(weights, -1, keepdims=True)
            own_grad = jnp.where(own, grad, 0.0)
            row_dot = jnp.sum(jnp.where(own, product, 0.0), -1, keepdims=True)
            grad_probs = dot(grad, jnp.where(own, values, 0.0), 1, 1)
            grad_scores = probs * (grad_probs - row_dot)
            parts = (
                dot(grad_scores, own_keys, 1, 0) * SCALE,
                dot(grad_scores, jnp.where(own, query, 0.0), 0, 0),
                dot(probs, own_grad, 0, 0),
            )
            grads = [b if a is None else a + b for a, b in zip(grads, parts)]
        for number, part in enumerate(grads):
            start = number * width + lanes.start
            grad_joined[:, start : start + 2 * HD] = part


def phi_big(value):
    return 0.5 * (1.0 + lax.erf(value * 0.7071067811865476))


def phi_small(value):
    return jnp.exp(-0.5 * value * value) * 0.3989422804014327


class Vectors:
    def __init__(self, ref, width, hidden):
        self.ref, self.width, self.hidden = ref, width, hidden

    def gain(self, which):
        return self.ref[which : which + 1, :]

    def shift(self, which):
        return self.ref[2 + which : 3 + which, :]

    def query(self):
        return self.ref[8:9, 0 : self.width]

    def value(self):
        return self.ref[8:9, self.width : 2 * self.width]

    def up(self, row):
        return self.ref[9 + row : 10 + row, :]


def add_rows(target, sources, step):
    rows = target.shape[0]

    @pl.loop(0, rows // step)
    def _(index):
        here = pl.ds(pl.multiple_of(index * step, 8), step)
        total = target[here, :]
        for source in sources:
            total = total + source[here, :]
        target[here, :] = total


def forward_kernel(
    chips,
    seq,
    sent_rows,
    x_in,
    live,
    vec_in,
    wq,
    wo,
    wu,
    wd,
    out_all,
    vec,
    hs,
    mid,
    gq_out,
    go_out,
    gu_out,
    gd_out,
    n1_out,
    n2_out,
    joined_out,
    mixed_out,
    pre_out,
    gq,
    go,
    gu,
    gd,
    n1,
    n2,
    joined,
    mixed,
    pre,
    hidden,
    received,
    sending,
    vs,
    vy,
    vc,
    vz,
    y_send,
    y_recv,
    v_send,
    v_recv,
    zs,
    zr,
    xs,
    xr,
    cs,
    cr,
    local,
    save,
):
    here = Place(chips)
    s, c, z = here.s, here.c, here.z
    shards = (wq, wo, wu, wd)
    whole = (gq, go, gu, gd)
    block = wq.shape[0]
    rows, depth = x_in.shape
    width = go.shape[2]
    tail = rows - sent_rows
    for buffer in (n1, n2):
        for layer in range(2):
            buffer[layer, 1, sent_rows:rows, :] = jnp.zeros((tail, depth), F32)
    for index in range(received.shape[0]):
        received[index, sent_rows:rows, :] = jnp.zeros((tail, depth), F32)
    vs[...] = vec_in[...]
    here.greet()

    def rows_of(matrix, layer, step, core):
        start = pl.multiple_of((here.z_at(step) * 2 + core) * block, 8)
        return whole[matrix].at[layer, pl.ds(start, block), :]

    departing = []

    def launch(copy):
        copy.start()
        departing.append(copy)
        return copy

    def departed(copy):
        copy.wait_send()
        departing[:] = [item for item in departing if item is not copy]

    def z_copy(matrix, step):
        return remote(
            shards[matrix],
            rows_of(matrix, s, 0, c),
            zs.at[matrix, step - 1],
            zr.at[matrix, step - 1],
            here.z_peer(step),
        )

    def x_copy(matrix, step, src=None):
        spot = rows_of(matrix, s, chips - step, c)
        return remote(
            spot if src is None else src,
            spot,
            xs.at[matrix, step],
            xr.at[matrix, step],
            here.x_peer,
        )

    def c_copy(kind, matrix, step, src=None):
        spot = rows_of(matrix, s if kind == 0 else 1 - s, chips - step, c)
        return remote(
            spot if src is None else src,
            spot,
            cs.at[kind, matrix, step],
            cr.at[kind, matrix, step],
            here.core_peer,
        )

    def z_arrived(matrix, step):
        spot = rows_of(matrix, s, chips - step, c)
        pltpu.make_async_copy(spot, spot, zr.at[matrix, step - 1]).wait()

    def x_arrived(matrix, step):
        spot = rows_of(matrix, 1 - s, chips - step, c)
        pltpu.make_async_copy(spot, spot, xr.at[matrix, step]).wait()

    def c_arrived(kind, matrix, step):
        spot = rows_of(matrix, s if kind == 0 else 1 - s, chips - step, 1 - c)
        pltpu.make_async_copy(spot, spot, cr.at[kind, matrix, step]).wait()

    def exchange_vectors():
        copy = remote(
            vs.at[pl.ds(0, 8)], vy, v_send.at[0], v_recv.at[0], here.y_peer
        )
        copy.start()
        copy.wait()
        vs[0:8, :] = vs[0:8, :] + vy[...]
        copy = remote(vs, vc, v_send.at[1], v_recv.at[1], here.core_peer)
        copy.start()
        copy.wait()
        vs[...] = vs[...] + vc[...]
        copies = []
        for step in range(1, chips):
            copy = remote(
                vs,
                vz.at[step - 1],
                v_send.at[1 + step],
                v_recv.at[1 + step],
                here.z_peer(step),
            )
            copy.start()
            copies.append(copy)
        for copy in copies:
            copy.wait()
        total = vs[...]
        for step in range(1, chips):
            total = total + vz[step - 1]
        vec[s] = total
        copy = remote(
            vec.at[s], vec.at[s], v_send.at[chips + 1], v_recv.at[chips + 1], here.x_peer
        )
        copy.start()
        copy.wait_send()
        spot = vec.at[1 - s]
        pltpu.make_async_copy(spot, spot, v_recv.at[chips + 1]).wait()

    exchange_vectors()

    own_copies = []
    for matrix in range(4):
        for step in range(1, chips):
            launch(z_copy(matrix, step))
        launch(x_copy(matrix, 0, shards[matrix]))
        launch(c_copy(0, matrix, 0, shards[matrix]))
        copy = pltpu.make_async_copy(
            shards[matrix], rows_of(matrix, s, 0, c), local.at[matrix]
        )
        copy.start()
        own_copies.append(copy)


    saves = {}

    def keep(name, src, dst, sem):
        copy = pltpu.make_async_copy(src, dst, save.at[sem])
        copy.start()
        saves[name] = copy

    def before_write(name):
        if name in saves:
            saves.pop(name).wait()

    def own_service(matrix):
        for step in range(1, chips):
            z_arrived(matrix, step)
            launch(x_copy(matrix, step))
            launch(c_copy(0, matrix, step))

    def other_service(matrix):
        for step in range(chips):
            x_arrived(matrix, step)
            launch(c_copy(1, matrix, step))

    def finish(layer, matrix):
        kind = s if layer == 0 else 1 - s

        @pl.when(kind == 0)
        def _():
            own_copies[matrix].wait()

        for step in range(chips):
            start = pl.multiple_of((here.z_at(step) * 2 + 1 - c) * block, 8)
            spot = whole[matrix].at[layer, pl.ds(start, block), :]
            pltpu.make_async_copy(
                spot, spot, cr.at[kind, matrix, (chips - step) % chips]
            ).wait()
        keep(
            "whole%d%d" % (layer, matrix),
            whole[matrix].at[layer],
            (gq_out, go_out, gu_out, gd_out)[matrix].at[layer],
            14 + 4 * layer + matrix,
        )

    hs[0] = x_in[...]

    def y_copy(src, dst, index):
        return launch(
            remote(
                src.at[pl.ds(0, sent_rows)],
                dst.at[pl.ds(0, sent_rows)],
                y_send.at[index],
                y_recv.at[index],
                here.y_peer,
            )
        )

    send_of = None
    for layer in range(2):
        vectors = Vectors(vec.at[layer], width, None)
        unit, _ = normalize(hs[layer])
        n1[layer, 0] = unit * vectors.gain(0) + vectors.shift(0)
        arrive = y_copy(n1.at[layer, 0], n1.at[layer, 1], 4 * layer)
        before_write("joined")
        before_write("mixed")
        if layer == 0:
            own_service(0)
            other_service(0)
        finish(layer, 0)
        for image in range(2):
            if image == 1:
                if layer == 0:
                    own_service(1)
                    other_service(1)
                finish(layer, 1)
                arrive.wait_recv()
            source = n1.at[layer, image]
            for part in range(3):
                lanes = slice(part * width, (part + 1) * width)
                value = dot(source[...], gq[layer, :, lanes], 1, 0)
                if part == 0:
                    value = value + vectors.query()
                if part == 2:
                    value = value + vectors.value()
                joined[image, :, lanes] = value
            attend(joined.at[image], mixed.at[image], seq)
        if send_of is not None:
            departed(send_of)
        sending[...] = dot(mixed[1], go[layer], 1, 1)
        send_of = y_copy(sending, received.at[2 * layer], 4 * layer + 1)
        middle = hs[layer] + dot(mixed[0], go[layer], 1, 1) + vectors.shift(2)
        keep("n1", n1.at[layer], n1_out.at[layer], 4 + layer)
        keep("joined", joined, joined_out.at[layer], 6 + layer)
        keep("mixed", mixed, mixed_out.at[layer], 8 + layer)
        saves["n1%d" % layer] = saves.pop("n1")
        send_of.wait_recv()
        middle = middle + received[2 * layer]
        mid[layer] = middle
        unit, _ = normalize(middle)
        n2[layer, 0] = unit * vectors.gain(1) + vectors.shift(1)
        arrive = y_copy(n2.at[layer, 0], n2.at[layer, 1], 4 * layer + 2)
        before_write("pre")
        if layer == 0:
            own_service(2)
            other_service(2)
        finish(layer, 2)
        for image in range(2):
            if image == 1:
                arrive.wait_recv()
            source = n2.at[layer, image]
            for part in range(pre.shape[2] // depth):
                lanes = slice(part * depth, (part + 1) * depth)
                value = dot(source[...], gu[layer, :, lanes], 1, 0) + vectors.up(part)
                pre[image, :, lanes] = value
                hidden[image, :, lanes] = value * phi_big(value)
        if layer == 0:
            own_service(3)
            other_service(3)
        finish(layer, 3)
        departed(send_of)
        sending[...] = dot(hidden[1], gd[layer], 1, 1)
        send_of = y_copy(sending, received.at[2 * layer + 1], 4 * layer + 3)
        keep("n2%d" % layer, n2.at[layer], n2_out.at[layer], 10 + layer)
        keep("pre", pre, pre_out.at[layer], 12 + layer)
        result = mid[layer] + dot(hidden[0], gd[layer], 1, 1) + vectors.shift(3)
        send_of.wait_recv()
        result = (result + received[2 * layer + 1]) * live[:, 0:1]
        out_all[layer] = result
        if layer == 0:
            hs[1] = result

    for saved in saves.values():
        saved.wait()
    for item in departing:
        item.wait_send()


def forward(chips, seq, x_in, live, vec_in, wq, wo, wu, wd):
    rows, depth = x_in.shape
    sent_rows = up_to(seq, 8)
    width = wo.shape[1]
    hidden = wu.shape[1]
    widths = (wq.shape[1], width, hidden, hidden)
    whole = [(2, depth, w) for w in widths]
    any_space = pl.BlockSpec(memory_space=pl.ANY)
    vmem = pl.BlockSpec(memory_space=pltpu.VMEM)
    outs = [
        ((2, rows, depth), vmem),
        ((2,) + vec_in.shape, vmem),
        ((2, rows, depth), vmem),
        ((2, rows, depth), vmem),
        *[(w, any_space) for w in whole],
        ((2, 2, rows, depth), any_space),
        ((2, 2, rows, depth), any_space),
        ((2, 2, rows, 3 * width), any_space),
        ((2, 2, rows, width), any_space),
        ((2, 2, rows, hidden), any_space),
    ]
    sems = pltpu.SemaphoreType.DMA
    scratch = [
        *[pltpu.VMEM(w, F32) for w in whole],
        pltpu.VMEM((2, 2, rows, depth), F32),
        pltpu.VMEM((2, 2, rows, depth), F32),
        pltpu.VMEM((2, rows, 3 * width), F32),
        pltpu.VMEM((2, rows, width), F32),
        pltpu.VMEM((2, rows, hidden), F32),
        pltpu.VMEM((2, rows, hidden), F32),
        pltpu.VMEM((4, rows, depth), F32),
        pltpu.VMEM((rows, depth), F32),
        pltpu.VMEM(vec_in.shape, F32),
        pltpu.VMEM((8, depth), F32),
        pltpu.VMEM(vec_in.shape, F32),
        pltpu.VMEM((chips - 1,) + vec_in.shape, F32),
        sems((8,)),
        sems((8,)),
        sems((chips + 2,)),
        sems((chips + 2,)),
        sems((4, chips - 1)),
        sems((4, chips - 1)),
        sems((4, chips)),
        sems((4, chips)),
        sems((2, 4, chips)),
        sems((2, 4, chips)),
        sems((4,)),
        sems((22,)),
    ]
    return pl.pallas_call(
        functools.partial(forward_kernel, chips, seq, sent_rows),
        out_shape=[jax.ShapeDtypeStruct(shape, F32) for shape, _ in outs],
        in_specs=[vmem] * 3 + [any_space] * 4,
        out_specs=[spec for _, spec in outs],
        scratch_shapes=scratch,
        compiler_params=pltpu.CompilerParams(
            collective_id=0, has_side_effects=True, vmem_limit_bytes=VMEM_BYTES
        ),
        name="forward_both",
    )(x_in, live, vec_in, wq, wo, wu, wd)


def backward_kernel(
    chips,
    seq,
    sent_rows,
    cot,
    live,
    vec,
    out_all,
    hs_in,
    mid_in,
    gq_in,
    go_in,
    gu_in,
    gd_in,
    n1_in,
    n2_in,
    joined_in,
    mixed_in,
    pre_in,
    gin,
    gvec,
    outq,
    outo,
    outu,
    outd,
    gin_x,
    out_x,
    rcq,
    rco,
    rcu,
    rcd,
    rxq,
    rxo,
    rxu,
    rxd,
    rzq,
    rzo,
    rzu,
    rzd,
    wb,
    wu,
    hs,
    mid,
    n1,
    n2,
    joined,
    mixed,
    pre,
    hidden,
    grad_all,
    mid_all,
    received,
    sending,
    own_part,
    grad_mixed,
    grad_joined,
    aq,
    ao,
    au,
    ad,
    tile,
    fetched,
    vc,
    vy,
    vz,
    vx,
    y_send,
    y_recv,
    loads,
    cs,
    cl,
    cr,
    xs,
    xr,
    zs,
    zr,
    fetch_sem,
    v_send,
    v_recv,
    g_send,
    g_recv,
):
    here = Place(chips)
    s, c, z = here.s, here.c, here.z
    rows, depth = cot.shape
    width = mixed.shape[2]
    width_ff = wu.shape[1]
    tail = rows - sent_rows
    mine = (aq, ao, au, ad)
    from_core = (rcq, rco, rcu, rcd)
    from_x = (rxq, rxo, rxu, rxd)
    from_z = (rzq, rzo, rzu, rzd)
    outs = (outq, outo, outu, outd)
    block = outq.shape[0]
    small = 24 if block % 24 == 0 else block
    for buffer in (grad_all, mid_all):
        for layer in range(2):
            buffer[layer, 1, sent_rows:rows, :] = jnp.zeros((tail, depth), F32)
    for index in range(received.shape[0]):
        received[index, sent_rows:rows, :] = jnp.zeros((tail, depth), F32)
    gvec[...] = jnp.zeros(gvec.shape, F32)

    wq, wo = wb.at[:, 0 : 3 * width], wb.at[:, 3 * width : 4 * width]
    sources = dict(
        wd=(gd_in, wb),
        pre=(pre_in, pre),
        wu=(gu_in, wu),
        n2=(n2_in, n2),
        mid=(mid_in, mid),
        joined=(joined_in, joined),
        mixed=(mixed_in, mixed),
        n1=(n1_in, n1),
        hs=(hs_in, hs),
        wo=(go_in, wo),
        wq=(gq_in, wq),
    )
    order = list(sources)
    loading = {}

    def load(name, layer):
        src, dst = sources[name]
        copy = pltpu.make_async_copy(src.at[layer], dst, loads.at[order.index(name)])
        copy.start()
        loading[name] = copy

    def loaded(name):
        loading.pop(name).wait()

    for name in order[:-2]:
        load(name, 1)
    here.greet()
    departing = []

    def launch(copy):
        copy.start()
        departing.append(copy)
        return copy

    def y_copy(src, dst, index):
        return launch(
            remote(
                src.at[pl.ds(0, sent_rows)],
                dst.at[pl.ds(0, sent_rows)],
                y_send.at[index],
                y_recv.at[index],
                here.y_peer,
            )
        )

    def departed(copy):
        copy.wait_send()
        departing[:] = [item for item in departing if item is not copy]

    x_arrivals = [
        launch(remote(out_all.at[1 - s], out_x, g_send.at[0], g_recv.at[0], here.x_peer))
    ]


    def tile_copies(slot, matrix, layer, number, start, size, step):
        lanes = pl.ds(start, size)
        spots = []
        for core in (1 - c, c):
            first = pl.multiple_of((here.z_at(step) * 2 + core) * block, 8)
            spots.append(tile.at[slot, pl.ds(first, block), pl.ds(0, size)])
        return (
            remote(
                spots[0],
                from_core[matrix].at[layer, step, :, lanes],
                cs.at[slot, step],
                cr.at[layer, matrix, number, step],
                here.core_peer,
            ),
            pltpu.make_async_copy(
                spots[1], mine[matrix].at[layer, step, :, lanes], cl.at[slot, step]
            ),
        )

    in_slot = [None, None]
    next_slot = [0]

    def settle(slot):
        if in_slot[slot] is not None:
            what = in_slot[slot]
            in_slot[slot] = None

            @pl.loop(0, chips)
            def _(step):
                away, kept = tile_copies(slot, *what, step)
                away.wait_send()
                kept.wait()

    def tiles_of(matrix):
        size = width if matrix < 2 else depth
        return [(n, n * size, size) for n in range(mine[matrix].shape[3] // size)]

    def flat(ref):
        return ref[...].reshape(2 * rows, ref.shape[-1])

    def product(matrix, layer, left, right):
        both = flat(left)
        for number, start, size in tiles_of(matrix):
            slot = next_slot[0]
            next_slot[0] = 1 - slot
            settle(slot)
            piece = right[:, :, start : start + size].reshape(2 * rows, size)
            tile[slot, :, 0:size] = dot(both, piece, 0, 0)
            what = (matrix, layer, number, start, size)

            @pl.loop(0, chips)
            def _(step):
                away, kept = tile_copies(slot, *what, step)
                away.start()
                kept.start()

            in_slot[slot] = what

    def fetch(src, dst):
        copy = pltpu.make_async_copy(src, dst, fetch_sem)
        copy.start()
        copy.wait()

    def x_grad(matrix, layer, step):
        return remote(
            mine[matrix].at[layer, step],
            from_x[matrix].at[step],
            xs.at[matrix, step],
            xr.at[matrix, step],
            here.x_peer,
        )

    def z_grad(matrix, layer, step):
        return remote(
            mine[matrix].at[layer, step],
            from_z[matrix].at[step - 1],
            zs.at[matrix, step - 1],
            zr.at[matrix, step - 1],
            here.z_peer(step),
        )

    def core_add(matrix, layer):
        for slot in range(2):
            if in_slot[slot] is not None and in_slot[slot][:2] == (matrix, layer):
                settle(slot)

        lanes = mine[matrix].shape[3]
        for number, start, size in tiles_of(matrix):

            @pl.loop(0, chips)
            def _(step):
                tile_copies(0, matrix, layer, number, start, size, step)[0].wait_recv()

        fetch(from_core[matrix].at[layer], fetched.at[:, :, pl.ds(0, lanes)])

        @pl.loop(0, chips)
        def _(step):
            add_rows(
                mine[matrix].at[layer, step],
                [fetched.at[step, :, pl.ds(0, lanes)]],
                small,
            )

            @pl.when(s != layer)
            def _():
                x_grad(matrix, layer, step).start()

    def x_add(matrix, layer):
        lanes = mine[matrix].shape[3]

        @pl.when(s == layer)
        def _():
            @pl.loop(1, chips + 1)
            def _(number):
                step = number % chips
                x_grad(matrix, layer, step).wait_recv()
                spot = fetched.at[0, :, pl.ds(0, lanes)]
                fetch(from_x[matrix].at[step], spot)
                add_rows(mine[matrix].at[layer, step], [spot], small)

                @pl.when(step != 0)
                def _():
                    z_grad(matrix, layer, step).start()

    def z_sum(matrix, layer):
        lanes = mine[matrix].shape[3]

        @pl.when(s == layer)
        def _():
            @pl.loop(1, chips)
            def _(step):
                z_grad(matrix, layer, step).wait_recv()

            spot = fetched.at[pl.ds(0, chips - 1), :, pl.ds(0, lanes)]
            fetch(from_z[matrix], spot)
            outs[matrix][...] = mine[matrix][layer, 0]
            add_rows(
                outs[matrix],
                [fetched.at[step, :, pl.ds(0, lanes)] for step in range(chips - 1)],
                small,
            )

    def total(value):
        return jnp.sum(value, 0, keepdims=True)

    send_of = None
    for layer in (1, 0):
        vectors = Vectors(vec.at[layer], width, None)
        incoming = (cot[...] if layer == 1 else gin[1]) * live[:, 0:1]
        grad_all[layer, 0] = incoming
        base = 4 * (1 - layer)
        arrive = y_copy(grad_all.at[layer, 0], grad_all.at[layer, 1], base)
        gvec[layer, 5:6, :] = total(incoming)
        if layer == 0:
            core_add(0, 1)
        loaded("wd")
        loaded("pre")
        loaded("wu")
        for image in range(2):
            if image == 1:
                arrive.wait_recv()
            for part in range(width_ff // depth):
                lanes = slice(part * depth, (part + 1) * depth)
                grad_hidden = dot(grad_all[layer, image], wb[:, lanes], 1, 0)
                value = pre[image, :, lanes]
                upper = phi_big(value)
                hidden[image, :, lanes] = value * upper
                pre[image, :, lanes] = grad_hidden * (upper + value * phi_small(value))
            if image == 1:
                load("wo", layer)
                load("wq", layer)
                if send_of is not None:
                    departed(send_of)
                sending[...] = dot(pre[1], wu[...], 1, 1)
                send_of = y_copy(sending, received.at[2 * (1 - layer)], base + 1)
            else:
                own_part[...] = dot(pre[0], wu[...], 1, 1)
        if layer == 1:
            load("wu", 0)
        for part in range(width_ff // depth):
            lanes = slice(part * depth, (part + 1) * depth)
            gvec[layer, 9 + part : 10 + part, :] = total(pre[0, :, lanes]) + total(
                pre[1, :, lanes]
            )
        product(3, layer, grad_all.at[layer], hidden)
        loaded("n2")
        product(2, layer, n2, pre)
        if layer == 1:
            load("pre", 0)
            load("n2", 0)
        core_add(3, layer)
        loaded("mid")
        unit, inverse = normalize(mid[...])
        if layer == 1:
            load("mid", 0)
        send_of.wait_recv()
        grad_second = own_part[...] + received[2 * (1 - layer)]
        gvec[layer, 1:2, :] = total(grad_second * unit)
        gvec[layer, 3:4, :] = total(grad_second)
        grad_middle = grad_all[layer, 0] + normalize_back(
            grad_second * vectors.gain(1), unit, inverse
        )
        mid_all[layer, 0] = grad_middle
        arrive = y_copy(mid_all.at[layer, 0], mid_all.at[layer, 1], base + 2)
        gvec[layer, 4:5, :] = total(grad_middle)
        core_add(2, layer)
        if layer == 0:
            x_add(3, 1)
        loaded("wo")
        loaded("joined")
        loaded("mixed")
        loaded("wq")
        for image in range(2):
            if image == 1:
                arrive.wait_recv()
            grad_mixed[...] = dot(mid_all[layer, image], wo[...], 1, 0)
            attend_back(
                joined.at[image], mixed.at[image], grad_mixed, grad_joined.at[image], seq
            )
            if image == 1:
                departed(send_of)
                sending[...] = dot(grad_joined[1], wq[...], 1, 1)
                send_of = y_copy(sending, received.at[2 * (1 - layer) + 1], base + 3)
            else:
                own_part[...] = dot(grad_joined[0], wq[...], 1, 1)
        if layer == 1:
            load("wd", 0)
            load("joined", 0)
        product(1, layer, mid_all.at[layer], mixed)
        loaded("n1")
        product(0, layer, n1, grad_joined)
        if layer == 1:
            load("mixed", 0)
            load("n1", 0)
        core_add(1, layer)
        gvec[layer, 8:9, 0:width] = total(grad_joined[0, :, 0:width]) + total(
            grad_joined[1, :, 0:width]
        )
        gvec[layer, 8:9, width : 2 * width] = total(
            grad_joined[0, :, 2 * width : 3 * width]
        ) + total(grad_joined[1, :, 2 * width : 3 * width])
        loaded("hs")
        unit, inverse = normalize(hs[...])
        if layer == 1:
            load("hs", 0)
        send_of.wait_recv()
        grad_first = own_part[...] + received[2 * (1 - layer) + 1]
        gvec[layer, 0:1, :] = total(grad_first * unit)
        gvec[layer, 2:3, :] = total(grad_first)
        gin[layer] = mid_all[layer, 0] + normalize_back(
            grad_first * vectors.gain(0), unit, inverse
        )
    core_add(0, 0)
    x_arrivals.append(
        launch(remote(gin.at[1 - s], gin_x, g_send.at[1], g_recv.at[1], here.x_peer))
    )
    copy = launch(remote(gvec, vy, v_send.at[0], v_recv.at[0], here.y_peer))
    departed(copy)
    copy.wait_recv()
    gvec[:, 0:8, :] = gvec[:, 0:8, :] + vy[:, 0:8, :]
    copy = launch(remote(gvec, vc, v_send.at[1], v_recv.at[1], here.core_peer))
    departed(copy)
    copy.wait_recv()
    gvec[...] = gvec[...] + vc[...]
    copies = []
    for step in range(1, chips):
        copies.append(
            launch(
                remote(
                    gvec,
                    vz.at[step - 1],
                    v_send.at[1 + step],
                    v_recv.at[1 + step],
                    here.z_peer(step),
                )
            )
        )
    x_add(3, 0)
    x_add(2, 1)
    for copy in copies:
        departed(copy)
        copy.wait_recv()
    for step in range(1, chips):
        gvec[...] = gvec[...] + vz[step - 1]
    copy = launch(
        remote(
            gvec.at[1 - s], vx, v_send.at[chips + 1], v_recv.at[chips + 1], here.x_peer
        )
    )
    x_add(2, 0)
    for matrix in (1, 0):
        x_add(matrix, 0)
        x_add(matrix, 1)
    copy.wait_recv()
    gvec[s] = gvec[s] + vx[...]
    for matrix in (3, 2, 1, 0):
        z_sum(matrix, 0)
        z_sum(matrix, 1)
    for slot in range(2):
        settle(slot)
    for item in x_arrivals:
        item.wait_recv()
    for item in departing:
        item.wait_send()
    for matrix in range(4):
        for layer in range(2):

            @pl.when(s != layer)
            def _():
                @pl.loop(0, chips)
                def _(step):
                    x_grad(matrix, layer, step).wait_send()

            @pl.when(s == layer)
            def _():
                @pl.loop(1, chips)
                def _(step):
                    z_grad(matrix, layer, step).wait_send()


def backward(chips, seq, cot, live, vec, out_all, hs, mid, whole, kept):
    rows, depth = cot.shape
    sent_rows = up_to(seq, 8)
    width, width_ff = whole[1].shape[2], whole[2].shape[2]
    widths = [w.shape[2] for w in whole]
    block = depth // (2 * chips)
    any_space = pl.BlockSpec(memory_space=pl.ANY)
    vmem = pl.BlockSpec(memory_space=pltpu.VMEM)
    outs = [
        ((2, rows, depth), vmem),
        (vec.shape, vmem),
        *[((block, w), vmem) for w in widths],
        ((rows, depth), any_space),
        ((rows, depth), any_space),
        *[((2, chips, block, w), any_space) for w in widths],
        *[((chips, block, w), any_space) for w in widths],
        *[((chips - 1, block, w), any_space) for w in widths],
    ]
    sems = pltpu.SemaphoreType.DMA
    scratch = [
        pltpu.VMEM((depth, width_ff), F32),
        pltpu.VMEM((depth, width_ff), F32),
        pltpu.VMEM((rows, depth), F32),
        pltpu.VMEM((rows, depth), F32),
        pltpu.VMEM((2, rows, depth), F32),
        pltpu.VMEM((2, rows, depth), F32),
        pltpu.VMEM((2, rows, 3 * width), F32),
        pltpu.VMEM((2, rows, width), F32),
        pltpu.VMEM((2, rows, width_ff), F32),
        pltpu.VMEM((2, rows, width_ff), F32),
        pltpu.VMEM((2, 2, rows, depth), F32),
        pltpu.VMEM((2, 2, rows, depth), F32),
        pltpu.VMEM((4, rows, depth), F32),
        pltpu.VMEM((rows, depth), F32),
        pltpu.VMEM((rows, depth), F32),
        pltpu.VMEM((rows, width), F32),
        pltpu.VMEM((2, rows, 3 * width), F32),
        *[pltpu.VMEM((2, chips, block, w), F32) for w in widths],
        pltpu.VMEM((2, depth, depth), F32),
        pltpu.VMEM((chips, block, width_ff), F32),
        pltpu.VMEM(vec.shape, F32),
        pltpu.VMEM(vec.shape, F32),
        pltpu.VMEM((chips - 1,) + vec.shape, F32),
        pltpu.VMEM(vec.shape[1:], F32),
        sems((8,)),
        sems((8,)),
        sems((11,)),
        sems((2, chips)),
        sems((2, chips)),
        sems((2, 4, 3, chips)),
        sems((4, chips)),
        sems((4, chips)),
        sems((4, chips - 1)),
        sems((4, chips - 1)),
        sems,
        sems((chips + 2,)),
        sems((chips + 2,)),
        sems((2,)),
        sems((2,)),
    ]
    results = pl.pallas_call(
        functools.partial(backward_kernel, chips, seq, sent_rows),
        out_shape=[jax.ShapeDtypeStruct(shape, F32) for shape, _ in outs],
        in_specs=[vmem] * 3 + [any_space] * 12,
        out_specs=[spec for _, spec in outs],
        scratch_shapes=scratch,
        compiler_params=pltpu.CompilerParams(
            collective_id=1, has_side_effects=True, vmem_limit_bytes=VMEM_BYTES
        ),
        name="backward_both",
    )(cot, live, vec, out_all, hs, mid, *whole, *kept)
    return results[:8]


def body(
    embedded,
    image_counts,
    cotangent,
    qkv_weight,
    qv_bias,
    out_weight,
    up_weight,
    up_bias,
    down_weight,
    norm_gains,
    shift_terms,
):
    groups = lax.axis_size("dp")
    chips = groups // 2
    tensors = lax.axis_size("tensor")
    s = lax.axis_index("section")
    t = lax.axis_index("tensor")
    d = lax.axis_index("dp")
    seq, depth = embedded.shape[3:]
    rows = up_to(seq, 16)
    block = qkv_weight.shape[1]
    width = qkv_weight.shape[3]
    width_ff = up_weight.shape[2]

    def padded(value):
        chosen = lax.dynamic_index_in_dim(value[:, 0, 0], s, 0, keepdims=False)
        return jnp.pad(chosen, ((0, rows - seq), (0, 0)))

    slot = s * tensors + t
    alive = (slot < image_counts[0]).astype(F32)
    inside = lax.broadcasted_iota(jnp.int32, (rows, 128), 0) < seq
    live = jnp.where(inside, alive, 0.0)

    def spread(pieces, parts, part):
        count, piece = pieces.shape
        tiled = jnp.broadcast_to(pieces[:, None, :], (count, parts, piece))
        mine = lax.broadcasted_iota(jnp.int32, (count, parts, piece), 1) == part
        return jnp.where(mine, tiled, 0.0).reshape(count, parts * piece)

    wide = jnp.concatenate([norm_gains[0], shift_terms[0], jnp.zeros_like(norm_gains[0])])
    wide = spread(wide, tensors * groups, t * groups + d)
    biases = spread(qv_bias[0], groups, d).reshape(-1, depth)
    ups = spread(up_bias, groups, d).reshape(-1, depth)
    packed = jnp.concatenate([wide, biases, ups])
    packed = jnp.pad(packed, ((0, up_to(packed.shape[0], 8) - packed.shape[0]), (0, 0)))

    shards = (
        qkv_weight[0].reshape(block, 3 * width),
        out_weight[0].T,
        up_weight[0],
        down_weight[0].T,
    )
    out_all, vec, hs, mid, gq, go, gu, gd, *kept = forward(
        chips, seq, padded(embedded), live, packed, *shards
    )
    gin, gvec, sum_q, sum_o, sum_u, sum_d, gin_x, out_x = backward(
        chips,
        seq,
        padded(cotangent),
        live,
        vec,
        out_all,
        hs,
        mid,
        (gq, go, gu, gd),
        kept,
    )
    vec_sum = lax.dynamic_index_in_dim(gvec, s, 0, keepdims=False)

    def both(own, other):
        mine = lax.dynamic_index_in_dim(own, s, 0, keepdims=False)[:seq]
        other = other[:seq]
        first = jnp.where(s == 0, mine, other)
        second = jnp.where(s == 0, other, mine)
        return jnp.stack([first, second])[None, :, None, None]

    piece = depth // (tensors * groups)
    wide = lax.dynamic_slice_in_dim(vec_sum[0:6], (t * groups + d) * piece, piece, 1)
    biases = vec_sum[8].reshape(2, width)
    biases = lax.dynamic_slice_in_dim(biases, d * (width // groups), width // groups, 1)
    count = width_ff // depth
    ups = vec_sum[9 : 9 + count].reshape(width_ff)
    ups = lax.dynamic_slice_in_dim(ups, d * (width_ff // groups), width_ff // groups, 0)
    return (
        both(out_all, out_x),
        both(gin, gin_x),
        sum_q.reshape(1, block, 3, width),
        biases[None],
        sum_o.T[None],
        sum_u[None],
        ups[None],
        sum_d.T[None],
        wide[None, 0:2],
        wide[None, 2:6],
    )


def solution(mesh):
    placed = (
        P(None, "dp", "tensor", None, None),
        P("dp"),
        P(None, "dp", "tensor", None, None),
        P("section", "dp", None, "tensor"),
        P("section", None, ("tensor", "dp")),
        P("section", "tensor", "dp"),
        P("section", "dp", "tensor"),
        P("section", ("tensor", "dp")),
        P("section", "tensor", "dp"),
        P("section", None, ("tensor", "dp")),
        P("section", None, ("tensor", "dp")),
    )
    return jax.shard_map(
        body,
        mesh=mesh,
        in_specs=placed,
        out_specs=(
            P("section", None, "dp", "tensor", None, None),
            P("section", None, "dp", "tensor", None, None),
            P("section", "dp", None, "tensor"),
            P("section", None, ("tensor", "dp")),
            P("section", "tensor", "dp"),
            P("section", "dp", "tensor"),
            P("section", ("tensor", "dp")),
            P("section", "tensor", "dp"),
            P("section", None, ("tensor", "dp")),
            P("section", None, ("tensor", "dp")),
        ),
        check_vma=False,
    )
```

```python
import functools

import jax
import jax.numpy as jnp
from jax import lax
from jax.experimental import pallas as pl
from jax.experimental.pallas import tpu as pltpu
from jax.sharding import PartitionSpec as P

HD = 64
SCALE = HD ** (-0.5)
EPS = 1e-06
HIGH = lax.Precision.HIGH
MESH = pl.DeviceIdType.MESH
VMEM_BYTES = 63 * 2**20
F32 = jnp.float32


def dot(left, right, left_dim, right_dim):
    return lax.dot_general(
        left,
        right,
        (((left_dim,), (right_dim,)), ((), ())),
        precision=HIGH,
        preferred_element_type=F32,
    )


def up_to(count, step):
    return -(-count // step) * step


def normalize(value):
    centred = value - jnp.mean(value, -1, keepdims=True)
    inverse = lax.rsqrt(jnp.mean(centred * centred, -1, keepdims=True) + EPS)
    return centred * inverse, inverse


def normalize_back(grad_unit, unit, inverse):
    return inverse * (
        grad_unit
        - jnp.mean(grad_unit, -1, keepdims=True)
        - unit * jnp.mean(grad_unit * unit, -1, keepdims=True)
    )


class Place:
    def __init__(self, chips):
        self.s = lax.axis_index("section")
        self.t = lax.axis_index("tensor")
        d = lax.axis_index("dp")
        self.chips = chips
        self.z = d // 2
        self.c = d % 2
        self.x_peer = (1 - self.s, self.t, d)
        self.y_peer = (self.s, 1 - self.t, d)
        self.core_peer = (self.s, self.t, self.z * 2 + 1 - self.c)

    def z_at(self, step):
        return (self.z + self.chips + step) % self.chips

    def z_peer(self, step):
        return (self.s, self.t, self.z_at(step) * 2 + self.c)

    def greet(self):
        barrier = pltpu.get_barrier_semaphore()
        peers = [self.x_peer, self.y_peer, self.core_peer]
        peers += [self.z_peer(step) for step in range(1, self.chips)]
        for peer in peers:
            pl.semaphore_signal(barrier, inc=1, device_id=peer, device_id_type=MESH)
        pl.semaphore_wait(barrier, len(peers))


    @property
    def relays(self):
        return self.chips == 4

    def arrivals(self):
        if not self.relays:
            return list(range(1, self.chips))
        near = jnp.where(self.z < 2, 3, 1)
        return [2, near, 4 - near]

    def departures(self):
        if not self.relays:
            return list(range(1, self.chips)) + [0]
        far = jnp.where(self.z < 2, 3, 1)
        return [far, 4 - far, 2, 0]

    @property
    def middle(self):
        return (self.z == 1) | (self.z == 2)

    def direct(self, step):
        if not self.relays or step == 2:
            return None
        return self.z <= 2 if step == 1 else self.z >= 1


def when(condition, action):
    if condition is None:
        action()
    else:
        pl.when(condition)(action)


def parts_of(rows):
    first = up_to(rows // 2, 8)
    return [(0, first), (first, rows)]


def remote(src, dst, send, recv, peer):
    return pltpu.make_async_remote_copy(
        src_ref=src,
        dst_ref=dst,
        send_sem=send,
        recv_sem=recv,
        device_id=peer,
        device_id_type=MESH,
    )


def key_mask(rows, seq):
    return lax.broadcasted_iota(jnp.int32, (rows, rows), 1) < seq


def head_lanes(which):
    return lax.broadcasted_iota(jnp.int32, (1, 2 * HD), 1) // HD == which


def attend(joined, mixed, seq):
    rows, width = mixed.shape
    keep = key_mask(rows, seq)
    for pair in range(width // (2 * HD)):
        lanes = slice(pair * 2 * HD, (pair + 1) * 2 * HD)
        query = joined[:, lanes] * SCALE
        keys = joined[:, width + lanes.start : width + lanes.stop]
        values = joined[:, 2 * width + lanes.start : 2 * width + lanes.stop]
        total = None
        for which in range(2):
            own = head_lanes(which)
            scores = dot(query, jnp.where(own, keys, 0.0), 1, 1)
            scores = jnp.where(keep, scores, -3e38)
            weights = jnp.exp(scores - jnp.max(scores, -1, keepdims=True))
            probs = weights / jnp.sum(weights, -1, keepdims=True)
            part = dot(probs, jnp.where(own, values, 0.0), 1, 0)
            total = part if total is None else total + part
        mixed[:, lanes] = total


def attend_back(joined, mixed, grad_mixed, grad_joined, seq):
    rows, width = mixed.shape
    keep = key_mask(rows, seq)
    for pair in range(width // (2 * HD)):
        lanes = slice(pair * 2 * HD, (pair + 1) * 2 * HD)
        query = joined[:, lanes] * SCALE
        keys = joined[:, width + lanes.start : width + lanes.stop]
        values = joined[:, 2 * width + lanes.start : 2 * width + lanes.stop]
        grad = grad_mixed[:, lanes]
        product = grad * mixed[:, lanes]
        grads = [None, None, None]
        for which in range(2):
            own = head_lanes(which)
            own_keys = jnp.where(own, keys, 0.0)
            scores = dot(query, own_keys, 1, 1)
            scores = jnp.where(keep, scores, -3e38)
            weights = jnp.exp(scores - jnp.max(scores, -1, keepdims=True))
            probs = weights / jnp.sum(weights, -1, keepdims=True)
            own_grad = jnp.where(own, grad, 0.0)
            row_dot = jnp.sum(jnp.where(own, product, 0.0), -1, keepdims=True)
            grad_probs = dot(grad, jnp.where(own, values, 0.0), 1, 1)
            grad_scores = probs * (grad_probs - row_dot)
            parts = (
                dot(grad_scores, own_keys, 1, 0) * SCALE,
                dot(grad_scores, jnp.where(own, query, 0.0), 0, 0),
                dot(probs, own_grad, 0, 0),
            )
            grads = [b if a is None else a + b for a, b in zip(grads, parts)]
        for number, part in enumerate(grads):
            start = number * width + lanes.start
            grad_joined[:, start : start + 2 * HD] = part


def phi_big(value):
    return 0.5 * (1.0 + lax.erf(value * 0.7071067811865476))


def phi_small(value):
    return jnp.exp(-0.5 * value * value) * 0.3989422804014327


class Vectors:
    def __init__(self, ref, width, hidden):
        self.ref, self.width, self.hidden = ref, width, hidden

    def gain(self, which):
        return self.ref[which : which + 1, :]

    def shift(self, which):
        return self.ref[2 + which : 3 + which, :]

    def query(self):
        return self.ref[8:9, 0 : self.width]

    def value(self):
        return self.ref[8:9, self.width : 2 * self.width]

    def up(self, row):
        return self.ref[9 + row : 10 + row, :]


def add_rows(target, sources, step):
    rows = target.shape[0]

    @pl.loop(0, rows // step)
    def _(index):
        here = pl.ds(pl.multiple_of(index * step, 8), step)
        total = target[here, :]
        for source in sources:
            total = total + source[here, :]
        target[here, :] = total


def forward_kernel(
    chips,
    seq,
    sent_rows,
    x_in,
    live,
    vec_in,
    wq,
    wo,
    wu,
    wd,
    out_all,
    vec,
    hs,
    mid,
    gq_out,
    go_out,
    gu_out,
    gd_out,
    n1_out,
    n2_out,
    joined_out,
    mixed_out,
    pre_out,
    gq,
    go,
    gu,
    gd,
    n1,
    n2,
    joined,
    mixed,
    pre,
    hidden,
    received,
    sending,
    vy,
    vc,
    vz,
    y_send,
    y_recv,
    v_send,
    v_recv,
    zs,
    zr,
    xs,
    xr,
    cs,
    cr,
    local,
    save,
):
    here = Place(chips)
    s, c, z = here.s, here.c, here.z
    shards = (wq, wo, wu, wd)
    whole = (gq, go, gu, gd)
    block = wq.shape[0]
    rows, depth = x_in.shape
    width = go.shape[2]
    tail = rows - sent_rows
    parts = parts_of(rows)
    for buffer in (n1, n2):
        for layer in range(2):
            buffer[layer, 1, sent_rows:rows, :] = jnp.zeros((tail, depth), F32)
    for index in range(received.shape[0]):
        received[index, sent_rows:rows, :] = jnp.zeros((tail, depth), F32)
    vec[s] = vec_in[...]
    here.greet()


    def x_first(matrix, layer):
        return layer == 0 and matrix < 2

    def spot(matrix, layer, back, core=None):
        start = (here.z_at(-back) * 2 + (c if core is None else core)) * block
        return whole[matrix].at[layer, pl.ds(pl.multiple_of(start, 8), block), :]

    def layer_of(kind):
        return s if kind == 0 else 1 - s

    def z_copy(kind, matrix, step, src=None):
        place = spot(matrix, layer_of(kind), 0)
        return remote(
            place if src is None else src,
            place,
            zs.at[kind, matrix, step],
            zr.at[kind, matrix, step],
            here.z_peer(step),
        )

    def z_relay(kind, matrix):
        place = spot(matrix, layer_of(kind), 2)
        step = jnp.where(z == 1, 3, 1)
        return remote(
            place,
            place,
            zs.at[kind, matrix, 0],
            zr.at[kind, matrix, 4 - step],
            here.z_peer(step),
        )

    def x_copy(matrix, back, src=None):
        place = spot(matrix, s, back)
        return remote(
            place if src is None else src,
            place,
            xs.at[matrix, back],
            xr.at[matrix, back],
            here.x_peer,
        )

    def c_copy(kind, matrix, back, src=None):
        place = spot(matrix, layer_of(kind), back)
        return remote(
            place if src is None else src,
            place,
            cs.at[kind, matrix, back],
            cr.at[kind, matrix, back],
            here.core_peer,
        )

    def landed(place, sem):
        pltpu.make_async_copy(place, place, sem).wait()

    def z_spread(kind, matrix, src=None):
        for step in [2, 1, 3] if here.relays else range(1, chips):
            copy = z_copy(kind, matrix, step, src)
            when(here.direct(step), copy.start)

    def z_event(layer, matrix, number):
        def action(kind, onward):
            back = here.arrivals()[number]
            landed(spot(matrix, layer_of(kind), back), zr.at[kind, matrix, back])
            if here.relays and number == 0:
                pl.when(here.middle)(z_relay(kind, matrix).start)
            if onward:
                x_copy(matrix, back).start()
            c_copy(kind, matrix, back).start()

        return lambda section: action(
            0 if section == layer else 1, section == layer and not x_first(matrix, layer)
        )

    def x_event(layer, matrix, number):
        def action():
            back = 0 if number < 0 else here.arrivals()[number]
            landed(spot(matrix, 1 - s, back), xr.at[matrix, back])
            if x_first(matrix, layer):
                z_spread(1, matrix)
            c_copy(1, matrix, back).start()

        return lambda section: action()

    def own_spread(section):
        for matrix in range(4):
            z_spread(0, matrix, shards[matrix])

    def both_of(matrix, layer, event, first=0, last=3):
        events = here_events[first:last]
        return [event(layer, matrix, number) for group in events for number in group]

    count = chips - 1
    here_events = [
        list(range(count * group // 3, count * (group + 1) // 3)) for group in range(3)
    ]

    def serve(of_zero, of_one):
        for section, events in ((0, of_zero), (1, of_one)):
            if events:

                @pl.when(s == section)
                def _():
                    for event in events:
                        event(section)

    def arrive(layer, matrix, first=0, last=3):
        return both_of(matrix, layer, z_event, first, last)

    def cross(layer, matrix, first=0, last=3):
        return both_of(matrix, layer, x_event, first, last)

    def cross_own(layer, matrix):
        return [x_event(layer, matrix, -1)]

    copy = remote(vec.at[s], vec.at[s], v_send.at[0], v_recv.at[0], here.x_peer)
    copy.start()
    copy.wait_send()
    landed(vec.at[1 - s], v_recv.at[0])
    vector_copies = []
    for step in range(1, chips):
        copy = remote(
            vec, vz.at[step - 1], v_send.at[step], v_recv.at[step], here.z_peer(step)
        )
        copy.start()
        vector_copies.append(copy)
    own_copies = []
    for matrix in range(4):
        x_copy(matrix, 0, shards[matrix]).start()
        c_copy(0, matrix, 0, shards[matrix]).start()
        copy = pltpu.make_async_copy(
            shards[matrix], spot(matrix, s, 0), local.at[matrix]
        )
        copy.start()
        own_copies.append(copy)
    serve([own_spread], [])
    for copy in vector_copies:
        copy.wait()
    for step in range(1, chips):
        vec[...] = vec[...] + vz[step - 1]
    copy = remote(vec, vc, v_send.at[chips], v_recv.at[chips], here.core_peer)
    copy.start()
    copy.wait()
    vec[...] = vec[...] + vc[...]
    copy = remote(vec, vy, v_send.at[chips + 1], v_recv.at[chips + 1], here.y_peer)
    copy.start()
    copy.wait()
    vec[:, 0:8, :] = vec[:, 0:8, :] + vy[:, 0:8, :]

    saves = {}

    def keep(name, src, dst, sem):
        copy = pltpu.make_async_copy(src, dst, save.at[sem])
        copy.start()
        saves[name] = copy

    def before_write(name):
        if name in saves:
            saves.pop(name).wait()

    def finish(layer, matrix):
        kind = s if layer == 0 else 1 - s

        @pl.when(kind == 0)
        def _():
            own_copies[matrix].wait()

        for back in range(chips):
            landed(spot(matrix, layer, back, 1 - c), cr.at[kind, matrix, back])
        keep(
            "whole%d%d" % (layer, matrix),
            whole[matrix].at[layer],
            (gq_out, go_out, gu_out, gd_out)[matrix].at[layer],
            14 + 4 * layer + matrix,
        )

    exchanges = {}

    def y_start(src, dst, index, part):
        start, stop = parts[part]
        span = pl.ds(start, min(stop, sent_rows) - start)
        copy = remote(
            src.at[span],
            dst.at[span],
            y_send.at[index, part],
            y_recv.at[index, part],
            here.y_peer,
        )
        copy.start()
        exchanges[index, part] = copy

    def y_wait(index, part):
        exchanges[index, part].wait_recv()

    def y_departed(index):
        for part in range(2):
            exchanges.pop((index, part)).wait_send()

    def begin(layer, part, value):
        span = slice(*parts[part])
        hs[layer, span] = value
        unit, _ = normalize(value)
        vectors = Vectors(vec.at[layer], width, None)
        n1[layer, 0, span] = unit * vectors.gain(0) + vectors.shift(0)
        y_start(n1.at[layer, 0], n1.at[layer, 1], 4 * layer, part)

    def project(layer, image, span):
        vectors = Vectors(vec.at[layer], width, None)
        for piece in range(3):
            lanes = slice(piece * width, (piece + 1) * width)
            value = dot(n1[layer, image, span], gq[layer, :, lanes], 1, 0)
            if piece == 0:
                value = value + vectors.query()
            if piece == 2:
                value = value + vectors.value()
            joined[image, span, lanes] = value

    def expand(layer, image, span):
        vectors = Vectors(vec.at[layer], width, None)
        for piece in range(pre.shape[2] // depth):
            lanes = slice(piece * depth, (piece + 1) * depth)
            value = dot(n2[layer, image, span], gu[layer, :, lanes], 1, 0)
            value = value + vectors.up(piece)
            pre[image, span, lanes] = value
            hidden[image, span, lanes] = value * phi_big(value)

    everything = slice(0, rows)
    for part in range(2):
        begin(0, part, x_in[slice(*parts[part])])
    for layer in range(2):
        vectors = Vectors(vec.at[layer], width, None)
        if layer == 0:
            serve(
                arrive(0, 0),
                cross_own(0, 0) + cross_own(0, 1) + [own_spread] + arrive(0, 0),
            )
        before_write("joined")
        before_write("mixed")
        finish(layer, 0)
        project(layer, 0, everything)
        attend(joined.at[0], mixed.at[0], seq)
        if layer == 0:
            serve(arrive(0, 1) + arrive(0, 2, 0, 1), arrive(0, 1))
        else:
            serve(cross(1, 2, 1, 3), arrive(1, 3, 1, 2))
        finish(layer, 1)
        mid[layer] = hs[layer] + dot(mixed[0], go[layer], 1, 1) + vectors.shift(2)
        for part in range(2):
            y_wait(4 * layer, part)
            project(layer, 1, slice(*parts[part]))
        attend(joined.at[1], mixed.at[1], seq)
        if layer == 1:
            y_departed(1)
        for part in range(2):
            span = slice(*parts[part])
            sending[0, span] = dot(mixed[1, span], go[layer], 1, 1)
            y_start(sending.at[0], received.at[2 * layer], 4 * layer + 1, part)
        keep("n1%d" % layer, n1.at[layer], n1_out.at[layer], 4 + layer)
        keep("joined", joined, joined_out.at[layer], 6 + layer)
        keep("mixed", mixed, mixed_out.at[layer], 8 + layer)
        if layer == 0:
            serve(
                arrive(0, 2, 1, 2),
                arrive(1, 0, 0, 1) + cross_own(0, 2) + arrive(1, 0, 1, 2),
            )
        else:
            serve(cross_own(1, 3) + cross(1, 3, 0, 1), arrive(1, 3, 2, 3))
        for part in range(2):
            span = slice(*parts[part])
            y_wait(4 * layer + 1, part)
            middle = mid[layer, span] + received[2 * layer, span]
            mid[layer, span] = middle
            unit, _ = normalize(middle)
            n2[layer, 0, span] = unit * vectors.gain(1) + vectors.shift(1)
            y_start(n2.at[layer, 0], n2.at[layer, 1], 4 * layer + 2, part)
        if layer == 0:
            serve(
                arrive(0, 2, 2, 3),
                arrive(1, 0, 2, 3) + cross(0, 2) + arrive(1, 1),
            )
        before_write("pre")
        finish(layer, 2)
        expand(layer, 0, everything)
        if layer == 0:
            for part in range(2):
                y_wait(2, part)
                expand(0, 1, slice(*parts[part]))
            serve(
                arrive(0, 3),
                arrive(1, 2, 0, 1)
                + cross_own(0, 3)
                + cross(0, 3, 0, 1)
                + arrive(1, 2, 1, 2)
                + cross(0, 3, 1, 2)
                + cross(0, 3, 2, 3)
                + arrive(1, 2, 2, 3),
            )
        else:
            serve(cross(1, 3, 1, 3), [])
            y_departed(3)
        finish(layer, 3)
        if layer == 1:
            out_all[layer] = mid[layer] + dot(hidden[0], gd[layer], 1, 1)
        for part in range(2):
            span = slice(*parts[part])
            if layer == 1:
                y_wait(6, part)
                expand(1, 1, span)
            sending[1, span] = dot(hidden[1, span], gd[layer], 1, 1)
            y_start(sending.at[1], received.at[2 * layer + 1], 4 * layer + 3, part)
        if layer == 0:
            out_all[layer] = mid[layer] + dot(hidden[0], gd[layer], 1, 1)
        keep("n2%d" % layer, n2.at[layer], n2_out.at[layer], 10 + layer)
        keep("pre", pre, pre_out.at[layer], 12 + layer)
        if layer == 0:
            serve(
                [
                    event
                    for matrix in (0, 1)
                    for event in cross_own(1, matrix) + cross(1, matrix)
                ]
                + cross_own(1, 2)
                + cross(1, 2, 0, 1),
                arrive(1, 3, 0, 1),
            )
        for part in range(2):
            span = slice(*parts[part])
            y_wait(4 * layer + 3, part)
            result = out_all[layer, span] + received[2 * layer + 1, span]
            result = (result + vectors.shift(3)) * live[span, 0:1]
            out_all[layer, span] = result
            if layer == 0:
                begin(1, part, result)

    for copy in saves.values():
        copy.wait()
    for copy in exchanges.values():
        copy.wait_send()
    for matrix in range(4):
        for kind in range(2):
            for back in range(chips):
                c_copy(kind, matrix, back).wait_send()
        x_copy(matrix, 0).wait_send()
        for section in range(2):

            def departures():
                kinds = [0] if section == 0 or not x_first(matrix, 0) else [0, 1]
                for kind in kinds:
                    for step in range(1, chips):
                        when(here.direct(step), z_copy(kind, matrix, step).wait_send)
                    if here.relays:
                        pl.when(here.middle)(z_relay(kind, matrix).wait_send)
                if not x_first(matrix, section):
                    for back in range(1, chips):
                        x_copy(matrix, back).wait_send()

            pl.when(s == section)(departures)


def forward(chips, seq, x_in, live, vec_in, wq, wo, wu, wd):
    rows, depth = x_in.shape
    sent_rows = up_to(seq, 8)
    width = wo.shape[1]
    hidden = wu.shape[1]
    widths = (wq.shape[1], width, hidden, hidden)
    whole = [(2, depth, w) for w in widths]
    any_space = pl.BlockSpec(memory_space=pl.ANY)
    vmem = pl.BlockSpec(memory_space=pltpu.VMEM)
    both = (2,) + vec_in.shape
    outs = [
        ((2, rows, depth), vmem),
        (both, vmem),
        ((2, rows, depth), vmem),
        ((2, rows, depth), vmem),
        *[(w, any_space) for w in whole],
        ((2, 2, rows, depth), any_space),
        ((2, 2, rows, depth), any_space),
        ((2, 2, rows, 3 * width), any_space),
        ((2, 2, rows, width), any_space),
        ((2, 2, rows, hidden), any_space),
    ]
    sems = pltpu.SemaphoreType.DMA
    scratch = [
        *[pltpu.VMEM(w, F32) for w in whole],
        pltpu.VMEM((2, 2, rows, depth), F32),
        pltpu.VMEM((2, 2, rows, depth), F32),
        pltpu.VMEM((2, rows, 3 * width), F32),
        pltpu.VMEM((2, rows, width), F32),
        pltpu.VMEM((2, rows, hidden), F32),
        pltpu.VMEM((2, rows, hidden), F32),
        pltpu.VMEM((4, rows, depth), F32),
        pltpu.VMEM((2, rows, depth), F32),
        pltpu.VMEM(both, F32),
        pltpu.VMEM(both, F32),
        pltpu.VMEM((chips - 1,) + both, F32),
        sems((8, 2)),
        sems((8, 2)),
        sems((chips + 2,)),
        sems((chips + 2,)),
        sems((2, 4, chips)),
        sems((2, 4, chips)),
        sems((4, chips)),
        sems((4, chips)),
        sems((2, 4, chips)),
        sems((2, 4, chips)),
        sems((4,)),
        sems((22,)),
    ]
    return pl.pallas_call(
        functools.partial(forward_kernel, chips, seq, sent_rows),
        out_shape=[jax.ShapeDtypeStruct(shape, F32) for shape, _ in outs],
        in_specs=[vmem] * 3 + [any_space] * 4,
        out_specs=[spec for _, spec in outs],
        scratch_shapes=scratch,
        compiler_params=pltpu.CompilerParams(
            collective_id=0, has_side_effects=True, vmem_limit_bytes=VMEM_BYTES
        ),
        name="forward_both",
    )(x_in, live, vec_in, wq, wo, wu, wd)


Q, O, U, D = range(4)
Z_FIRST = ((0, Q), (0, O))


def points():
    both = {
        (1, "e0"): [("core", 1, D)],
        (1, "e1"): [("send", 1, D), ("core", 1, U)],
        (1, "g0"): [("send", 1, U)],
        (1, "j0"): [("core", 1, O)],
        (0, "a"): [("send", 1, O), ("core", 1, Q)],
        (0, "b0"): [("send", 1, Q)],
        (0, "e0"): [("core", 0, D)],
        (0, "e1"): [("send", 0, D), ("core", 0, U)],
        (0, "g0"): [("send", 0, U)],
        (0, "j0"): [("core", 0, O)],
        (0, "t0"): [("send", 0, O), ("core", 0, Q)],
        (0, "t1"): [("send", 0, Q)],
    }
    one = {
        (0, "b1"): [("add", 1, D, 0), ("add", 1, D, 1)],
        (0, "d"): [("add", 1, D, 2)],
        (0, "g0"): [("add", 1, D, 3)],
        (0, "h"): [("add", 1, U, 0), ("add", 1, U, 1)],
        (0, "t2"): [("add", 1, U, 2)],
        (0, "t3"): [
            ("add", 1, U, 3),
            ("relay", 0, O),
            ("relay", 0, Q),
            *[("add", 1, O, n) for n in range(4)],
            ("sum", 0, O),
            ("sum", 0, Q),
            *[("add", 1, Q, n) for n in range(4)],
        ],
        (0, "t4"): [("sum", 1, m) for m in (D, U, O, Q)],
    }
    zero = {
        (0, "t2"): [("add", 0, D, 0), ("add", 0, D, 1)],
        (0, "t3"): [
            ("add", 0, D, 2),
            ("add", 0, D, 3),
            ("relay", 0, O),
            ("relay", 0, Q),
            *[("add", 0, U, n) for n in range(4)],
        ],
        (0, "t4"): [
            *[("sum", 0, m) for m in (O, Q, D, U)],
            ("last", 0, O),
            ("last", 0, Q),
        ],
    }
    return both, (zero, one)


def backward_kernel(
    chips,
    seq,
    sent_rows,
    cot,
    live,
    vec,
    out_all,
    hs_in,
    mid_in,
    gq_in,
    go_in,
    gu_in,
    gd_in,
    n1_in,
    n2_in,
    joined_in,
    mixed_in,
    pre_in,
    gin,
    gvec,
    outq,
    outo,
    outu,
    outd,
    gin_x,
    out_x,
    rcq,
    rco,
    rcu,
    rcd,
    rxq,
    rxo,
    rxu,
    rxd,
    rzq,
    rzo,
    rzu,
    rzd,
    wb,
    wu,
    hs,
    mid,
    n1,
    n2,
    joined,
    mixed,
    pre,
    hidden,
    grad_all,
    mid_all,
    received,
    sending,
    own_part,
    grad_mixed,
    grad_joined,
    aq,
    ao,
    au,
    ad,
    tile,
    fetched,
    single,
    vc,
    vy,
    vz,
    vx,
    y_send,
    y_recv,
    loads,
    cs,
    cl,
    cr,
    xs,
    xr,
    zs,
    zr,
    fetch_sem,
    single_sem,
    v_send,
    v_recv,
    g_send,
    g_recv,
):
    here = Place(chips)
    s, c, z = here.s, here.c, here.z
    rows, depth = cot.shape
    width = mixed.shape[2]
    width_ff = wu.shape[1]
    tail = rows - sent_rows
    parts = parts_of(rows)
    mine = (aq, ao, au, ad)
    from_core = (rcq, rco, rcu, rcd)
    from_x = (rxq, rxo, rxu, rxd)
    from_z = (rzq, rzo, rzu, rzd)
    outs = (outq, outo, outu, outd)
    block = outq.shape[0]
    small = 24 if block % 24 == 0 else block
    for buffer in (grad_all, mid_all):
        for layer in range(2):
            buffer[layer, 1, sent_rows:rows, :] = jnp.zeros((tail, depth), F32)
    for index in range(received.shape[0]):
        received[index, sent_rows:rows, :] = jnp.zeros((tail, depth), F32)
    gvec[...] = jnp.zeros(gvec.shape, F32)

    wq, wo = wb.at[:, 0 : 3 * width], wb.at[:, 3 * width : 4 * width]
    sources = dict(
        wd=(gd_in, wb),
        pre=(pre_in, pre),
        wu=(gu_in, wu),
        n2=(n2_in, n2),
        mid=(mid_in, mid),
        joined=(joined_in, joined),
        mixed=(mixed_in, mixed),
        n1=(n1_in, n1),
        hs=(hs_in, hs),
        wo=(go_in, wo),
        wq=(gq_in, wq),
    )
    order = list(sources)
    loading = {}

    def load(name, layer):
        src, dst = sources[name]
        copy = pltpu.make_async_copy(src.at[layer], dst, loads.at[order.index(name)])
        copy.start()
        loading[name] = copy

    def loaded(name):
        loading.pop(name).wait()

    for name in order[:-2]:
        load(name, 1)
    here.greet()
    departing = []

    def launch(copy):
        copy.start()
        departing.append(copy)
        return copy

    def departed(copy):
        copy.wait_send()
        departing[:] = [item for item in departing if item is not copy]

    exchanges = {}

    def y_start(src, dst, index, part):
        start, stop = parts[part]
        span = pl.ds(start, min(stop, sent_rows) - start)
        copy = remote(
            src.at[span],
            dst.at[span],
            y_send.at[index, part],
            y_recv.at[index, part],
            here.y_peer,
        )
        copy.start()
        exchanges[index, part] = copy

    def y_wait(index, part):
        exchanges[index, part].wait_recv()

    def y_departed(index):
        for part in range(2):
            exchanges.pop((index, part)).wait_send()

    x_arrivals = [
        launch(remote(out_all.at[1 - s], out_x, g_send.at[0], g_recv.at[0], here.x_peer))
    ]


    def tile_copies(slot, matrix, layer, number, start, size, step):
        lanes = pl.ds(start, size)
        spots = []
        for core in (1 - c, c):
            first = pl.multiple_of((here.z_at(step) * 2 + core) * block, 8)
            spots.append(tile.at[slot, pl.ds(first, block), pl.ds(0, size)])
        return (
            remote(
                spots[0],
                from_core[matrix].at[layer, step, :, lanes],
                cs.at[slot, step],
                cr.at[layer, matrix, number, step],
                here.core_peer,
            ),
            pltpu.make_async_copy(
                spots[1], mine[matrix].at[layer, step, :, lanes], cl.at[slot, step]
            ),
        )

    in_slot = [None, None]
    next_slot = [0]

    def settle(slot):
        if in_slot[slot] is not None:
            what = in_slot[slot]
            in_slot[slot] = None

            @pl.loop(0, chips)
            def _(step):
                away, kept = tile_copies(slot, *what, step)
                away.wait_send()
                kept.wait()

    def tiles_of(matrix):
        size = width if matrix < 2 else depth
        return [(n, n * size, size) for n in range(mine[matrix].shape[3] // size)]

    def flat(ref):
        return ref[...].reshape(2 * rows, ref.shape[-1])

    def product(matrix, layer, left, right):
        both = flat(left)
        for number, start, size in tiles_of(matrix):
            slot = next_slot[0]
            next_slot[0] = 1 - slot
            settle(slot)
            piece = right[:, :, start : start + size].reshape(2 * rows, size)
            tile[slot, :, 0:size] = dot(both, piece, 0, 0)
            what = (matrix, layer, number, start, size)

            @pl.loop(0, chips)
            def _(step):
                away, kept = tile_copies(slot, *what, step)
                away.start()
                kept.start()

            in_slot[slot] = what

    def add_from(src, target):
        lanes = target.shape[1]
        spot = single.at[:, pl.ds(0, lanes)]
        copy = pltpu.make_async_copy(src, spot, single_sem)
        copy.start()
        copy.wait()
        add_rows(target, [spot], small)

    def x_grad(matrix, layer, step):
        return remote(
            mine[matrix].at[layer, step],
            from_x[matrix].at[step],
            xs.at[matrix, step],
            xr.at[matrix, step],
            here.x_peer,
        )

    def z_grad(matrix, layer, step):
        return remote(
            mine[matrix].at[layer, step],
            from_z[matrix].at[layer, step],
            zs.at[layer, matrix, step],
            zr.at[layer, matrix, step],
            here.z_peer(step),
        )

    def z_left(matrix, layer):
        far = here.departures()[0]
        return remote(
            mine[matrix].at[layer, far],
            from_z[matrix].at[layer, 0],
            zs.at[layer, matrix, far],
            zr.at[layer, matrix, 0],
            here.z_peer(4 - far),
        )

    def z_out(matrix, layer, number, ends_only=False):
        step = here.departures()[number]
        if not here.relays:
            if step:
                z_grad(matrix, layer, step).start()
        elif number == 0:
            pl.when(here.middle)(z_grad(matrix, layer, step).start)
            pl.when(~here.middle)(z_left(matrix, layer).start)
        elif number == 1:
            z_grad(matrix, layer, step).start()
        elif number == 2:
            pl.when(~here.middle)(z_grad(matrix, layer, step).start)
            if not ends_only:
                relay(matrix, layer)

    def relay(matrix, layer):
        if here.relays:

            @pl.when(here.middle)
            def _():
                z_left(matrix, layer).wait_recv()
                add_from(from_z[matrix].at[layer, 0], mine[matrix].at[layer, 2])
                z_grad(matrix, layer, 2).start()

    def core(matrix, layer):
        for slot in range(2):
            if in_slot[slot] is not None and in_slot[slot][:2] == (matrix, layer):
                settle(slot)
        for what in tiles_of(matrix):

            @pl.loop(0, chips)
            def _(step):
                tile_copies(0, matrix, layer, *what, step)[0].wait_recv()

        lanes = pl.ds(0, mine[matrix].shape[3])
        pltpu.make_async_copy(
            from_core[matrix].at[layer], fetched.at[:, :, lanes], fetch_sem
        ).start()

    def send(matrix, layer):
        lanes = pl.ds(0, mine[matrix].shape[3])
        pltpu.make_async_copy(
            from_core[matrix].at[layer], fetched.at[:, :, lanes], fetch_sem
        ).wait()
        for number, step in enumerate(here.departures()):
            add_rows(mine[matrix].at[layer, step], [fetched.at[step, :, lanes]], small)
            if (layer, matrix) in Z_FIRST:
                z_out(matrix, layer, number, ends_only=True)
            else:
                pl.when(s != layer)(x_grad(matrix, layer, step).start)

    def add(matrix, layer, quarter):
        steps = here.departures()
        for number in range(quarter * chips // 4, (quarter + 1) * chips // 4):
            step = steps[number]
            x_grad(matrix, layer, step).wait_recv()
            add_from(from_x[matrix].at[step], mine[matrix].at[layer, step])
            z_out(matrix, layer, number)

    def sum_z(matrix, layer):
        def one(step):
            z_grad(matrix, layer, step).wait_recv()
            add_from(from_z[matrix].at[layer, step], mine[matrix].at[layer, 0])

        steps = here.departures()[:-1]
        if here.relays:
            one(steps[0])
            pl.when(here.middle)(lambda: one(steps[1]))
            one(2)
        else:
            for step in steps:
                one(step)
        pl.when(s != layer)(x_grad(matrix, layer, 0).start)

    def last(matrix, layer):
        x_grad(matrix, layer, 0).wait_recv()
        add_from(from_x[matrix].at[0], mine[matrix].at[layer, 0])

    actions = dict(core=core, send=send, add=add, relay=relay, sum=sum_z, last=last)
    for_both, for_section = points()

    def act(events):
        for name, layer, matrix, *more in events:
            actions[name](matrix, layer, *more)

    def point(layer, name):
        act(for_both.get((layer, name), []))
        for section in range(2):
            events = for_section[section].get((layer, name))
            if events:
                pl.when(s == section)(functools.partial(act, events))

    def total(value):
        return jnp.sum(value, 0, keepdims=True)

    def note(layer, row, value):
        gvec[layer, row : row + 1, :] = gvec[layer, row : row + 1, :] + total(value)

    def begin(layer, part, value):
        span = slice(*parts[part])
        grad_all[layer, 0, span] = value
        y_start(grad_all.at[layer, 0], grad_all.at[layer, 1], 4 * (1 - layer), part)
        note(layer, 5, value)

    def contract(layer, image, span):
        for piece in range(width_ff // depth):
            lanes = slice(piece * depth, (piece + 1) * depth)
            grad_hidden = dot(grad_all[layer, image, span], wb[:, lanes], 1, 0)
            value = pre[image, span, lanes]
            upper = phi_big(value)
            hidden[image, span, lanes] = value * upper
            pre[image, span, lanes] = grad_hidden * (upper + value * phi_small(value))

    everything = slice(0, rows)
    for part in range(2):
        span = slice(*parts[part])
        begin(1, part, cot[span] * live[span, 0:1])
    for layer in (1, 0):
        vectors = Vectors(vec.at[layer], width, None)
        base = 4 * (1 - layer)
        point(layer, "a")
        loaded("wd")
        loaded("pre")
        contract(layer, 0, everything)
        loaded("wu")
        own_part[...] = dot(pre[0], wu[...], 1, 1)
        if layer == 0:
            y_departed(1)
        for part in range(2):
            span = slice(*parts[part])
            point(layer, "b%d" % part)
            y_wait(base, part)
            contract(layer, 1, span)
            sending[0, span] = dot(pre[1, span], wu[...], 1, 1)
            y_start(sending.at[0], received.at[2 * (1 - layer)], base + 1, part)
        load("wo", layer)
        load("wq", layer)
        if layer == 1:
            load("wu", 0)
        point(layer, "c")
        product(D, layer, grad_all.at[layer], hidden)
        point(layer, "d")
        loaded("n2")
        product(U, layer, n2, pre)
        for piece in range(width_ff // depth):
            lanes = slice(piece * depth, (piece + 1) * depth)
            note(layer, 9 + piece, pre[0, :, lanes])
            note(layer, 9 + piece, pre[1, :, lanes])
        if layer == 1:
            load("pre", 0)
            load("n2", 0)
        loaded("mid")
        for part in range(2):
            span = slice(*parts[part])
            point(layer, "e%d" % part)
            unit, inverse = normalize(mid[span])
            y_wait(base + 1, part)
            grad_second = own_part[span] + received[2 * (1 - layer), span]
            grad_middle = grad_all[layer, 0, span] + normalize_back(
                grad_second * vectors.gain(1), unit, inverse
            )
            mid_all[layer, 0, span] = grad_middle
            y_start(mid_all.at[layer, 0], mid_all.at[layer, 1], base + 2, part)
            note(layer, 1, grad_second * unit)
            note(layer, 3, grad_second)
            note(layer, 4, grad_middle)
        if layer == 1:
            load("mid", 0)
        point(layer, "f")
        loaded("wo")
        loaded("joined")
        loaded("mixed")
        grad_mixed[...] = dot(mid_all[layer, 0], wo[...], 1, 0)
        attend_back(joined.at[0], mixed.at[0], grad_mixed, grad_joined.at[0], seq)
        loaded("wq")
        own_part[...] = dot(grad_joined[0], wq[...], 1, 1)
        for part in range(2):
            span = slice(*parts[part])
            point(layer, "g%d" % part)
            y_wait(base + 2, part)
            grad_mixed[span] = dot(mid_all[layer, 1, span], wo[...], 1, 0)
        attend_back(joined.at[1], mixed.at[1], grad_mixed, grad_joined.at[1], seq)
        if layer == 0:
            y_departed(3)
        for part in range(2):
            span = slice(*parts[part])
            sending[1, span] = dot(grad_joined[1, span], wq[...], 1, 1)
            y_start(sending.at[1], received.at[2 * (1 - layer) + 1], base + 3, part)
        if layer == 1:
            load("wd", 0)
            load("joined", 0)
        point(layer, "h")
        product(O, layer, mid_all.at[layer], mixed)
        loaded("n1")
        product(Q, layer, n1, grad_joined)
        if layer == 1:
            load("mixed", 0)
            load("n1", 0)
        for image in range(2):
            for piece in (0, 2):
                lanes = slice(piece * width, (piece + 1) * width)
                spot = slice(piece // 2 * width, (piece // 2 + 1) * width)
                gvec[layer, 8:9, spot] = gvec[layer, 8:9, spot] + total(
                    grad_joined[image, :, lanes]
                )
        point(layer, "i")
        loaded("hs")
        for part in range(2):
            span = slice(*parts[part])
            point(layer, "j%d" % part)
            unit, inverse = normalize(hs[span])
            y_wait(base + 3, part)
            grad_first = own_part[span] + received[2 * (1 - layer) + 1, span]
            value = mid_all[layer, 0, span] + normalize_back(
                grad_first * vectors.gain(0), unit, inverse
            )
            gin[layer, span] = value
            if layer == 1:
                begin(0, part, value * live[span, 0:1])
            note(layer, 0, grad_first * unit)
            note(layer, 2, grad_first)
        if layer == 1:
            load("hs", 0)
    point(0, "t0")
    copy = launch(remote(gvec, vy, v_send.at[0], v_recv.at[0], here.y_peer))
    point(0, "t1")
    departed(copy)
    copy.wait_recv()
    gvec[:, 0:8, :] = gvec[:, 0:8, :] + vy[:, 0:8, :]
    copy = launch(remote(gvec, vc, v_send.at[1], v_recv.at[1], here.core_peer))
    point(0, "t2")
    departed(copy)
    copy.wait_recv()
    gvec[...] = gvec[...] + vc[...]
    copies = []
    for step in range(1, chips):
        copies.append(
            launch(
                remote(
                    gvec,
                    vz.at[step - 1],
                    v_send.at[1 + step],
                    v_recv.at[1 + step],
                    here.z_peer(step),
                )
            )
        )
    x_arrivals.append(
        launch(remote(gin.at[1 - s], gin_x, g_send.at[1], g_recv.at[1], here.x_peer))
    )
    point(0, "t3")
    for copy in copies:
        departed(copy)
        copy.wait_recv()
    for step in range(1, chips):
        gvec[...] = gvec[...] + vz[step - 1]
    copy = launch(
        remote(
            gvec.at[1 - s], vx, v_send.at[chips + 1], v_recv.at[chips + 1], here.x_peer
        )
    )
    point(0, "t4")
    for section in range(2):

        @pl.when(s == section)
        def _():
            for matrix in range(4):
                outs[matrix][...] = mine[matrix][section, 0]

    copy.wait_recv()
    gvec[s] = gvec[s] + vx[...]
    for slot in range(2):
        settle(slot)
    for item in x_arrivals:
        item.wait_recv()
    for item in departing:
        item.wait_send()
    for item in exchanges.values():
        item.wait_send()

    def z_departures(matrix, layer):
        for step in here.departures()[:-1]:
            z_grad(matrix, layer, step).wait_send()

    for matrix in range(4):
        for layer in range(2):
            if (layer, matrix) in Z_FIRST:
                z_departures(matrix, layer)
                pl.when(s != layer)(x_grad(matrix, layer, 0).wait_send)
            else:
                pl.when(s == layer)(functools.partial(z_departures, matrix, layer))

                @pl.when(s != layer)
                def _():
                    for step in range(chips):
                        x_grad(matrix, layer, step).wait_send()


def backward(chips, seq, cot, live, vec, out_all, hs, mid, whole, kept):
    rows, depth = cot.shape
    sent_rows = up_to(seq, 8)
    width, width_ff = whole[1].shape[2], whole[2].shape[2]
    widths = [w.shape[2] for w in whole]
    block = depth // (2 * chips)
    any_space = pl.BlockSpec(memory_space=pl.ANY)
    vmem = pl.BlockSpec(memory_space=pltpu.VMEM)
    outs = [
        ((2, rows, depth), vmem),
        (vec.shape, vmem),
        *[((block, w), vmem) for w in widths],
        ((rows, depth), any_space),
        ((rows, depth), any_space),
        *[((2, chips, block, w), any_space) for w in widths],
        *[((chips, block, w), any_space) for w in widths],
        *[((2, chips, block, w), any_space) for w in widths],
    ]
    sems = pltpu.SemaphoreType.DMA
    scratch = [
        pltpu.VMEM((depth, width_ff), F32),
        pltpu.VMEM((depth, width_ff), F32),
        pltpu.VMEM((rows, depth), F32),
        pltpu.VMEM((rows, depth), F32),
        pltpu.VMEM((2, rows, depth), F32),
        pltpu.VMEM((2, rows, depth), F32),
        pltpu.VMEM((2, rows, 3 * width), F32),
        pltpu.VMEM((2, rows, width), F32),
        pltpu.VMEM((2, rows, width_ff), F32),
        pltpu.VMEM((2, rows, width_ff), F32),
        pltpu.VMEM((2, 2, rows, depth), F32),
        pltpu.VMEM((2, 2, rows, depth), F32),
        pltpu.VMEM((4, rows, depth), F32),
        pltpu.VMEM((2, rows, depth), F32),
        pltpu.VMEM((rows, depth), F32),
        pltpu.VMEM((rows, width), F32),
        pltpu.VMEM((2, rows, 3 * width), F32),
        *[pltpu.VMEM((2, chips, block, w), F32) for w in widths],
        pltpu.VMEM((2, depth, depth), F32),
        pltpu.VMEM((chips, block, width_ff), F32),
        pltpu.VMEM((block, width_ff), F32),
        pltpu.VMEM(vec.shape, F32),
        pltpu.VMEM(vec.shape, F32),
        pltpu.VMEM((chips - 1,) + vec.shape, F32),
        pltpu.VMEM(vec.shape[1:], F32),
        sems((8, 2)),
        sems((8, 2)),
        sems((11,)),
        sems((2, chips)),
        sems((2, chips)),
        sems((2, 4, 3, chips)),
        sems((4, chips)),
        sems((4, chips)),
        sems((2, 4, chips)),
        sems((2, 4, chips)),
        sems,
        sems,
        sems((chips + 2,)),
        sems((chips + 2,)),
        sems((2,)),
        sems((2,)),
    ]
    results = pl.pallas_call(
        functools.partial(backward_kernel, chips, seq, sent_rows),
        out_shape=[jax.ShapeDtypeStruct(shape, F32) for shape, _ in outs],
        in_specs=[vmem] * 3 + [any_space] * 12,
        out_specs=[spec for _, spec in outs],
        scratch_shapes=scratch,
        compiler_params=pltpu.CompilerParams(
            collective_id=1, has_side_effects=True, vmem_limit_bytes=VMEM_BYTES
        ),
        name="backward_both",
    )(cot, live, vec, out_all, hs, mid, *whole, *kept)
    return results[:8]


def body(
    embedded,
    image_counts,
    cotangent,
    qkv_weight,
    qv_bias,
    out_weight,
    up_weight,
    up_bias,
    down_weight,
    norm_gains,
    shift_terms,
):
    groups = lax.axis_size("dp")
    chips = groups // 2
    tensors = lax.axis_size("tensor")
    s = lax.axis_index("section")
    t = lax.axis_index("tensor")
    d = lax.axis_index("dp")
    seq, depth = embedded.shape[3:]
    rows = up_to(seq, 16)
    block = qkv_weight.shape[1]
    width = qkv_weight.shape[3]
    width_ff = up_weight.shape[2]

    def padded(value):
        chosen = lax.dynamic_index_in_dim(value[:, 0, 0], s, 0, keepdims=False)
        return jnp.pad(chosen, ((0, rows - seq), (0, 0)))

    slot = s * tensors + t
    alive = (slot < image_counts[0]).astype(F32)
    inside = lax.broadcasted_iota(jnp.int32, (rows, 128), 0) < seq
    live = jnp.where(inside, alive, 0.0)

    def spread(pieces, parts, part):
        count, piece = pieces.shape
        tiled = jnp.broadcast_to(pieces[:, None, :], (count, parts, piece))
        mine = lax.broadcasted_iota(jnp.int32, (count, parts, piece), 1) == part
        return jnp.where(mine, tiled, 0.0).reshape(count, parts * piece)

    wide = jnp.concatenate([norm_gains[0], shift_terms[0], jnp.zeros_like(norm_gains[0])])
    wide = spread(wide, tensors * groups, t * groups + d)
    biases = spread(qv_bias[0], groups, d).reshape(-1, depth)
    ups = spread(up_bias, groups, d).reshape(-1, depth)
    packed = jnp.concatenate([wide, biases, ups])
    packed = jnp.pad(packed, ((0, up_to(packed.shape[0], 8) - packed.shape[0]), (0, 0)))

    shards = (
        qkv_weight[0].reshape(block, 3 * width),
        out_weight[0].T,
        up_weight[0],
        down_weight[0].T,
    )
    out_all, vec, hs, mid, gq, go, gu, gd, *kept = forward(
        chips, seq, padded(embedded), live, packed, *shards
    )
    gin, gvec, sum_q, sum_o, sum_u, sum_d, gin_x, out_x = backward(
        chips,
        seq,
        padded(cotangent),
        live,
        vec,
        out_all,
        hs,
        mid,
        (gq, go, gu, gd),
        kept,
    )
    vec_sum = lax.dynamic_index_in_dim(gvec, s, 0, keepdims=False)

    def both(own, other):
        mine = lax.dynamic_index_in_dim(own, s, 0, keepdims=False)[:seq]
        other = other[:seq]
        first = jnp.where(s == 0, mine, other)
        second = jnp.where(s == 0, other, mine)
        return jnp.stack([first, second])[None, :, None, None]

    piece = depth // (tensors * groups)
    wide = lax.dynamic_slice_in_dim(vec_sum[0:6], (t * groups + d) * piece, piece, 1)
    biases = vec_sum[8].reshape(2, width)
    biases = lax.dynamic_slice_in_dim(biases, d * (width // groups), width // groups, 1)
    count = width_ff // depth
    ups = vec_sum[9 : 9 + count].reshape(width_ff)
    ups = lax.dynamic_slice_in_dim(ups, d * (width_ff // groups), width_ff // groups, 0)
    return (
        both(out_all, out_x),
        both(gin, gin_x),
        sum_q.reshape(1, block, 3, width),
        biases[None],
        sum_o.T[None],
        sum_u[None],
        ups[None],
        sum_d.T[None],
        wide[None, 0:2],
        wide[None, 2:6],
    )


def solution(mesh):
    placed = (
        P(None, "dp", "tensor", None, None),
        P("dp"),
        P(None, "dp", "tensor", None, None),
        P("section", "dp", None, "tensor"),
        P("section", None, ("tensor", "dp")),
        P("section", "tensor", "dp"),
        P("section", "dp", "tensor"),
        P("section", ("tensor", "dp")),
        P("section", "tensor", "dp"),
        P("section", None, ("tensor", "dp")),
        P("section", None, ("tensor", "dp")),
    )
    return jax.shard_map(
        body,
        mesh=mesh,
        in_specs=placed,
        out_specs=(
            P("section", None, "dp", "tensor", None, None),
            P("section", None, "dp", "tensor", None, None),
            P("section", "dp", None, "tensor"),
            P("section", None, ("tensor", "dp")),
            P("section", "tensor", "dp"),
            P("section", "dp", "tensor"),
            P("section", ("tensor", "dp")),
            P("section", "tensor", "dp"),
            P("section", None, ("tensor", "dp")),
            P("section", None, ("tensor", "dp")),
        ),
        check_vma=False,
    )
```

```python
import functools

import jax
import jax.numpy as jnp
from jax import lax
from jax.experimental import pallas as pl
from jax.experimental.pallas import tpu as pltpu
from jax.sharding import PartitionSpec as P

HD = 64
SCALE = HD ** (-0.5)
EPS = 1e-06
HIGH = lax.Precision.HIGH
MESH = pl.DeviceIdType.MESH
VMEM_BYTES = 63 * 2**20
F32 = jnp.float32


def dot(left, right, left_dim, right_dim):
    return lax.dot_general(
        left,
        right,
        (((left_dim,), (right_dim,)), ((), ())),
        precision=HIGH,
        preferred_element_type=F32,
    )


def up_to(count, step):
    return -(-count // step) * step


def normalize(value):
    centred = value - jnp.mean(value, -1, keepdims=True)
    inverse = lax.rsqrt(jnp.mean(centred * centred, -1, keepdims=True) + EPS)
    return centred * inverse, inverse


def normalize_back(grad_unit, unit, inverse):
    return inverse * (
        grad_unit
        - jnp.mean(grad_unit, -1, keepdims=True)
        - unit * jnp.mean(grad_unit * unit, -1, keepdims=True)
    )


class Place:
    def __init__(self, chips):
        self.s = lax.axis_index("section")
        self.t = lax.axis_index("tensor")
        d = lax.axis_index("dp")
        self.chips = chips
        self.z = d // 2
        self.c = d % 2
        self.x_peer = (1 - self.s, self.t, d)
        self.y_peer = (self.s, 1 - self.t, d)
        self.core_peer = (self.s, self.t, self.z * 2 + 1 - self.c)

    def z_at(self, step):
        return (self.z + self.chips + step) % self.chips

    def z_peer(self, step):
        return (self.s, self.t, self.z_at(step) * 2 + self.c)

    def greet(self):
        barrier = pltpu.get_barrier_semaphore()
        peers = [self.x_peer, self.y_peer, self.core_peer]
        peers += [self.z_peer(step) for step in range(1, self.chips)]
        for peer in peers:
            pl.semaphore_signal(barrier, inc=1, device_id=peer, device_id_type=MESH)
        pl.semaphore_wait(barrier, len(peers))


    @property
    def relays(self):
        return self.chips == 4

    def arrivals(self):
        if not self.relays:
            return list(range(1, self.chips))
        near = jnp.where(self.z < 2, 3, 1)
        return [2, near, 4 - near]

    def departures(self):
        if not self.relays:
            return list(range(1, self.chips)) + [0]
        far = jnp.where(self.z < 2, 3, 1)
        return [far, 4 - far, 2, 0]

    @property
    def middle(self):
        return (self.z == 1) | (self.z == 2)

    def direct(self, step):
        if not self.relays or step == 2:
            return None
        return self.z <= 2 if step == 1 else self.z >= 1


def when(condition, action):
    if condition is None:
        action()
    else:
        pl.when(condition)(action)


def parts_of(rows):
    first = up_to(rows // 2, 8)
    return [(0, first), (first, rows)]


def remote(src, dst, send, recv, peer):
    return pltpu.make_async_remote_copy(
        src_ref=src,
        dst_ref=dst,
        send_sem=send,
        recv_sem=recv,
        device_id=peer,
        device_id_type=MESH,
    )


def key_mask(rows, seq):
    return lax.broadcasted_iota(jnp.int32, (rows, rows), 1) < seq


def head_lanes(which):
    return lax.broadcasted_iota(jnp.int32, (1, 2 * HD), 1) // HD == which


def attend(joined, mixed, seq):
    rows, width = mixed.shape
    keep = key_mask(rows, seq)
    for pair in range(width // (2 * HD)):
        lanes = slice(pair * 2 * HD, (pair + 1) * 2 * HD)
        query = joined[:, lanes] * SCALE
        keys = joined[:, width + lanes.start : width + lanes.stop]
        values = joined[:, 2 * width + lanes.start : 2 * width + lanes.stop]
        total = None
        for which in range(2):
            own = head_lanes(which)
            scores = dot(query, jnp.where(own, keys, 0.0), 1, 1)
            scores = jnp.where(keep, scores, -3e38)
            weights = jnp.exp(scores - jnp.max(scores, -1, keepdims=True))
            probs = weights / jnp.sum(weights, -1, keepdims=True)
            part = dot(probs, jnp.where(own, values, 0.0), 1, 0)
            total = part if total is None else total + part
        mixed[:, lanes] = total


def attend_back(joined, mixed, grad_mixed, grad_joined, seq):
    rows, width = mixed.shape
    keep = key_mask(rows, seq)
    for pair in range(width // (2 * HD)):
        lanes = slice(pair * 2 * HD, (pair + 1) * 2 * HD)
        query = joined[:, lanes] * SCALE
        keys = joined[:, width + lanes.start : width + lanes.stop]
        values = joined[:, 2 * width + lanes.start : 2 * width + lanes.stop]
        grad = grad_mixed[:, lanes]
        product = grad * mixed[:, lanes]
        grads = [None, None, None]
        for which in range(2):
            own = head_lanes(which)
            own_keys = jnp.where(own, keys, 0.0)
            scores = dot(query, own_keys, 1, 1)
            scores = jnp.where(keep, scores, -3e38)
            weights = jnp.exp(scores - jnp.max(scores, -1, keepdims=True))
            probs = weights / jnp.sum(weights, -1, keepdims=True)
            own_grad = jnp.where(own, grad, 0.0)
            row_dot = jnp.sum(jnp.where(own, product, 0.0), -1, keepdims=True)
            grad_probs = dot(grad, jnp.where(own, values, 0.0), 1, 1)
            grad_scores = probs * (grad_probs - row_dot)
            parts = (
                dot(grad_scores, own_keys, 1, 0) * SCALE,
                dot(grad_scores, jnp.where(own, query, 0.0), 0, 0),
                dot(probs, own_grad, 0, 0),
            )
            grads = [b if a is None else a + b for a, b in zip(grads, parts)]
        for number, part in enumerate(grads):
            start = number * width + lanes.start
            grad_joined[:, start : start + 2 * HD] = part


def phi_big(value):
    return 0.5 * (1.0 + lax.erf(value * 0.7071067811865476))


def phi_small(value):
    return jnp.exp(-0.5 * value * value) * 0.3989422804014327


class Vectors:
    def __init__(self, ref, width, hidden):
        self.ref, self.width, self.hidden = ref, width, hidden

    def gain(self, which):
        return self.ref[which : which + 1, :]

    def shift(self, which):
        return self.ref[2 + which : 3 + which, :]

    def query(self):
        return self.ref[8:9, 0 : self.width]

    def value(self):
        return self.ref[8:9, self.width : 2 * self.width]

    def up(self, row):
        return self.ref[9 + row : 10 + row, :]


def add_rows(target, sources, step):
    rows = target.shape[0]

    @pl.loop(0, rows // step)
    def _(index):
        here = pl.ds(pl.multiple_of(index * step, 8), step)
        total = target[here, :]
        for source in sources:
            total = total + source[here, :]
        target[here, :] = total


Q, O, U, D = range(4)

VIA_OWN, BOTH, VIA_OTHER = range(3)
GATHER = (
    (VIA_OWN, VIA_OWN, VIA_OTHER, VIA_OWN),
    (VIA_OWN, VIA_OWN, VIA_OTHER, VIA_OWN),
)

PASS_ON = (
    {
        (0, "start"): (
            ("own", 0, U), ("spread", 0, O), ("own", 0, Q), ("z", 0, O, 1),
            ("spread", 0, Q), ("z", 0, O, 0), ("own", 0, O), ("z", 0, Q, 0),
            ("z", 0, Q, 1), ("z", 0, Q, 2), ("spread", 0, D), ("own", 0, D),
            ("z", 0, O, 2), ("x", 1, O, 0),
        ),
        (0, "a"): (
            ("z", 0, D, 1),
        ),
        (0, "b"): (
            ("x", 1, U, -1),
        ),
        (0, "c0"): (
            ("x", 1, Q, 0), ("x", 1, D, -1),
        ),
        (0, "c1"): (
            ("z", 0, D, 0),
        ),
        (0, "d0"): (
            ("x", 0, U, 0),
        ),
        (0, "d1"): (
            ("z", 0, D, 2), ("x", 1, Q, 1), ("x", 0, U, 1),
        ),
        (0, "e"): (
            ("x", 0, U, 2),
        ),
        (0, "f1"): (
            ("z", 1, U, 0),
        ),
        (0, "h0"): (
            ("x", 1, Q, -1), ("x", 1, O, -1), ("z", 1, U, 1), ("x", 1, Q, 2),
        ),
        (0, "h1"): (
            ("x", 1, O, 1), ("x", 1, D, 0),
        ),
        (1, "b"): (
            ("x", 1, O, 2), ("z", 1, U, 2),
        ),
        (1, "e"): (
            ("x", 1, D, 2),
        ),
        (1, "g"): (
            ("x", 1, D, 1),
        ),
    },
    {
        (0, "start"): (
            ("spread", 1, O), ("own", 1, U), ("own", 1, D), ("spread", 1, Q),
            ("own", 1, Q), ("z", 1, O, 0), ("z", 1, O, 1), ("x", 0, U, -1), ("z", 1, Q, 0),
        ),
        (0, "a"): (
            ("own", 1, O), ("x", 0, O, -1), ("x", 0, Q, -1), ("x", 0, O, 0),
            ("z", 1, Q, 1), ("x", 0, O, 1), ("x", 0, Q, 2), ("z", 0, U, 1), ("x", 0, Q, 1),
            ("spread", 1, D), ("x", 0, Q, 0),
        ),
        (0, "b"): (
            ("x", 0, D, -1), ("z", 0, U, 0), ("x", 0, O, 2),
        ),
        (0, "d0"): (
            ("z", 0, U, 2),
        ),
        (0, "f0"): (
            ("x", 0, D, 1), ("z", 1, Q, 2), ("x", 0, D, 0),
        ),
        (0, "f1"): (
            ("z", 1, D, 0), ("x", 0, D, 2),
        ),
        (0, "h0"): (
            ("z", 1, O, 2), ("z", 1, D, 1), ("x", 1, U, 0),
        ),
        (1, "c0"): (
            ("z", 1, D, 2), ("x", 1, U, 1),
        ),
        (1, "d0"): (
            ("x", 1, U, 2),
        ),
    },
)


def forward_kernel(
    chips,
    seq,
    sent_rows,
    x_in,
    live,
    vec_in,
    wq,
    wo,
    wu,
    wd,
    out_all,
    vec,
    hs,
    mid,
    gq_out,
    go_out,
    gu_out,
    gd_out,
    n1_out,
    n2_out,
    joined_out,
    mixed_out,
    pre_out,
    gq,
    go,
    gu,
    gd,
    n1,
    n2,
    joined,
    mixed,
    pre,
    hidden,
    received,
    sending,
    vy,
    vc,
    vz,
    y_send,
    y_recv,
    v_send,
    v_recv,
    zs,
    zr,
    xs,
    xr,
    cs,
    cr,
    local,
    save,
):
    here = Place(chips)
    s, c, z = here.s, here.c, here.z
    shards = (wq, wo, wu, wd)
    whole = (gq, go, gu, gd)
    block = wq.shape[0]
    rows, depth = x_in.shape
    width = go.shape[2]
    tail = rows - sent_rows
    parts = parts_of(rows)
    for buffer in (n1, n2):
        for layer in range(2):
            buffer[layer, 1, sent_rows:rows, :] = jnp.zeros((tail, depth), F32)
    for index in range(received.shape[0]):
        received[index, sent_rows:rows, :] = jnp.zeros((tail, depth), F32)
    vec[s] = vec_in[...]
    here.greet()


    def spot(matrix, layer, back, core=None):
        start = (here.z_at(-back) * 2 + (c if core is None else core)) * block
        return whole[matrix].at[layer, pl.ds(pl.multiple_of(start, 8), block), :]

    def z_copy(layer, matrix, step, src=None):
        place = spot(matrix, layer, 0)
        return remote(
            place if src is None else src,
            place,
            zs.at[layer, matrix, step],
            zr.at[layer, matrix, step],
            here.z_peer(step),
        )

    def z_relay(layer, matrix):
        place = spot(matrix, layer, 2)
        step = jnp.where(z == 1, 3, 1)
        return remote(
            place,
            place,
            zs.at[layer, matrix, 0],
            zr.at[layer, matrix, 4 - step],
            here.z_peer(step),
        )

    def x_copy(layer, matrix, back, src=None):
        place = spot(matrix, layer, back)
        return remote(
            place if src is None else src,
            place,
            xs.at[layer, matrix, back],
            xr.at[layer, matrix, back],
            here.x_peer,
        )

    def c_copy(layer, matrix, back, src=None):
        place = spot(matrix, layer, back)
        return remote(
            place if src is None else src,
            place,
            cs.at[layer, matrix, back],
            cr.at[layer, matrix, back],
            here.core_peer,
        )

    def landed(place, sem):
        pltpu.make_async_copy(place, place, sem).wait()

    def z_spread(layer, matrix, src=None):
        for step in [2, 1, 3] if here.relays else range(1, chips):
            when(here.direct(step), z_copy(layer, matrix, step, src).start)

    count = chips - 1

    def act(section, event):
        kind, layer, matrix, *third = event
        own = section == layer
        path = GATHER[layer][matrix]
        if kind == "own":
            x_copy(layer, matrix, 0, shards[matrix]).start()
        elif kind == "spread":
            z_spread(layer, matrix, shards[matrix])
        elif third[0] < 0:
            landed(spot(matrix, layer, 0), xr.at[layer, matrix, 0])
            if path != VIA_OWN:
                z_spread(layer, matrix)
            c_copy(layer, matrix, 0).start()
        else:
            for number in range(count * third[0] // 3, count * (third[0] + 1) // 3):
                back = here.arrivals()[number]
                place = spot(matrix, layer, back)
                if kind == "x":
                    landed(place, xr.at[layer, matrix, back])
                else:
                    landed(place, zr.at[layer, matrix, back])
                    if here.relays and number == 0:
                        pl.when(here.middle)(z_relay(layer, matrix).start)
                    if path == (VIA_OWN if own else VIA_OTHER):
                        x_copy(layer, matrix, back).start()
                c_copy(layer, matrix, back).start()

    def point(layer, name):
        for section in range(2):
            events = PASS_ON[section].get((layer, name))
            if events:

                @pl.when(s == section)
                def _():
                    for event in events:
                        act(section, event)

    copy = remote(vec.at[s], vec.at[s], v_send.at[0], v_recv.at[0], here.x_peer)
    copy.start()
    copy.wait_send()
    landed(vec.at[1 - s], v_recv.at[0])
    vector_copies = []
    for step in range(1, chips):
        copy = remote(
            vec, vz.at[step - 1], v_send.at[step], v_recv.at[step], here.z_peer(step)
        )
        copy.start()
        vector_copies.append(copy)
    own_copies = []
    for matrix in range(4):
        c_copy(s, matrix, 0, shards[matrix]).start()
        copy = pltpu.make_async_copy(
            shards[matrix], spot(matrix, s, 0), local.at[matrix]
        )
        copy.start()
        own_copies.append(copy)
    point(0, "start")
    for copy in vector_copies:
        copy.wait()
    for step in range(1, chips):
        vec[...] = vec[...] + vz[step - 1]
    copy = remote(vec, vc, v_send.at[chips], v_recv.at[chips], here.core_peer)
    copy.start()
    copy.wait()
    vec[...] = vec[...] + vc[...]
    copy = remote(vec, vy, v_send.at[chips + 1], v_recv.at[chips + 1], here.y_peer)
    copy.start()
    copy.wait()
    vec[:, 0:8, :] = vec[:, 0:8, :] + vy[:, 0:8, :]

    saves = {}

    def keep(name, src, dst, sem):
        copy = pltpu.make_async_copy(src, dst, save.at[sem])
        copy.start()
        saves[name] = copy

    def before_write(name):
        if name in saves:
            saves.pop(name).wait()

    def finish(layer, matrix):
        pl.when(s == layer)(own_copies[matrix].wait)
        for back in range(chips):
            landed(spot(matrix, layer, back, 1 - c), cr.at[layer, matrix, back])
        keep(
            "whole%d%d" % (layer, matrix),
            whole[matrix].at[layer],
            (gq_out, go_out, gu_out, gd_out)[matrix].at[layer],
            14 + 4 * layer + matrix,
        )

    exchanges = {}

    def y_start(src, dst, index, part):
        start, stop = parts[part]
        span = pl.ds(start, min(stop, sent_rows) - start)
        copy = remote(
            src.at[span],
            dst.at[span],
            y_send.at[index, part],
            y_recv.at[index, part],
            here.y_peer,
        )
        copy.start()
        exchanges[index, part] = copy

    def y_wait(index, part):
        exchanges[index, part].wait_recv()

    def y_departed(index):
        for part in range(2):
            exchanges.pop((index, part)).wait_send()

    def begin(layer, part, value):
        span = slice(*parts[part])
        hs[layer, span] = value
        unit, _ = normalize(value)
        vectors = Vectors(vec.at[layer], width, None)
        n1[layer, 0, span] = unit * vectors.gain(0) + vectors.shift(0)
        y_start(n1.at[layer, 0], n1.at[layer, 1], 4 * layer, part)

    def project(layer, image, span):
        vectors = Vectors(vec.at[layer], width, None)
        for piece in range(3):
            lanes = slice(piece * width, (piece + 1) * width)
            value = dot(n1[layer, image, span], gq[layer, :, lanes], 1, 0)
            if piece == 0:
                value = value + vectors.query()
            if piece == 2:
                value = value + vectors.value()
            joined[image, span, lanes] = value

    def expand(layer, image, span):
        vectors = Vectors(vec.at[layer], width, None)
        for piece in range(pre.shape[2] // depth):
            lanes = slice(piece * depth, (piece + 1) * depth)
            value = dot(n2[layer, image, span], gu[layer, :, lanes], 1, 0)
            value = value + vectors.up(piece)
            pre[image, span, lanes] = value
            hidden[image, span, lanes] = value * phi_big(value)

    everything = slice(0, rows)
    for part in range(2):
        begin(0, part, x_in[slice(*parts[part])])
    for layer in range(2):
        vectors = Vectors(vec.at[layer], width, None)
        point(layer, "a")
        before_write("joined")
        before_write("mixed")
        finish(layer, Q)
        project(layer, 0, everything)
        attend(joined.at[0], mixed.at[0], seq)
        point(layer, "b")
        finish(layer, O)
        mid[layer] = hs[layer] + dot(mixed[0], go[layer], 1, 1) + vectors.shift(2)
        for part in range(2):
            point(layer, "c%d" % part)
            y_wait(4 * layer, part)
            project(layer, 1, slice(*parts[part]))
        attend(joined.at[1], mixed.at[1], seq)
        if layer == 1:
            y_departed(1)
        for part in range(2):
            span = slice(*parts[part])
            sending[0, span] = dot(mixed[1, span], go[layer], 1, 1)
            y_start(sending.at[0], received.at[2 * layer], 4 * layer + 1, part)
        keep("n1%d" % layer, n1.at[layer], n1_out.at[layer], 4 + layer)
        keep("joined", joined, joined_out.at[layer], 6 + layer)
        keep("mixed", mixed, mixed_out.at[layer], 8 + layer)
        for part in range(2):
            span = slice(*parts[part])
            point(layer, "d%d" % part)
            y_wait(4 * layer + 1, part)
            middle = mid[layer, span] + received[2 * layer, span]
            mid[layer, span] = middle
            unit, _ = normalize(middle)
            n2[layer, 0, span] = unit * vectors.gain(1) + vectors.shift(1)
            y_start(n2.at[layer, 0], n2.at[layer, 1], 4 * layer + 2, part)
        point(layer, "e")
        before_write("pre")
        finish(layer, U)
        expand(layer, 0, everything)
        if layer == 0:
            for part in range(2):
                point(0, "f%d" % part)
                y_wait(2, part)
                expand(0, 1, slice(*parts[part]))
        else:
            y_departed(3)
        point(layer, "g")
        finish(layer, D)
        if layer == 1:
            out_all[layer] = mid[layer] + dot(hidden[0], gd[layer], 1, 1)
        for part in range(2):
            span = slice(*parts[part])
            if layer == 1:
                point(1, "f%d" % part)
                y_wait(6, part)
                expand(1, 1, span)
            sending[1, span] = dot(hidden[1, span], gd[layer], 1, 1)
            y_start(sending.at[1], received.at[2 * layer + 1], 4 * layer + 3, part)
        if layer == 0:
            out_all[layer] = mid[layer] + dot(hidden[0], gd[layer], 1, 1)
        keep("n2%d" % layer, n2.at[layer], n2_out.at[layer], 10 + layer)
        keep("pre", pre, pre_out.at[layer], 12 + layer)
        for part in range(2):
            span = slice(*parts[part])
            point(layer, "h%d" % part)
            y_wait(4 * layer + 3, part)
            result = out_all[layer, span] + received[2 * layer + 1, span]
            result = (result + vectors.shift(3)) * live[span, 0:1]
            out_all[layer, span] = result
            if layer == 0:
                begin(1, part, result)

    for copy in saves.values():
        copy.wait()
    for copy in exchanges.values():
        copy.wait_send()
    def z_departures(layer, matrix):
        for step in range(1, chips):
            when(here.direct(step), z_copy(layer, matrix, step).wait_send)
        if here.relays:
            pl.when(here.middle)(z_relay(layer, matrix).wait_send)

    def departures(section):
        for layer in range(2):
            for matrix in range(4):
                path = GATHER[layer][matrix]
                own = section == layer
                if own:
                    x_copy(layer, matrix, 0).wait_send()
                if path == (VIA_OWN if own else VIA_OTHER):
                    for back in range(1, chips):
                        x_copy(layer, matrix, back).wait_send()
                if path != (VIA_OTHER if own else VIA_OWN):
                    z_departures(layer, matrix)

    for section in range(2):
        pl.when(s == section)(functools.partial(departures, section))
    for layer in range(2):
        for matrix in range(4):
            for back in range(chips):
                c_copy(layer, matrix, back).wait_send()


def forward(chips, seq, x_in, live, vec_in, wq, wo, wu, wd):
    rows, depth = x_in.shape
    sent_rows = up_to(seq, 8)
    width = wo.shape[1]
    hidden = wu.shape[1]
    widths = (wq.shape[1], width, hidden, hidden)
    whole = [(2, depth, w) for w in widths]
    any_space = pl.BlockSpec(memory_space=pl.ANY)
    vmem = pl.BlockSpec(memory_space=pltpu.VMEM)
    both = (2,) + vec_in.shape
    outs = [
        ((2, rows, depth), vmem),
        (both, vmem),
        ((2, rows, depth), vmem),
        ((2, rows, depth), vmem),
        *[(w, any_space) for w in whole],
        ((2, 2, rows, depth), any_space),
        ((2, 2, rows, depth), any_space),
        ((2, 2, rows, 3 * width), any_space),
        ((2, 2, rows, width), any_space),
        ((2, 2, rows, hidden), any_space),
    ]
    sems = pltpu.SemaphoreType.DMA
    scratch = [
        *[pltpu.VMEM(w, F32) for w in whole],
        pltpu.VMEM((2, 2, rows, depth), F32),
        pltpu.VMEM((2, 2, rows, depth), F32),
        pltpu.VMEM((2, rows, 3 * width), F32),
        pltpu.VMEM((2, rows, width), F32),
        pltpu.VMEM((2, rows, hidden), F32),
        pltpu.VMEM((2, rows, hidden), F32),
        pltpu.VMEM((4, rows, depth), F32),
        pltpu.VMEM((2, rows, depth), F32),
        pltpu.VMEM(both, F32),
        pltpu.VMEM(both, F32),
        pltpu.VMEM((chips - 1,) + both, F32),
        sems((8, 2)),
        sems((8, 2)),
        sems((chips + 2,)),
        sems((chips + 2,)),
        *[sems((2, 4, chips)) for _ in range(6)],
        sems((4,)),
        sems((22,)),
    ]
    return pl.pallas_call(
        functools.partial(forward_kernel, chips, seq, sent_rows),
        out_shape=[jax.ShapeDtypeStruct(shape, F32) for shape, _ in outs],
        in_specs=[vmem] * 3 + [any_space] * 4,
        out_specs=[spec for _, spec in outs],
        scratch_shapes=scratch,
        compiler_params=pltpu.CompilerParams(
            collective_id=0, has_side_effects=True, vmem_limit_bytes=VMEM_BYTES
        ),
        name="forward_both",
    )(x_in, live, vec_in, wq, wo, wu, wd)


SUMS = (
    (VIA_OTHER, VIA_OTHER, VIA_OWN, BOTH),
    (VIA_OTHER, VIA_OWN, VIA_OWN, VIA_OTHER),
)

SUM_UP = (
    {
        (1, "e0"): (
            ("core", 1, D),
        ),
        (1, "e1"): (
            ("send", 1, D), ("core", 1, U),
        ),
        (1, "f"): (
            ("send", 1, U),
        ),
        (1, "h"): (
            ("add", 1, D, 0),
        ),
        (1, "i"): (
            ("add", 1, D, 1),
        ),
        (0, "b0"): (
            ("add", 1, D, 2), ("relay", 1, D), ("core", 1, O), ("send", 1, O),
        ),
        (0, "b1"): (
            ("core", 1, Q),
        ),
        (0, "d"): (
            ("send", 1, Q),
        ),
        (0, "e0"): (
            ("core", 0, D), ("send", 0, D),
        ),
        (0, "f"): (
            ("sum", 1, D), ("add", 1, Q, 0), ("add", 1, Q, 1), ("core", 0, U),
            ("relay", 0, D),
        ),
        (0, "g0"): (
            ("send", 0, U), ("add", 1, Q, 2),
        ),
        (0, "i"): (
            ("core", 0, O), ("send", 0, O),
        ),
        (0, "j0"): (
            ("relay", 1, Q), ("core", 0, Q),
        ),
        (0, "t0"): (
            ("send", 0, Q), ("add", 0, U, 0), ("sum", 0, D), ("add", 0, U, 2),
            ("add", 0, U, 3), ("add", 0, U, 1), ("sum", 1, Q), ("relay", 0, U),
        ),
        (0, "t3"): (
            ("last", 0, D), ("sum", 0, U), ("last", 0, O), ("last", 0, Q),
        ),
    },
    {
        (1, "e0"): (
            ("core", 1, D), ("send", 1, D), ("core", 1, U),
        ),
        (1, "h"): (
            ("send", 1, U),
        ),
        (1, "i"): (
            ("core", 1, O), ("add", 1, U, 0), ("add", 1, U, 1),
        ),
        (0, "a"): (
            ("send", 1, O), ("core", 1, Q), ("send", 1, Q),
        ),
        (0, "b1"): (
            ("add", 1, U, 2),
        ),
        (0, "d"): (
            ("relay", 1, U),
        ),
        (0, "e1"): (
            ("core", 0, D),
        ),
        (0, "f"): (
            ("send", 0, D), ("core", 0, U), ("send", 0, U),
        ),
        (0, "g1"): (
            ("relay", 0, D),
        ),
        (0, "i"): (
            ("core", 0, O), ("send", 0, O), ("add", 0, O, 2), ("add", 1, U, 3),
            ("add", 0, O, 0), ("add", 0, O, 1), ("core", 0, Q),
        ),
        (0, "j0"): (
            ("add", 1, O, 3),
        ),
        (0, "j1"): (
            ("send", 0, Q), ("add", 1, O, 1), ("last", 1, D), ("relay", 0, O),
            ("add", 0, Q, 0), ("add", 1, O, 2), ("sum", 0, D), ("add", 0, Q, 1),
        ),
        (0, "t1"): (
            ("sum", 0, O),
        ),
        (0, "t2"): (
            ("add", 0, Q, 2), ("add", 1, O, 0), ("relay", 0, Q),
        ),
        (0, "t3"): (
            ("last", 1, Q), ("relay", 1, O), ("sum", 1, U), ("sum", 0, Q), ("sum", 1, O),
        ),
    },
)


def backward_kernel(
    chips,
    seq,
    sent_rows,
    cot,
    live,
    vec,
    out_all,
    hs_in,
    mid_in,
    gq_in,
    go_in,
    gu_in,
    gd_in,
    n1_in,
    n2_in,
    joined_in,
    mixed_in,
    pre_in,
    gin,
    gvec,
    outq,
    outo,
    outu,
    outd,
    gin_x,
    out_x,
    rcq,
    rco,
    rcu,
    rcd,
    rxq,
    rxo,
    rxu,
    rxd,
    rzq,
    rzo,
    rzu,
    rzd,
    wb,
    wu,
    hs,
    mid,
    n1,
    n2,
    joined,
    mixed,
    pre,
    hidden,
    grad_all,
    mid_all,
    received,
    sending,
    own_part,
    grad_mixed,
    grad_joined,
    aq,
    ao,
    au,
    ad,
    tile,
    fetched,
    single,
    vc,
    vy,
    vz,
    vx,
    y_send,
    y_recv,
    loads,
    cs,
    cl,
    cr,
    xs,
    xr,
    zs,
    zr,
    fetch_sem,
    single_sem,
    v_send,
    v_recv,
    g_send,
    g_recv,
):
    here = Place(chips)
    s, c, z = here.s, here.c, here.z
    rows, depth = cot.shape
    width = mixed.shape[2]
    width_ff = wu.shape[1]
    tail = rows - sent_rows
    parts = parts_of(rows)
    mine = (aq, ao, au, ad)
    from_core = (rcq, rco, rcu, rcd)
    from_x = (rxq, rxo, rxu, rxd)
    from_z = (rzq, rzo, rzu, rzd)
    outs = (outq, outo, outu, outd)
    block = outq.shape[0]
    small = 24 if block % 24 == 0 else block
    for buffer in (grad_all, mid_all):
        for layer in range(2):
            buffer[layer, 1, sent_rows:rows, :] = jnp.zeros((tail, depth), F32)
    for index in range(received.shape[0]):
        received[index, sent_rows:rows, :] = jnp.zeros((tail, depth), F32)
    gvec[...] = jnp.zeros(gvec.shape, F32)

    wq, wo = wb.at[:, 0 : 3 * width], wb.at[:, 3 * width : 4 * width]
    sources = dict(
        wd=(gd_in, wb),
        pre=(pre_in, pre),
        wu=(gu_in, wu),
        n2=(n2_in, n2),
        mid=(mid_in, mid),
        joined=(joined_in, joined),
        mixed=(mixed_in, mixed),
        n1=(n1_in, n1),
        hs=(hs_in, hs),
        wo=(go_in, wo),
        wq=(gq_in, wq),
    )
    order = list(sources)
    loading = {}

    def load(name, layer):
        src, dst = sources[name]
        copy = pltpu.make_async_copy(src.at[layer], dst, loads.at[order.index(name)])
        copy.start()
        loading[name] = copy

    def loaded(name):
        loading.pop(name).wait()

    for name in order[:-2]:
        load(name, 1)
    here.greet()
    departing = []

    def launch(copy):
        copy.start()
        departing.append(copy)
        return copy

    def departed(copy):
        copy.wait_send()
        departing[:] = [item for item in departing if item is not copy]

    exchanges = {}

    def y_start(src, dst, index, part):
        start, stop = parts[part]
        span = pl.ds(start, min(stop, sent_rows) - start)
        copy = remote(
            src.at[span],
            dst.at[span],
            y_send.at[index, part],
            y_recv.at[index, part],
            here.y_peer,
        )
        copy.start()
        exchanges[index, part] = copy

    def y_wait(index, part):
        exchanges[index, part].wait_recv()

    def y_departed(index):
        for part in range(2):
            exchanges.pop((index, part)).wait_send()

    def gin_copy():
        return remote(gin.at[1 - s], gin_x, g_send.at[1], g_recv.at[1], here.x_peer)

    out_copy = launch(
        remote(out_all.at[1 - s], out_x, g_send.at[0], g_recv.at[0], here.x_peer)
    )


    def tile_copies(slot, matrix, layer, number, start, size, step):
        lanes = pl.ds(start, size)
        spots = []
        for core in (1 - c, c):
            first = pl.multiple_of((here.z_at(step) * 2 + core) * block, 8)
            spots.append(tile.at[slot, pl.ds(first, block), pl.ds(0, size)])
        return (
            remote(
                spots[0],
                from_core[matrix].at[layer, step, :, lanes],
                cs.at[slot, step],
                cr.at[layer, matrix, number, step],
                here.core_peer,
            ),
            pltpu.make_async_copy(
                spots[1], mine[matrix].at[layer, step, :, lanes], cl.at[slot, step]
            ),
        )

    in_slot = [[None, None], [None, None]]
    next_slot = [0]

    def settle(section, slot):
        what = in_slot[section][slot]
        if what is not None:
            in_slot[section][slot] = None

            @pl.loop(0, chips)
            def _(step):
                away, kept = tile_copies(slot, *what, step)
                away.wait_send()
                kept.wait()

    def settle_all(slot):
        if in_slot[0][slot] == in_slot[1][slot]:
            settle(0, slot)
            in_slot[1][slot] = None
        for section in range(2):
            if in_slot[section][slot] is not None:
                pl.when(s == section)(functools.partial(settle, section, slot))

    def tiles_of(matrix):
        size = width if matrix < 2 else depth
        return [(n, n * size, size) for n in range(mine[matrix].shape[3] // size)]

    def flat(ref):
        return ref[...].reshape(2 * rows, ref.shape[-1])

    def product(matrix, layer, left, right):
        both = flat(left)
        for number, start, size in tiles_of(matrix):
            slot = next_slot[0]
            next_slot[0] = 1 - slot
            settle_all(slot)
            piece = right[:, :, start : start + size].reshape(2 * rows, size)
            tile[slot, :, 0:size] = dot(both, piece, 0, 0)
            what = (matrix, layer, number, start, size)

            @pl.loop(0, chips)
            def _(step):
                away, kept = tile_copies(slot, *what, step)
                away.start()
                kept.start()

            in_slot[0][slot] = in_slot[1][slot] = what

    def add_from(src, target):
        lanes = target.shape[1]
        spot = single.at[:, pl.ds(0, lanes)]
        copy = pltpu.make_async_copy(src, spot, single_sem)
        copy.start()
        copy.wait()
        add_rows(target, [spot], small)

    def x_grad(matrix, layer, step):
        return remote(
            mine[matrix].at[layer, step],
            from_x[matrix].at[layer, step],
            xs.at[layer, matrix, step],
            xr.at[layer, matrix, step],
            here.x_peer,
        )

    def z_grad(matrix, layer, step):
        return remote(
            mine[matrix].at[layer, step],
            from_z[matrix].at[layer, step],
            zs.at[layer, matrix, step],
            zr.at[layer, matrix, step],
            here.z_peer(step),
        )

    def z_left(matrix, layer):
        far = here.departures()[0]
        return remote(
            mine[matrix].at[layer, far],
            from_z[matrix].at[layer, 0],
            zs.at[layer, matrix, far],
            zr.at[layer, matrix, 0],
            here.z_peer(4 - far),
        )

    def z_out(matrix, layer, number):
        step = here.departures()[number]
        if not here.relays:
            if step:
                z_grad(matrix, layer, step).start()
        elif number == 0:
            pl.when(here.middle)(z_grad(matrix, layer, step).start)
            pl.when(~here.middle)(z_left(matrix, layer).start)
        elif number == 1:
            z_grad(matrix, layer, step).start()
        elif number == 2:
            pl.when(~here.middle)(z_grad(matrix, layer, step).start)

    def core(section, layer, matrix):
        for slot in range(2):
            what = in_slot[section][slot]
            if what is not None and what[:2] == (matrix, layer):
                settle(section, slot)
        for what in tiles_of(matrix):

            @pl.loop(0, chips)
            def _(step):
                tile_copies(0, matrix, layer, *what, step)[0].wait_recv()

        lanes = pl.ds(0, mine[matrix].shape[3])
        pltpu.make_async_copy(
            from_core[matrix].at[layer], fetched.at[:, :, lanes], fetch_sem
        ).start()

    def send(section, layer, matrix):
        lanes = pl.ds(0, mine[matrix].shape[3])
        pltpu.make_async_copy(
            from_core[matrix].at[layer], fetched.at[:, :, lanes], fetch_sem
        ).wait()
        path = SUMS[layer][matrix]
        for number, step in enumerate(here.departures()):
            add_rows(mine[matrix].at[layer, step], [fetched.at[step, :, lanes]], small)
            if path == BOTH:
                z_out(matrix, layer, number)
            elif path == VIA_OWN and section != layer:
                x_grad(matrix, layer, step).start()
            elif path == VIA_OTHER and section == layer and number < chips - 1:
                x_grad(matrix, layer, step).start()

    def add(section, layer, matrix, group):
        steps = here.departures()
        count, groups = (chips, 4) if section == layer else (chips - 1, 3)
        for number in range(count * group // groups, count * (group + 1) // groups):
            step = steps[number]
            x_grad(matrix, layer, step).wait_recv()
            add_from(from_x[matrix].at[layer, step], mine[matrix].at[layer, step])
            z_out(matrix, layer, number)

    def relay(section, layer, matrix):
        if here.relays:

            @pl.when(here.middle)
            def _():
                z_left(matrix, layer).wait_recv()
                add_from(from_z[matrix].at[layer, 0], mine[matrix].at[layer, 2])
                z_grad(matrix, layer, 2).start()

    def sum_z(section, layer, matrix):
        def one(step):
            z_grad(matrix, layer, step).wait_recv()
            add_from(from_z[matrix].at[layer, step], mine[matrix].at[layer, 0])

        steps = here.departures()[:-1]
        if here.relays:
            one(steps[0])
            pl.when(here.middle)(lambda: one(steps[1]))
            one(2)
        else:
            for step in steps:
                one(step)
        if section != layer:
            x_grad(matrix, layer, 0).start()

    def last(section, layer, matrix):
        x_grad(matrix, layer, 0).wait_recv()
        add_from(from_x[matrix].at[layer, 0], mine[matrix].at[layer, 0])

    actions = dict(core=core, send=send, add=add, relay=relay, sum=sum_z, last=last)

    def act(section, events):
        for name, layer, matrix, *more in events:
            actions[name](section, layer, matrix, *more)

    def point(layer, name):
        for section in range(2):
            events = SUM_UP[section].get((layer, name))
            if events:
                pl.when(s == section)(functools.partial(act, section, events))

    def total(value):
        return jnp.sum(value, 0, keepdims=True)

    def note(layer, row, value):
        gvec[layer, row : row + 1, :] = gvec[layer, row : row + 1, :] + total(value)

    def begin(layer, part, value):
        span = slice(*parts[part])
        grad_all[layer, 0, span] = value
        y_start(grad_all.at[layer, 0], grad_all.at[layer, 1], 4 * (1 - layer), part)
        note(layer, 5, value)

    def contract(layer, image, span):
        for piece in range(width_ff // depth):
            lanes = slice(piece * depth, (piece + 1) * depth)
            grad_hidden = dot(grad_all[layer, image, span], wb[:, lanes], 1, 0)
            value = pre[image, span, lanes]
            upper = phi_big(value)
            hidden[image, span, lanes] = value * upper
            pre[image, span, lanes] = grad_hidden * (upper + value * phi_small(value))

    everything = slice(0, rows)
    for part in range(2):
        span = slice(*parts[part])
        begin(1, part, cot[span] * live[span, 0:1])
    for layer in (1, 0):
        vectors = Vectors(vec.at[layer], width, None)
        base = 4 * (1 - layer)
        point(layer, "a")
        loaded("wd")
        loaded("pre")
        contract(layer, 0, everything)
        loaded("wu")
        own_part[...] = dot(pre[0], wu[...], 1, 1)
        if layer == 0:
            y_departed(1)
        for part in range(2):
            span = slice(*parts[part])
            point(layer, "b%d" % part)
            y_wait(base, part)
            contract(layer, 1, span)
            sending[0, span] = dot(pre[1, span], wu[...], 1, 1)
            y_start(sending.at[0], received.at[2 * (1 - layer)], base + 1, part)
        load("wo", layer)
        load("wq", layer)
        if layer == 1:
            load("wu", 0)
        point(layer, "c")
        product(D, layer, grad_all.at[layer], hidden)
        point(layer, "d")
        loaded("n2")
        product(U, layer, n2, pre)
        for piece in range(width_ff // depth):
            lanes = slice(piece * depth, (piece + 1) * depth)
            note(layer, 9 + piece, pre[0, :, lanes])
            note(layer, 9 + piece, pre[1, :, lanes])
        if layer == 1:
            load("pre", 0)
            load("n2", 0)
        loaded("mid")
        for part in range(2):
            span = slice(*parts[part])
            point(layer, "e%d" % part)
            unit, inverse = normalize(mid[span])
            y_wait(base + 1, part)
            grad_second = own_part[span] + received[2 * (1 - layer), span]
            grad_middle = grad_all[layer, 0, span] + normalize_back(
                grad_second * vectors.gain(1), unit, inverse
            )
            mid_all[layer, 0, span] = grad_middle
            y_start(mid_all.at[layer, 0], mid_all.at[layer, 1], base + 2, part)
            note(layer, 1, grad_second * unit)
            note(layer, 3, grad_second)
            note(layer, 4, grad_middle)
        if layer == 1:
            load("mid", 0)
        point(layer, "f")
        loaded("wo")
        loaded("joined")
        loaded("mixed")
        grad_mixed[...] = dot(mid_all[layer, 0], wo[...], 1, 0)
        attend_back(joined.at[0], mixed.at[0], grad_mixed, grad_joined.at[0], seq)
        loaded("wq")
        own_part[...] = dot(grad_joined[0], wq[...], 1, 1)
        for part in range(2):
            span = slice(*parts[part])
            point(layer, "g%d" % part)
            y_wait(base + 2, part)
            grad_mixed[span] = dot(mid_all[layer, 1, span], wo[...], 1, 0)
        attend_back(joined.at[1], mixed.at[1], grad_mixed, grad_joined.at[1], seq)
        if layer == 0:
            y_departed(3)
        for part in range(2):
            span = slice(*parts[part])
            sending[1, span] = dot(grad_joined[1, span], wq[...], 1, 1)
            y_start(sending.at[1], received.at[2 * (1 - layer) + 1], base + 3, part)
        if layer == 1:
            load("wd", 0)
            load("joined", 0)
        point(layer, "h")
        product(O, layer, mid_all.at[layer], mixed)
        loaded("n1")
        product(Q, layer, n1, grad_joined)
        if layer == 1:
            load("mixed", 0)
            load("n1", 0)
        for image in range(2):
            for piece in (0, 2):
                lanes = slice(piece * width, (piece + 1) * width)
                spot = slice(piece // 2 * width, (piece // 2 + 1) * width)
                gvec[layer, 8:9, spot] = gvec[layer, 8:9, spot] + total(
                    grad_joined[image, :, lanes]
                )
        point(layer, "i")
        loaded("hs")
        for part in range(2):
            span = slice(*parts[part])
            point(layer, "j%d" % part)
            unit, inverse = normalize(hs[span])
            y_wait(base + 3, part)
            grad_first = own_part[span] + received[2 * (1 - layer) + 1, span]
            value = mid_all[layer, 0, span] + normalize_back(
                grad_first * vectors.gain(0), unit, inverse
            )
            gin[layer, span] = value
            if layer == 1:
                begin(0, part, value * live[span, 0:1])
            note(layer, 0, grad_first * unit)
            note(layer, 2, grad_first)
        if layer == 1:
            load("hs", 0)
            pl.when(s == 0)(gin_copy().start)
    point(0, "t0")
    copy = launch(remote(gvec, vy, v_send.at[0], v_recv.at[0], here.y_peer))
    point(0, "t1")
    departed(copy)
    copy.wait_recv()
    gvec[:, 0:8, :] = gvec[:, 0:8, :] + vy[:, 0:8, :]
    copy = launch(remote(gvec, vc, v_send.at[1], v_recv.at[1], here.core_peer))
    point(0, "t2")
    departed(copy)
    copy.wait_recv()
    gvec[...] = gvec[...] + vc[...]
    copies = []
    for step in range(1, chips):
        copies.append(
            launch(
                remote(
                    gvec,
                    vz.at[step - 1],
                    v_send.at[1 + step],
                    v_recv.at[1 + step],
                    here.z_peer(step),
                )
            )
        )
    pl.when(s == 1)(gin_copy().start)
    point(0, "t3")
    for copy in copies:
        departed(copy)
        copy.wait_recv()
    for step in range(1, chips):
        gvec[...] = gvec[...] + vz[step - 1]
    copy = launch(
        remote(
            gvec.at[1 - s], vx, v_send.at[chips + 1], v_recv.at[chips + 1], here.x_peer
        )
    )
    point(0, "t4")
    for section in range(2):

        @pl.when(s == section)
        def _():
            for matrix in range(4):
                outs[matrix][...] = mine[matrix][section, 0]

    copy.wait_recv()
    gvec[s] = gvec[s] + vx[...]
    for slot in range(2):
        settle_all(slot)
    out_copy.wait_recv()
    gin_copy().wait()
    for item in departing:
        item.wait_send()
    for item in exchanges.values():
        item.wait_send()

    def departures(section):
        for layer in range(2):
            own = section == layer
            for matrix in range(4):
                path = SUMS[layer][matrix]
                if path != (VIA_OTHER if own else VIA_OWN):
                    for step in here.departures()[:-1]:
                        z_grad(matrix, layer, step).wait_send()
                    if not own:
                        x_grad(matrix, layer, 0).wait_send()
                elif own:
                    for step in range(1, chips):
                        x_grad(matrix, layer, step).wait_send()
                else:
                    for step in range(chips):
                        x_grad(matrix, layer, step).wait_send()

    for section in range(2):
        pl.when(s == section)(functools.partial(departures, section))


def backward(chips, seq, cot, live, vec, out_all, hs, mid, whole, kept):
    rows, depth = cot.shape
    sent_rows = up_to(seq, 8)
    width, width_ff = whole[1].shape[2], whole[2].shape[2]
    widths = [w.shape[2] for w in whole]
    block = depth // (2 * chips)
    any_space = pl.BlockSpec(memory_space=pl.ANY)
    vmem = pl.BlockSpec(memory_space=pltpu.VMEM)
    outs = [
        ((2, rows, depth), vmem),
        (vec.shape, vmem),
        *[((block, w), vmem) for w in widths],
        ((rows, depth), any_space),
        ((rows, depth), any_space),
        *[((2, chips, block, w), any_space) for w in widths * 3],
    ]
    sems = pltpu.SemaphoreType.DMA
    scratch = [
        pltpu.VMEM((depth, width_ff), F32),
        pltpu.VMEM((depth, width_ff), F32),
        pltpu.VMEM((rows, depth), F32),
        pltpu.VMEM((rows, depth), F32),
        pltpu.VMEM((2, rows, depth), F32),
        pltpu.VMEM((2, rows, depth), F32),
        pltpu.VMEM((2, rows, 3 * width), F32),
        pltpu.VMEM((2, rows, width), F32),
        pltpu.VMEM((2, rows, width_ff), F32),
        pltpu.VMEM((2, rows, width_ff), F32),
        pltpu.VMEM((2, 2, rows, depth), F32),
        pltpu.VMEM((2, 2, rows, depth), F32),
        pltpu.VMEM((4, rows, depth), F32),
        pltpu.VMEM((2, rows, depth), F32),
        pltpu.VMEM((rows, depth), F32),
        pltpu.VMEM((rows, width), F32),
        pltpu.VMEM((2, rows, 3 * width), F32),
        *[pltpu.VMEM((2, chips, block, w), F32) for w in widths],
        pltpu.VMEM((2, depth, depth), F32),
        pltpu.VMEM((chips, block, width_ff), F32),
        pltpu.VMEM((block, width_ff), F32),
        pltpu.VMEM(vec.shape, F32),
        pltpu.VMEM(vec.shape, F32),
        pltpu.VMEM((chips - 1,) + vec.shape, F32),
        pltpu.VMEM(vec.shape[1:], F32),
        sems((8, 2)),
        sems((8, 2)),
        sems((11,)),
        sems((2, chips)),
        sems((2, chips)),
        sems((2, 4, 3, chips)),
        *[sems((2, 4, chips)) for _ in range(4)],
        sems,
        sems,
        sems((chips + 2,)),
        sems((chips + 2,)),
        sems((2,)),
        sems((2,)),
    ]
    results = pl.pallas_call(
        functools.partial(backward_kernel, chips, seq, sent_rows),
        out_shape=[jax.ShapeDtypeStruct(shape, F32) for shape, _ in outs],
        in_specs=[vmem] * 3 + [any_space] * 12,
        out_specs=[spec for _, spec in outs],
        scratch_shapes=scratch,
        compiler_params=pltpu.CompilerParams(
            collective_id=1, has_side_effects=True, vmem_limit_bytes=VMEM_BYTES
        ),
        name="backward_both",
    )(cot, live, vec, out_all, hs, mid, *whole, *kept)
    return results[:8]


def body(
    embedded,
    image_counts,
    cotangent,
    qkv_weight,
    qv_bias,
    out_weight,
    up_weight,
    up_bias,
    down_weight,
    norm_gains,
    shift_terms,
):
    groups = lax.axis_size("dp")
    chips = groups // 2
    tensors = lax.axis_size("tensor")
    s = lax.axis_index("section")
    t = lax.axis_index("tensor")
    d = lax.axis_index("dp")
    seq, depth = embedded.shape[3:]
    rows = up_to(seq, 16)
    block = qkv_weight.shape[1]
    width = qkv_weight.shape[3]
    width_ff = up_weight.shape[2]

    def padded(value):
        chosen = lax.dynamic_index_in_dim(value[:, 0, 0], s, 0, keepdims=False)
        return jnp.pad(chosen, ((0, rows - seq), (0, 0)))

    slot = s * tensors + t
    alive = (slot < image_counts[0]).astype(F32)
    inside = lax.broadcasted_iota(jnp.int32, (rows, 128), 0) < seq
    live = jnp.where(inside, alive, 0.0)

    def spread(pieces, parts, part):
        count, piece = pieces.shape
        tiled = jnp.broadcast_to(pieces[:, None, :], (count, parts, piece))
        mine = lax.broadcasted_iota(jnp.int32, (count, parts, piece), 1) == part
        return jnp.where(mine, tiled, 0.0).reshape(count, parts * piece)

    wide = jnp.concatenate([norm_gains[0], shift_terms[0], jnp.zeros_like(norm_gains[0])])
    wide = spread(wide, tensors * groups, t * groups + d)
    biases = spread(qv_bias[0], groups, d).reshape(-1, depth)
    ups = spread(up_bias, groups, d).reshape(-1, depth)
    packed = jnp.concatenate([wide, biases, ups])
    packed = jnp.pad(packed, ((0, up_to(packed.shape[0], 8) - packed.shape[0]), (0, 0)))

    shards = (
        qkv_weight[0].reshape(block, 3 * width),
        out_weight[0].T,
        up_weight[0],
        down_weight[0].T,
    )
    out_all, vec, hs, mid, gq, go, gu, gd, *kept = forward(
        chips, seq, padded(embedded), live, packed, *shards
    )
    gin, gvec, sum_q, sum_o, sum_u, sum_d, gin_x, out_x = backward(
        chips,
        seq,
        padded(cotangent),
        live,
        vec,
        out_all,
        hs,
        mid,
        (gq, go, gu, gd),
        kept,
    )
    vec_sum = lax.dynamic_index_in_dim(gvec, s, 0, keepdims=False)

    def both(own, other):
        mine = lax.dynamic_index_in_dim(own, s, 0, keepdims=False)[:seq]
        other = other[:seq]
        first = jnp.where(s == 0, mine, other)
        second = jnp.where(s == 0, other, mine)
        return jnp.stack([first, second])[None, :, None, None]

    piece = depth // (tensors * groups)
    wide = lax.dynamic_slice_in_dim(vec_sum[0:6], (t * groups + d) * piece, piece, 1)
    biases = vec_sum[8].reshape(2, width)
    biases = lax.dynamic_slice_in_dim(biases, d * (width // groups), width // groups, 1)
    count = width_ff // depth
    ups = vec_sum[9 : 9 + count].reshape(width_ff)
    ups = lax.dynamic_slice_in_dim(ups, d * (width_ff // groups), width_ff // groups, 0)
    return (
        both(out_all, out_x),
        both(gin, gin_x),
        sum_q.reshape(1, block, 3, width),
        biases[None],
        sum_o.T[None],
        sum_u[None],
        ups[None],
        sum_d.T[None],
        wide[None, 0:2],
        wide[None, 2:6],
    )


def solution(mesh):
    placed = (
        P(None, "dp", "tensor", None, None),
        P("dp"),
        P(None, "dp", "tensor", None, None),
        P("section", "dp", None, "tensor"),
        P("section", None, ("tensor", "dp")),
        P("section", "tensor", "dp"),
        P("section", "dp", "tensor"),
        P("section", ("tensor", "dp")),
        P("section", "tensor", "dp"),
        P("section", None, ("tensor", "dp")),
        P("section", None, ("tensor", "dp")),
    )
    return jax.shard_map(
        body,
        mesh=mesh,
        in_specs=placed,
        out_specs=(
            P("section", None, "dp", "tensor", None, None),
            P("section", None, "dp", "tensor", None, None),
            P("section", "dp", None, "tensor"),
            P("section", None, ("tensor", "dp")),
            P("section", "tensor", "dp"),
            P("section", "dp", "tensor"),
            P("section", ("tensor", "dp")),
            P("section", "tensor", "dp"),
            P("section", None, ("tensor", "dp")),
            P("section", None, ("tensor", "dp")),
        ),
        check_vma=False,
    )
```

```python
import functools

import jax
import jax.numpy as jnp
from jax import lax
from jax.experimental import pallas as pl
from jax.experimental.pallas import tpu as pltpu
from jax.sharding import PartitionSpec as P

HD = 64
SCALE = HD ** (-0.5)
EPS = 1e-06
HIGH = lax.Precision.HIGH
MESH = pl.DeviceIdType.MESH
VMEM_BYTES = 63 * 2**20
F32 = jnp.float32


def dot(left, right, left_dim, right_dim):
    return lax.dot_general(
        left,
        right,
        (((left_dim,), (right_dim,)), ((), ())),
        precision=HIGH,
        preferred_element_type=F32,
    )


def up_to(count, step):
    return -(-count // step) * step


def normalize(value):
    centred = value - jnp.mean(value, -1, keepdims=True)
    inverse = lax.rsqrt(jnp.mean(centred * centred, -1, keepdims=True) + EPS)
    return centred * inverse, inverse


def normalize_back(grad_unit, unit, inverse):
    return inverse * (
        grad_unit
        - jnp.mean(grad_unit, -1, keepdims=True)
        - unit * jnp.mean(grad_unit * unit, -1, keepdims=True)
    )


class Place:
    def __init__(self, chips):
        self.s = lax.axis_index("section")
        self.t = lax.axis_index("tensor")
        d = lax.axis_index("dp")
        self.chips = chips
        self.z = d // 2
        self.c = d % 2
        self.x_peer = (1 - self.s, self.t, d)
        self.y_peer = (self.s, 1 - self.t, d)
        self.core_peer = (self.s, self.t, self.z * 2 + 1 - self.c)

    def z_at(self, step):
        return (self.z + self.chips + step) % self.chips

    def z_peer(self, step):
        return (self.s, self.t, self.z_at(step) * 2 + self.c)

    def greet(self):
        barrier = pltpu.get_barrier_semaphore()
        peers = [self.x_peer, self.y_peer, self.core_peer]
        peers += [self.z_peer(step) for step in range(1, self.chips)]
        for peer in peers:
            pl.semaphore_signal(barrier, inc=1, device_id=peer, device_id_type=MESH)
        pl.semaphore_wait(barrier, len(peers))


    @property
    def relays(self):
        return self.chips == 4

    def arrivals(self):
        if not self.relays:
            return list(range(1, self.chips))
        near = jnp.where(self.z < 2, 3, 1)
        return [2, near, 4 - near]

    def departures(self):
        if not self.relays:
            return list(range(1, self.chips)) + [0]
        far = jnp.where(self.z < 2, 3, 1)
        return [far, 4 - far, 2, 0]

    @property
    def middle(self):
        return (self.z == 1) | (self.z == 2)

    def direct(self, step):
        if not self.relays or step == 2:
            return None
        return self.z <= 2 if step == 1 else self.z >= 1


def when(condition, action):
    if condition is None:
        action()
    else:
        pl.when(condition)(action)


def parts_of(rows):
    first = up_to(rows // 2, 8)
    return [(0, first), (first, rows)]


def remote(src, dst, send, recv, peer):
    return pltpu.make_async_remote_copy(
        src_ref=src,
        dst_ref=dst,
        send_sem=send,
        recv_sem=recv,
        device_id=peer,
        device_id_type=MESH,
    )


def key_mask(rows, seq):
    return lax.broadcasted_iota(jnp.int32, (rows, rows), 1) < seq


def head_lanes(which):
    return lax.broadcasted_iota(jnp.int32, (1, 2 * HD), 1) // HD == which


def attend(joined, mixed, seq):
    rows, width = mixed.shape
    keep = key_mask(rows, seq)
    for pair in range(width // (2 * HD)):
        lanes = slice(pair * 2 * HD, (pair + 1) * 2 * HD)
        query = joined[:, lanes] * SCALE
        keys = joined[:, width + lanes.start : width + lanes.stop]
        values = joined[:, 2 * width + lanes.start : 2 * width + lanes.stop]
        total = None
        for which in range(2):
            own = head_lanes(which)
            scores = dot(query, jnp.where(own, keys, 0.0), 1, 1)
            scores = jnp.where(keep, scores, -3e38)
            weights = jnp.exp(scores - jnp.max(scores, -1, keepdims=True))
            probs = weights / jnp.sum(weights, -1, keepdims=True)
            part = dot(probs, jnp.where(own, values, 0.0), 1, 0)
            total = part if total is None else total + part
        mixed[:, lanes] = total


def attend_back(joined, mixed, grad_mixed, grad_joined, seq):
    rows, width = mixed.shape
    keep = key_mask(rows, seq)
    for pair in range(width // (2 * HD)):
        lanes = slice(pair * 2 * HD, (pair + 1) * 2 * HD)
        query = joined[:, lanes] * SCALE
        keys = joined[:, width + lanes.start : width + lanes.stop]
        values = joined[:, 2 * width + lanes.start : 2 * width + lanes.stop]
        grad = grad_mixed[:, lanes]
        product = grad * mixed[:, lanes]
        grads = [None, None, None]
        for which in range(2):
            own = head_lanes(which)
            own_keys = jnp.where(own, keys, 0.0)
            scores = dot(query, own_keys, 1, 1)
            scores = jnp.where(keep, scores, -3e38)
            weights = jnp.exp(scores - jnp.max(scores, -1, keepdims=True))
            probs = weights / jnp.sum(weights, -1, keepdims=True)
            own_grad = jnp.where(own, grad, 0.0)
            row_dot = jnp.sum(jnp.where(own, product, 0.0), -1, keepdims=True)
            grad_probs = dot(grad, jnp.where(own, values, 0.0), 1, 1)
            grad_scores = probs * (grad_probs - row_dot)
            parts = (
                dot(grad_scores, own_keys, 1, 0) * SCALE,
                dot(grad_scores, jnp.where(own, query, 0.0), 0, 0),
                dot(probs, own_grad, 0, 0),
            )
            grads = [b if a is None else a + b for a, b in zip(grads, parts)]
        for number, part in enumerate(grads):
            start = number * width + lanes.start
            grad_joined[:, start : start + 2 * HD] = part


def phi_big(value):
    return 0.5 * (1.0 + lax.erf(value * 0.7071067811865476))


def phi_small(value):
    return jnp.exp(-0.5 * value * value) * 0.3989422804014327


class Vectors:
    def __init__(self, ref, width, hidden):
        self.ref, self.width, self.hidden = ref, width, hidden

    def gain(self, which):
        return self.ref[which : which + 1, :]

    def shift(self, which):
        return self.ref[2 + which : 3 + which, :]

    def query(self):
        return self.ref[8:9, 0 : self.width]

    def value(self):
        return self.ref[8:9, self.width : 2 * self.width]

    def up(self, row):
        return self.ref[9 + row : 10 + row, :]


def place(tile, start, piece, lanes):
    lane = lax.broadcasted_iota(jnp.int32, tile.shape, 1)
    tile = jnp.where(lane < piece, tile, 0.0)
    first, shift = divmod(start, 128)
    if shift == 0:
        return {first: tile}
    turned = pltpu.roll(tile, shift, 1)
    if shift + piece <= 128:
        return {first: turned}
    return {
        first: jnp.where(lane >= shift, turned, 0.0),
        first + 1: jnp.where(lane < shift, turned, 0.0),
    }


def take(read, start, piece):
    first, shift = divmod(start, 128)
    tile = read(first)
    lane = lax.broadcasted_iota(jnp.int32, tile.shape, 1)
    if shift:
        tile = pltpu.roll(tile, 128 - shift, 1)
        if shift + piece > 128:
            after = pltpu.roll(read(first + 1), 128 - shift, 1)
            tile = jnp.where(lane < 128 - shift, tile, after)
    return jnp.where(lane < piece, tile, 0.0)


def spread_vectors(target, pieces, piece, chips, own):
    depth = target.shape[1]
    width = depth // 2
    tiles = [{} for _ in range(3)]

    def gather(kind, found, rows):
        for index, value in found.items():
            value = jnp.where(rows, value, 0.0)
            old = tiles[kind].get(index)
            tiles[kind][index] = value if old is None else old + value

    row = lax.broadcasted_iota(jnp.int32, (8, 128), 0)
    for chip in range(chips):
        for core in range(2):
            number = chip * 2 + core
            for tensor in range(2):
                tile = pieces(tensor, core, chip)[0:8]
                start = (tensor * 2 * chips + number) * piece
                gather(0, place(tile, start, piece, depth), row < 6)
            tile = pieces(own, core, chip)
            for part in range(2):
                found = place(tile[0:8], part * width + number * piece, piece, depth)
                gather(1, found, row == 6 + part)
            for part in range(4):
                found = place(tile[8:16], (number * 4 + part) * piece, piece, depth)
                gather(2, found, row == part)
    for index in range(depth // 128):
        lanes = slice(index * 128, (index + 1) * 128)
        target[0:8, lanes] = tiles[0][index]
        target[8:9, lanes] = jnp.sum(tiles[1][index], 0, keepdims=True)
        for up in range(2):
            value = tiles[2][up * (depth // 128) + index]
            target[9 + up : 10 + up, lanes] = jnp.sum(value, 0, keepdims=True)


def cut_vectors(source, piece, chips, own, write):
    depth = source.shape[1]
    width = depth // 2
    row = lax.broadcasted_iota(jnp.int32, (8, 128), 0)
    for chip in range(chips):
        for core in range(2):
            number = chip * 2 + core
            upper = jnp.zeros((8, 128), F32)
            for part in range(2):
                start = part * width + number * piece
                found = take(lambda n: source[8:9, n * 128 : n * 128 + 128], start, piece)
                upper = jnp.where(row == 6 + part, found, upper)
            lower = jnp.zeros((8, 128), F32)
            for part in range(4):
                up, start = divmod((number * 4 + part) * piece, depth)
                found = take(
                    lambda n: source[9 + up : 10 + up, n * 128 : n * 128 + 128], start, piece
                )
                lower = jnp.where(row == part, found, lower)
            for tensor in range(2):
                start = (tensor * 2 * chips + number) * piece
                wide = take(lambda n: source[0:8, n * 128 : n * 128 + 128], start, piece)
                mine = jnp.where(own == tensor, 1.0, 0.0)
                write(
                    tensor,
                    core,
                    chip,
                    jnp.where(row < 6, wide, upper * mine),
                    lower * mine,
                )


def add_rows(target, sources, step):
    rows = target.shape[0]

    @pl.loop(0, rows // step)
    def _(index):
        here = pl.ds(pl.multiple_of(index * step, 8), step)
        total = target[here, :]
        for source in sources:
            total = total + source[here, :]
        target[here, :] = total


Q, O, U, D = range(4)

VIA_OWN, BOTH, VIA_OTHER = range(3)

(START, LAYER, MIXED, TOKENS, MIDDLE, SECOND, SECONDS, HIDDEN, RESULT) = range(0, 72, 8)
(GRADS, PRODUCTS, PRODUCT_UP, HEADS, MIDDLES, PRODUCT_OUT, REST, ENDING) = range(72, 136, 8)

OWN, SPREAD, OVER_Z, OVER_X = range(4)
CORE, SEND, ADD, RELAY, SUM, LAST = range(6)
GATHER = (
    (VIA_OWN, VIA_OWN, VIA_OTHER, VIA_OWN),
    (VIA_OWN, VIA_OWN, VIA_OTHER, VIA_OWN),
)

PASS_ON = (
    {
        (0, START): (
            (OWN, 0, U), (SPREAD, 0, O), (OWN, 0, Q), (OVER_Z, 0, O, 1), (SPREAD, 0, Q),
            (OVER_Z, 0, O, 0), (OWN, 0, O), (OVER_Z, 0, Q, 0), (OVER_Z, 0, Q, 1),
            (OVER_Z, 0, Q, 2), (SPREAD, 0, D), (OWN, 0, D), (OVER_Z, 0, O, 2),
            (OVER_X, 1, O, 0),
        ),
        (0, LAYER): (
            (OVER_Z, 0, D, 1),
        ),
        (0, MIXED): (
            (OVER_X, 1, U, -1),
        ),
        (0, TOKENS + 0): (
            (OVER_X, 1, Q, 0), (OVER_X, 1, D, -1),
        ),
        (0, TOKENS + 1): (
            (OVER_Z, 0, D, 0),
        ),
        (0, MIDDLE + 0): (
            (OVER_X, 0, U, 0),
        ),
        (0, MIDDLE + 1): (
            (OVER_Z, 0, D, 2), (OVER_X, 1, Q, 1), (OVER_X, 0, U, 1),
        ),
        (0, SECOND): (
            (OVER_X, 0, U, 2),
        ),
        (0, SECONDS + 1): (
            (OVER_Z, 1, U, 0),
        ),
        (0, RESULT + 0): (
            (OVER_X, 1, Q, -1), (OVER_X, 1, O, -1), (OVER_Z, 1, U, 1), (OVER_X, 1, Q, 2),
        ),
        (0, RESULT + 1): (
            (OVER_X, 1, O, 1), (OVER_X, 1, D, 0),
        ),
        (1, MIXED): (
            (OVER_X, 1, O, 2), (OVER_Z, 1, U, 2),
        ),
        (1, SECOND): (
            (OVER_X, 1, D, 2),
        ),
        (1, HIDDEN): (
            (OVER_X, 1, D, 1),
        ),
    },
    {
        (0, START): (
            (SPREAD, 1, O), (OWN, 1, U), (OWN, 1, D), (SPREAD, 1, Q), (OWN, 1, Q),
            (OVER_Z, 1, O, 0), (OVER_Z, 1, O, 1), (OVER_X, 0, U, -1), (OVER_Z, 1, Q, 0),
        ),
        (0, LAYER): (
            (OWN, 1, O), (OVER_X, 0, O, -1), (OVER_X, 0, Q, -1), (OVER_X, 0, O, 0),
            (OVER_Z, 1, Q, 1), (OVER_X, 0, O, 1), (OVER_X, 0, Q, 2), (OVER_Z, 0, U, 1),
            (OVER_X, 0, Q, 1), (SPREAD, 1, D), (OVER_X, 0, Q, 0),
        ),
        (0, MIXED): (
            (OVER_X, 0, D, -1), (OVER_Z, 0, U, 0), (OVER_X, 0, O, 2),
        ),
        (0, MIDDLE + 0): (
            (OVER_Z, 0, U, 2),
        ),
        (0, SECONDS + 0): (
            (OVER_X, 0, D, 1), (OVER_Z, 1, Q, 2), (OVER_X, 0, D, 0),
        ),
        (0, SECONDS + 1): (
            (OVER_Z, 1, D, 0), (OVER_X, 0, D, 2),
        ),
        (0, RESULT + 0): (
            (OVER_Z, 1, O, 2), (OVER_Z, 1, D, 1), (OVER_X, 1, U, 0),
        ),
        (1, TOKENS + 0): (
            (OVER_Z, 1, D, 2), (OVER_X, 1, U, 1),
        ),
        (1, MIDDLE + 0): (
            (OVER_X, 1, U, 2),
        ),
    },
)


def forward_kernel(
    chips,
    seq,
    sent_rows,
    x_in,
    live,
    vec_in,
    wq,
    wo,
    wu,
    wd,
    out_all,
    vec,
    hs,
    mid,
    gq_out,
    go_out,
    gu_out,
    gd_out,
    n1_out,
    n2_out,
    joined_out,
    mixed_out,
    pre_out,
    gq,
    go,
    gu,
    gd,
    n1,
    n2,
    joined,
    mixed,
    pre,
    hidden,
    received,
    sending,
    pieces,
    y_send,
    y_recv,
    v_send,
    v_recv,
    zs,
    zr,
    xs,
    xr,
    cs,
    cr,
    local,
    save,
):
    here = Place(chips)
    s, c, z = here.s, here.c, here.z
    shards = (wq, wo, wu, wd)
    whole = (gq, go, gu, gd)
    block = wo.shape[0]
    rows, depth = x_in.shape
    width = go.shape[2]
    tail = rows - sent_rows
    parts = parts_of(rows)
    for buffer in (n1, n2):
        for layer in range(2):
            buffer[layer, 1, sent_rows:rows, :] = jnp.zeros((tail, depth), F32)
    for index in range(received.shape[0]):
        received[index, sent_rows:rows, :] = jnp.zeros((tail, depth), F32)
    here.greet()


    def spot(matrix, layer, back, core=None):
        start = (here.z_at(-back) * 2 + (c if core is None else core)) * block
        span = pl.ds(pl.multiple_of(start, 8), block)
        if matrix == Q:
            return whole[matrix].at[layer, :, span, :]
        return whole[matrix].at[layer, span, :]

    def z_copy(layer, matrix, step, src=None):
        place = spot(matrix, layer, 0)
        return remote(
            place if src is None else src,
            place,
            zs.at[layer, matrix, step],
            zr.at[layer, matrix, step],
            here.z_peer(step),
        )

    def z_relay(layer, matrix):
        place = spot(matrix, layer, 2)
        step = jnp.where(z == 1, 3, 1)
        return remote(
            place,
            place,
            zs.at[layer, matrix, 0],
            zr.at[layer, matrix, 4 - step],
            here.z_peer(step),
        )

    def x_copy(layer, matrix, back, src=None):
        place = spot(matrix, layer, back)
        return remote(
            place if src is None else src,
            place,
            xs.at[layer, matrix, back],
            xr.at[layer, matrix, back],
            here.x_peer,
        )

    def c_copy(layer, matrix, back, src=None):
        place = spot(matrix, layer, back)
        return remote(
            place if src is None else src,
            place,
            cs.at[layer, matrix, back],
            cr.at[layer, matrix, back],
            here.core_peer,
        )

    def landed(place, sem):
        pltpu.make_async_copy(place, place, sem).wait()

    def z_spread(layer, matrix, src=None):
        for step in [2, 1, 3] if here.relays else range(1, chips):
            when(here.direct(step), z_copy(layer, matrix, step, src).start)

    count = chips - 1

    def act(section, event):
        kind, layer, matrix, *third = event
        own = section == layer
        path = GATHER[layer][matrix]
        if kind == OWN:
            x_copy(layer, matrix, 0, shards[matrix]).start()
        elif kind == SPREAD:
            z_spread(layer, matrix, shards[matrix])
        elif third[0] < 0:
            landed(spot(matrix, layer, 0), xr.at[layer, matrix, 0])
            if path != VIA_OWN:
                z_spread(layer, matrix)
            c_copy(layer, matrix, 0).start()
        else:
            for number in range(count * third[0] // 3, count * (third[0] + 1) // 3):
                back = here.arrivals()[number]
                place = spot(matrix, layer, back)
                if kind == OVER_X:
                    landed(place, xr.at[layer, matrix, back])
                else:
                    landed(place, zr.at[layer, matrix, back])
                    if here.relays and number == 0:
                        pl.when(here.middle)(z_relay(layer, matrix).start)
                    if path == (VIA_OWN if own else VIA_OTHER):
                        x_copy(layer, matrix, back).start()
                c_copy(layer, matrix, back).start()

    def point(layer, name):
        for section in range(2):
            events = PASS_ON[section].get((layer, name))
            if events:

                @pl.when(s == section)
                def _():
                    for event in events:
                        act(section, event)

    piece = depth // (4 * chips)
    pieces[here.t, c, s, z] = vec_in[...]
    copy = remote(
        pieces.at[here.t, c, s, z],
        pieces.at[here.t, c, s, z],
        v_send.at[0],
        v_recv.at[0],
        here.x_peer,
    )
    copy.start()
    copy.wait_send()
    landed(pieces.at[here.t, c, 1 - s, z], v_recv.at[0])
    vector_copies = []
    for step in range(1, chips):
        place_ = pieces.at[here.t, c, :, z]
        copy = remote(
            place_, place_, v_send.at[step], v_recv.at[step], here.z_peer(step)
        )
        copy.start()
        vector_copies.append(copy)
    own_copies = []
    for matrix in range(4):
        c_copy(s, matrix, 0, shards[matrix]).start()
        copy = pltpu.make_async_copy(
            shards[matrix], spot(matrix, s, 0), local.at[matrix]
        )
        copy.start()
        own_copies.append(copy)
    point(0, START)
    for step in range(1, chips):
        vector_copies[step - 1].wait_send()
        landed(pieces.at[here.t, c, :, here.z_at(-step)], v_recv.at[step])
    place_ = pieces.at[here.t, c]
    copy = remote(place_, place_, v_send.at[chips], v_recv.at[chips], here.y_peer)
    copy.start()
    copy.wait_send()
    landed(pieces.at[1 - here.t, c], v_recv.at[chips])
    place_ = pieces.at[:, c]
    copy = remote(
        place_, place_, v_send.at[chips + 1], v_recv.at[chips + 1], here.core_peer
    )
    copy.start()
    copy.wait_send()
    landed(pieces.at[:, 1 - c], v_recv.at[chips + 1])
    for layer in range(2):
        spread_vectors(
            vec.at[layer],
            lambda tensor, core, chip: pieces[tensor, core, layer, chip],
            piece,
            chips,
            here.t,
        )

    saves = {}

    def keep(name, src, dst, sem):
        copy = pltpu.make_async_copy(src, dst, save.at[sem])
        copy.start()
        saves[name] = copy

    def before_write(name):
        if name in saves:
            saves.pop(name).wait()

    def finish(layer, matrix):
        pl.when(s == layer)(own_copies[matrix].wait)
        for back in range(chips):
            landed(spot(matrix, layer, back, 1 - c), cr.at[layer, matrix, back])
        if matrix == Q:
            for part in range(3):
                keep(
                    "whole%d%d%d" % (layer, matrix, part),
                    whole[matrix].at[layer, part],
                    gq_out.at[layer, :, pl.ds(part * width, width)],
                    22 + 3 * layer + part,
                )
        else:
            keep(
                "whole%d%d" % (layer, matrix),
                whole[matrix].at[layer],
                (None, go_out, gu_out, gd_out)[matrix].at[layer],
                14 + 4 * layer + matrix,
            )

    exchanges = {}

    def y_start(src, dst, index, part):
        start, stop = parts[part]
        span = pl.ds(start, min(stop, sent_rows) - start)
        copy = remote(
            src.at[span],
            dst.at[span],
            y_send.at[index, part],
            y_recv.at[index, part],
            here.y_peer,
        )
        copy.start()
        exchanges[index, part] = copy

    def y_wait(index, part):
        exchanges[index, part].wait_recv()

    def y_departed(index):
        for part in range(2):
            exchanges.pop((index, part)).wait_send()

    def begin(layer, part, value):
        span = slice(*parts[part])
        hs[layer, span] = value
        unit, _ = normalize(value)
        vectors = Vectors(vec.at[layer], width, None)
        n1[layer, 0, span] = unit * vectors.gain(0) + vectors.shift(0)
        y_start(n1.at[layer, 0], n1.at[layer, 1], 4 * layer, part)

    def project(layer, image, span):
        vectors = Vectors(vec.at[layer], width, None)
        for piece in range(3):
            lanes = slice(piece * width, (piece + 1) * width)
            value = dot(n1[layer, image, span], gq[layer, piece], 1, 0)
            if piece == 0:
                value = value + vectors.query()
            if piece == 2:
                value = value + vectors.value()
            joined[image, span, lanes] = value

    def expand(layer, image, span):
        vectors = Vectors(vec.at[layer], width, None)
        for piece in range(pre.shape[2] // depth):
            lanes = slice(piece * depth, (piece + 1) * depth)
            value = dot(n2[layer, image, span], gu[layer, :, lanes], 1, 0)
            value = value + vectors.up(piece)
            pre[image, span, lanes] = value
            hidden[image, span, lanes] = value * phi_big(value)

    everything = slice(0, rows)
    for part in range(2):
        begin(0, part, x_in[slice(*parts[part])])
    for layer in range(2):
        vectors = Vectors(vec.at[layer], width, None)
        point(layer, LAYER)
        before_write("joined")
        before_write("mixed")
        finish(layer, Q)
        project(layer, 0, everything)
        attend(joined.at[0], mixed.at[0], seq)
        point(layer, MIXED)
        finish(layer, O)
        mid[layer] = hs[layer] + dot(mixed[0], go[layer], 1, 1) + vectors.shift(2)
        for part in range(2):
            point(layer, TOKENS + part)
            y_wait(4 * layer, part)
            project(layer, 1, slice(*parts[part]))
        attend(joined.at[1], mixed.at[1], seq)
        if layer == 1:
            y_departed(1)
        for part in range(2):
            span = slice(*parts[part])
            sending[0, span] = dot(mixed[1, span], go[layer], 1, 1)
            y_start(sending.at[0], received.at[2 * layer], 4 * layer + 1, part)
        keep("n1%d" % layer, n1.at[layer], n1_out.at[layer], 4 + layer)
        keep("joined", joined, joined_out.at[layer], 6 + layer)
        keep("mixed", mixed, mixed_out.at[layer], 8 + layer)
        for part in range(2):
            span = slice(*parts[part])
            point(layer, MIDDLE + part)
            y_wait(4 * layer + 1, part)
            middle = mid[layer, span] + received[2 * layer, span]
            mid[layer, span] = middle
            unit, _ = normalize(middle)
            n2[layer, 0, span] = unit * vectors.gain(1) + vectors.shift(1)
            y_start(n2.at[layer, 0], n2.at[layer, 1], 4 * layer + 2, part)
        point(layer, SECOND)
        before_write("pre")
        finish(layer, U)
        expand(layer, 0, everything)
        if layer == 0:
            for part in range(2):
                point(0, SECONDS + part)
                y_wait(2, part)
                expand(0, 1, slice(*parts[part]))
        else:
            y_departed(3)
        point(layer, HIDDEN)
        finish(layer, D)
        if layer == 1:
            out_all[layer] = mid[layer] + dot(hidden[0], gd[layer], 1, 1)
        for part in range(2):
            span = slice(*parts[part])
            if layer == 1:
                point(1, SECONDS + part)
                y_wait(6, part)
                expand(1, 1, span)
            sending[1, span] = dot(hidden[1, span], gd[layer], 1, 1)
            y_start(sending.at[1], received.at[2 * layer + 1], 4 * layer + 3, part)
        if layer == 0:
            out_all[layer] = mid[layer] + dot(hidden[0], gd[layer], 1, 1)
        keep("n2%d" % layer, n2.at[layer], n2_out.at[layer], 10 + layer)
        keep("pre", pre, pre_out.at[layer], 12 + layer)
        for part in range(2):
            span = slice(*parts[part])
            point(layer, RESULT + part)
            y_wait(4 * layer + 3, part)
            result = out_all[layer, span] + received[2 * layer + 1, span]
            result = (result + vectors.shift(3)) * live[span, 0:1]
            out_all[layer, span] = result
            if layer == 0:
                begin(1, part, result)

    for copy in saves.values():
        copy.wait()
    for copy in exchanges.values():
        copy.wait_send()
    def z_departures(layer, matrix):
        for step in range(1, chips):
            when(here.direct(step), z_copy(layer, matrix, step).wait_send)
        if here.relays:
            pl.when(here.middle)(z_relay(layer, matrix).wait_send)

    def departures(section):
        for layer in range(2):
            for matrix in range(4):
                path = GATHER[layer][matrix]
                own = section == layer
                if own:
                    x_copy(layer, matrix, 0).wait_send()
                if path == (VIA_OWN if own else VIA_OTHER):
                    for back in range(1, chips):
                        x_copy(layer, matrix, back).wait_send()
                if path != (VIA_OTHER if own else VIA_OWN):
                    z_departures(layer, matrix)

    for section in range(2):
        pl.when(s == section)(functools.partial(departures, section))
    for layer in range(2):
        for matrix in range(4):
            for back in range(chips):
                c_copy(layer, matrix, back).wait_send()


def forward(chips, seq, x_in, live, vec_in, wq, wo, wu, wd):
    rows, depth = x_in.shape
    sent_rows = up_to(seq, 8)
    width = wo.shape[1]
    hidden = wu.shape[1]
    widths = (3 * width, width, hidden, hidden)
    whole = [(2, depth, w) for w in widths]
    any_space = pl.BlockSpec(memory_space=pl.ANY)
    vmem = pl.BlockSpec(memory_space=pltpu.VMEM)
    both = (2, 16, depth)
    outs = [
        ((2, rows, depth), vmem),
        (both, vmem),
        ((2, rows, depth), vmem),
        ((2, rows, depth), vmem),
        *[(w, any_space) for w in whole],
        ((2, 2, rows, depth), any_space),
        ((2, 2, rows, depth), any_space),
        ((2, 2, rows, 3 * width), any_space),
        ((2, 2, rows, width), any_space),
        ((2, 2, rows, hidden), any_space),
    ]
    sems = pltpu.SemaphoreType.DMA
    scratch = [
        pltpu.VMEM((2, 3, depth, width), F32),
        *[pltpu.VMEM(w, F32) for w in whole[1:]],
        pltpu.VMEM((2, 2, rows, depth), F32),
        pltpu.VMEM((2, 2, rows, depth), F32),
        pltpu.VMEM((2, rows, 3 * width), F32),
        pltpu.VMEM((2, rows, width), F32),
        pltpu.VMEM((2, rows, hidden), F32),
        pltpu.VMEM((2, rows, hidden), F32),
        pltpu.VMEM((4, rows, depth), F32),
        pltpu.VMEM((2, rows, depth), F32),
        pltpu.VMEM((2, 2, 2, chips) + vec_in.shape, F32),
        sems((8, 2)),
        sems((8, 2)),
        sems((chips + 2,)),
        sems((chips + 2,)),
        *[sems((2, 4, chips)) for _ in range(6)],
        sems((4,)),
        sems((28,)),
    ]
    return pl.pallas_call(
        functools.partial(forward_kernel, chips, seq, sent_rows),
        out_shape=[jax.ShapeDtypeStruct(shape, F32) for shape, _ in outs],
        in_specs=[vmem] * 3 + [any_space] * 4,
        out_specs=[spec for _, spec in outs],
        scratch_shapes=scratch,
        compiler_params=pltpu.CompilerParams(
            collective_id=0, has_side_effects=True, vmem_limit_bytes=VMEM_BYTES
        ),
        name="forward_both",
    )(x_in, live, vec_in, wq, wo, wu, wd)


SUMS = (
    (VIA_OTHER, VIA_OTHER, VIA_OWN, BOTH),
    (VIA_OTHER, VIA_OWN, VIA_OWN, VIA_OTHER),
)

SUM_UP = (
    {
        (1, MIDDLE + 0): (
            (CORE, 1, D),
        ),
        (1, HEADS): (
            (SEND, 1, D), (CORE, 1, U), (SEND, 1, U),
        ),
        (1, MIDDLES + 0): (
            (ADD, 1, D, 0),
        ),
        (1, RESULT + 0): (
            (ADD, 1, D, 1), (CORE, 1, O),
        ),
        (0, LAYER): (
            (ADD, 1, D, 2), (SEND, 1, O), (RELAY, 1, D), (CORE, 1, Q),
        ),
        (0, GRADS + 1): (
            (SEND, 1, Q), (ADD, 1, Q, 0),
        ),
        (0, MIDDLE + 0): (
            (CORE, 0, D), (SEND, 0, D),
        ),
        (0, MIDDLE + 1): (
            (CORE, 0, U), (SEND, 0, U), (ADD, 1, Q, 2), (ADD, 1, Q, 1),
        ),
        (0, MIDDLES + 0): (
            (RELAY, 1, Q),
        ),
        (0, REST): (
            (CORE, 0, O),
        ),
        (0, RESULT + 0): (
            (SEND, 0, O), (CORE, 0, Q), (RELAY, 0, D), (SEND, 0, Q),
        ),
        (0, RESULT + 1): (
            (ADD, 0, U, 2), (ADD, 0, U, 0), (SUM, 1, D), (ADD, 0, U, 1), (SUM, 0, D),
            (SUM, 1, Q), (ADD, 0, U, 3),
        ),
        (0, ENDING + 2): (
            (RELAY, 0, U),
        ),
        (0, ENDING + 3): (
            (LAST, 0, D), (LAST, 0, O),
        ),
        (0, ENDING + 4): (
            (SUM, 0, U), (LAST, 0, Q),
        ),
    },
    {
        (1, MIDDLE + 0): (
            (CORE, 1, D),
        ),
        (1, MIDDLE + 1): (
            (SEND, 1, D), (CORE, 1, U),
        ),
        (1, REST): (
            (SEND, 1, U), (CORE, 1, O),
        ),
        (1, RESULT + 1): (
            (SEND, 1, O), (CORE, 1, Q), (SEND, 1, Q), (ADD, 1, U, 1),
        ),
        (0, GRADS + 1): (
            (ADD, 1, U, 2), (ADD, 1, U, 0),
        ),
        (0, PRODUCT_UP): (
            (CORE, 0, D), (SEND, 0, D),
        ),
        (0, MIDDLE + 1): (
            (RELAY, 1, U), (ADD, 1, O, 0), (CORE, 0, U), (ADD, 1, U, 3), (SEND, 0, U),
        ),
        (0, MIDDLES + 0): (
            (RELAY, 0, D),
        ),
        (0, REST): (
            (CORE, 0, O), (ADD, 1, O, 2),
        ),
        (0, RESULT + 0): (
            (SEND, 0, O), (ADD, 0, O, 0),
        ),
        (0, RESULT + 1): (
            (RELAY, 1, O), (CORE, 0, Q),
        ),
        (0, ENDING + 0): (
            (SUM, 0, D), (ADD, 0, O, 2), (ADD, 0, O, 1), (RELAY, 0, O), (SEND, 0, Q),
        ),
        (0, ENDING + 2): (
            (ADD, 0, Q, 0), (ADD, 0, Q, 1), (SUM, 1, U), (ADD, 0, Q, 2), (ADD, 1, O, 3),
            (RELAY, 0, Q), (SUM, 0, O),
        ),
        (0, ENDING + 4): (
            (LAST, 1, D), (ADD, 1, O, 1), (SUM, 0, Q), (SUM, 1, O), (LAST, 1, Q),
        ),
    },
)


def slots_of(matrix, chips):
    slots = {}
    counts = [0, 0]
    for layer in range(2):
        path = SUMS[layer][matrix]
        slots[layer, layer] = counts[layer]
        counts[layer] += chips if path == VIA_OWN else 1
        if path == VIA_OTHER:
            slots[1 - layer, layer] = counts[1 - layer] - 1
            counts[1 - layer] += chips - 1
    return slots, max(counts)


def backward_kernel(
    chips,
    seq,
    sent_rows,
    cot,
    live,
    vec,
    out_all,
    hs_in,
    mid_in,
    gq_in,
    go_in,
    gu_in,
    gd_in,
    n1_in,
    n2_in,
    joined_in,
    mixed_in,
    pre_in,
    vec_out,
    outq,
    outo,
    outu,
    outd,
    gin_both,
    out_both,
    rcq,
    rco,
    rcu,
    rcd,
    rzq,
    rzo,
    rzu,
    rzd,
    gin,
    gvec,
    wb,
    wu,
    before,
    normed,
    joined,
    mixed,
    pre,
    hidden,
    grad_all,
    mid_all,
    received,
    sending,
    own_part,
    grad_mixed,
    grad_joined,
    aq,
    ao,
    au,
    ad,
    rxq,
    rxo,
    rxu,
    rxd,
    tile,
    fetched,
    single,
    cut,
    vc,
    vy,
    vz,
    vx,
    y_send,
    y_recv,
    loads,
    cs,
    cl,
    cr,
    xs,
    xr,
    zs,
    zr,
    fetch_sem,
    single_sem,
    v_send,
    v_recv,
    g_send,
    g_recv,
    g_own,
):
    here = Place(chips)
    s, c, z = here.s, here.c, here.z
    rows, depth = cot.shape
    width = mixed.shape[2]
    width_ff = wu.shape[1]
    tail = rows - sent_rows
    parts = parts_of(rows)
    mine = (aq, ao, au, ad)
    from_core = (rcq, rco, rcu, rcd)
    from_x = (rxq, rxo, rxu, rxd)
    x_slots = [slots_of(matrix, chips)[0] for matrix in range(4)]
    from_z = (rzq, rzo, rzu, rzd)
    outs = (outq, outo, outu, outd)
    block = outo.shape[0]
    small = 24 if block % 24 == 0 else block
    for buffer in (grad_all, mid_all):
        buffer[1, sent_rows:rows, :] = jnp.zeros((tail, depth), F32)
    for index in range(received.shape[0]):
        received[index, sent_rows:rows, :] = jnp.zeros((tail, depth), F32)
    gvec[...] = jnp.zeros(gvec.shape, F32)

    wq, wo = wb.at[:, 0 : 3 * width], wb.at[:, 3 * width : 4 * width]
    sources = dict(
        wd=(gd_in, wb),
        pre=(pre_in, pre),
        wu=(gu_in, wu),
        n2=(n2_in, normed),
        mid=(mid_in, before),
        joined=(joined_in, joined),
        mixed=(mixed_in, mixed),
        n1=(n1_in, normed),
        hs=(hs_in, before),
        wo=(go_in, wo),
        wq=(gq_in, wq),
    )
    order = list(sources)
    loading = {}

    def load(name, layer):
        src, dst = sources[name]
        copy = pltpu.make_async_copy(src.at[layer], dst, loads.at[order.index(name)])
        copy.start()
        loading[name] = copy

    def loaded(name):
        loading.pop(name).wait()

    for name in order[:-2]:
        if name not in ("hs", "n1"):
            load(name, 1)
    cot_copy = pltpu.make_async_copy(cot, own_part, loads.at[len(order)])
    cot_copy.start()
    here.greet()
    departing = []

    def launch(copy):
        copy.start()
        departing.append(copy)
        return copy

    def departed(copy):
        copy.wait_send()
        departing[:] = [item for item in departing if item is not copy]

    exchanges = {}

    def y_start(src, dst, index, part):
        start, stop = parts[part]
        span = pl.ds(start, min(stop, sent_rows) - start)
        copy = remote(
            src.at[span],
            dst.at[span],
            y_send.at[index, part],
            y_recv.at[index, part],
            here.y_peer,
        )
        copy.start()
        exchanges[index, part] = copy

    def y_wait(index, part):
        exchanges[index, part].wait_recv()

    def y_departed(index):
        for part in range(2):
            exchanges.pop((index, part)).wait_send()

    def gin_copy():
        return remote(
            gin.at[1 - s], gin_both.at[s], g_send.at[1], g_recv.at[1], here.x_peer
        )

    out_copy = launch(
        remote(
            out_all.at[1 - s], out_both.at[s], g_send.at[0], g_recv.at[0], here.x_peer
        )
    )
    own_out = pltpu.make_async_copy(out_all.at[s], out_both.at[s], g_own.at[0])
    own_out.start()


    def tile_copies(slot, matrix, layer, number, start, size, step):
        lanes = pl.ds(start, size)
        spots = []
        for core in (1 - c, c):
            first = pl.multiple_of((here.z_at(step) * 2 + core) * block, 8)
            spots.append(tile.at[slot, pl.ds(first, block), pl.ds(0, size)])
        return (
            remote(
                spots[0],
                from_core[matrix].at[layer, step, :, lanes],
                cs.at[slot, step],
                cr.at[layer, matrix, number, step],
                here.core_peer,
            ),
            pltpu.make_async_copy(
                spots[1], mine[matrix].at[layer, step, :, lanes], cl.at[slot, step]
            ),
        )

    in_slot = [[None, None], [None, None]]
    next_slot = [0]

    def settle(section, slot):
        what = in_slot[section][slot]
        if what is not None:
            in_slot[section][slot] = None

            @pl.loop(0, chips)
            def _(step):
                away, kept = tile_copies(slot, *what, step)
                away.wait_send()
                kept.wait()

    def settle_all(slot):
        if in_slot[0][slot] == in_slot[1][slot]:
            settle(0, slot)
            in_slot[1][slot] = None
        for section in range(2):
            if in_slot[section][slot] is not None:
                pl.when(s == section)(functools.partial(settle, section, slot))

    def tiles_of(matrix):
        size = width if matrix < 2 else depth
        return [(n, n * size, size) for n in range(mine[matrix].shape[3] // size)]

    def flat(ref):
        return ref[...].reshape(2 * rows, ref.shape[-1])

    def product(matrix, layer, left, right):
        both = flat(left)
        for number, start, size in tiles_of(matrix):
            slot = next_slot[0]
            next_slot[0] = 1 - slot
            settle_all(slot)
            piece = right[:, :, start : start + size].reshape(2 * rows, size)
            tile[slot, :, 0:size] = dot(both, piece, 0, 0)
            what = (matrix, layer, number, start, size)

            @pl.loop(0, chips)
            def _(step):
                away, kept = tile_copies(slot, *what, step)
                away.start()
                kept.start()

            in_slot[0][slot] = in_slot[1][slot] = what

    def fetch(slot, src):
        spot = single.at[slot, :, pl.ds(0, src.shape[1])]
        copy = pltpu.make_async_copy(src, spot, single_sem.at[slot])
        copy.start()
        return copy, spot

    def add_from(src, target):
        copy, spot = fetch(0, src)
        copy.wait()
        add_rows(target, [spot], small)

    def x_slot(matrix, layer, step):
        to_own = SUMS[layer][matrix] == VIA_OWN or (isinstance(step, int) and step == 0)
        section = layer if to_own else 1 - layer
        return x_slots[matrix][section, layer] + step

    def x_grad(matrix, layer, step):
        return remote(
            mine[matrix].at[layer, step],
            from_x[matrix].at[x_slot(matrix, layer, step)],
            xs.at[layer, matrix, step],
            xr.at[layer, matrix, step],
            here.x_peer,
        )

    def z_grad(matrix, layer, step):
        return remote(
            mine[matrix].at[layer, step],
            from_z[matrix].at[layer, step],
            zs.at[layer, matrix, step],
            zr.at[layer, matrix, step],
            here.z_peer(step),
        )

    def z_left(matrix, layer):
        far = here.departures()[0]
        return remote(
            mine[matrix].at[layer, far],
            from_z[matrix].at[layer, 0],
            zs.at[layer, matrix, far],
            zr.at[layer, matrix, 0],
            here.z_peer(4 - far),
        )

    def z_out(matrix, layer, number):
        step = here.departures()[number]
        if not here.relays:
            if step:
                z_grad(matrix, layer, step).start()
        elif number == 0:
            pl.when(here.middle)(z_grad(matrix, layer, step).start)
            pl.when(~here.middle)(z_left(matrix, layer).start)
        elif number == 1:
            z_grad(matrix, layer, step).start()
        elif number == 2:
            pl.when(~here.middle)(z_grad(matrix, layer, step).start)

    def core(section, layer, matrix):
        for slot in range(2):
            what = in_slot[section][slot]
            if what is not None and what[:2] == (matrix, layer):
                settle(section, slot)
        for what in tiles_of(matrix):

            @pl.loop(0, chips)
            def _(step):
                tile_copies(0, matrix, layer, *what, step)[0].wait_recv()

        lanes = pl.ds(0, mine[matrix].shape[3])
        pltpu.make_async_copy(
            from_core[matrix].at[layer], fetched.at[:, :, lanes], fetch_sem
        ).start()

    def send(section, layer, matrix):
        lanes = pl.ds(0, mine[matrix].shape[3])
        pltpu.make_async_copy(
            from_core[matrix].at[layer], fetched.at[:, :, lanes], fetch_sem
        ).wait()
        path = SUMS[layer][matrix]
        for number, step in enumerate(here.departures()):
            add_rows(mine[matrix].at[layer, step], [fetched.at[step, :, lanes]], small)
            if path == BOTH:
                z_out(matrix, layer, number)
            elif path == VIA_OWN and section != layer:
                x_grad(matrix, layer, step).start()
            elif path == VIA_OTHER and section == layer and number < chips - 1:
                x_grad(matrix, layer, step).start()

    def add(section, layer, matrix, group):
        steps = here.departures()
        count, groups = (chips, 4) if section == layer else (chips - 1, 3)
        for number in range(count * group // groups, count * (group + 1) // groups):
            step = steps[number]
            x_grad(matrix, layer, step).wait_recv()
            block_in = from_x[matrix].at[x_slot(matrix, layer, step)]
            add_rows(mine[matrix].at[layer, step], [block_in], small)
            z_out(matrix, layer, number)

    def relay(section, layer, matrix):
        if here.relays:

            @pl.when(here.middle)
            def _():
                z_left(matrix, layer).wait_recv()
                add_from(from_z[matrix].at[layer, 0], mine[matrix].at[layer, 2])
                z_grad(matrix, layer, 2).start()

    def sum_z(section, layer, matrix):
        target = mine[matrix].at[layer, 0]

        def several(steps):
            fetched_now = []
            for slot, step in enumerate(steps):
                z_grad(matrix, layer, step).wait_recv()
                fetched_now.append(fetch(slot, from_z[matrix].at[layer, step]))
            for copy, _ in fetched_now:
                copy.wait()
            add_rows(target, [spot for _, spot in fetched_now], small)

        steps = here.departures()[:-1]
        if here.relays:
            pl.when(here.middle)(lambda: several([steps[0], 2, steps[1]]))
            pl.when(~here.middle)(lambda: several([steps[0], 2]))
        else:
            for step in steps:
                several([step])
        if section != layer:
            x_grad(matrix, layer, 0).start()

    def last(section, layer, matrix):
        x_grad(matrix, layer, 0).wait_recv()
        block_in = from_x[matrix].at[x_slot(matrix, layer, 0)]
        add_rows(mine[matrix].at[layer, 0], [block_in], small)

    actions = (core, send, add, relay, sum_z, last)

    def act(section, events):
        for name, layer, matrix, *more in events:
            actions[name](section, layer, matrix, *more)

    def point(layer, name):
        for section in range(2):
            events = SUM_UP[section].get((layer, name))
            if events:
                pl.when(s == section)(functools.partial(act, section, events))

    def total(value):
        return jnp.sum(value, 0, keepdims=True)

    def note(layer, row, value):
        gvec[layer, row : row + 1, :] = gvec[layer, row : row + 1, :] + total(value)

    def begin(layer, part, value):
        span = slice(*parts[part])
        grad_all[0, span] = value
        y_start(grad_all.at[0], grad_all.at[1], 4 * (1 - layer), part)
        note(layer, 5, value)

    def contract(layer, image, span):
        for piece in range(width_ff // depth):
            lanes = slice(piece * depth, (piece + 1) * depth)
            grad_hidden = dot(grad_all[image, span], wb[:, lanes], 1, 0)
            value = pre[image, span, lanes]
            upper = phi_big(value)
            hidden[image, span, lanes] = value * upper
            pre[image, span, lanes] = grad_hidden * (upper + value * phi_small(value))

    everything = slice(0, rows)
    cot_copy.wait()
    for part in range(2):
        span = slice(*parts[part])
        begin(1, part, own_part[span] * live[span, 0:1])
    for layer in (1, 0):
        vectors = Vectors(vec.at[layer], width, None)
        base = 4 * (1 - layer)
        point(layer, LAYER)
        loaded("wd")
        loaded("pre")
        contract(layer, 0, everything)
        loaded("wu")
        own_part[...] = dot(pre[0], wu[...], 1, 1)
        if layer == 0:
            y_departed(3)
        for part in range(2):
            span = slice(*parts[part])
            point(layer, GRADS + part)
            y_wait(base, part)
            contract(layer, 1, span)
            sending[span] = dot(pre[1, span], wu[...], 1, 1)
            y_start(sending, received.at[0], base + 1, part)
        load("wo", layer)
        load("wq", layer)
        if layer == 1:
            load("wu", 0)
        point(layer, PRODUCTS)
        product(D, layer, grad_all, hidden)
        point(layer, PRODUCT_UP)
        loaded("n2")
        product(U, layer, normed, pre)
        load("n1", layer)
        for piece in range(width_ff // depth):
            lanes = slice(piece * depth, (piece + 1) * depth)
            note(layer, 9 + piece, pre[0, :, lanes])
            note(layer, 9 + piece, pre[1, :, lanes])
        if layer == 1:
            load("pre", 0)
        loaded("mid")
        if layer == 0:
            y_departed(2)
        for part in range(2):
            span = slice(*parts[part])
            point(layer, MIDDLE + part)
            unit, inverse = normalize(before[span])
            y_wait(base + 1, part)
            grad_second = own_part[span] + received[0, span]
            grad_middle = grad_all[0, span] + normalize_back(
                grad_second * vectors.gain(1), unit, inverse
            )
            mid_all[0, span] = grad_middle
            y_start(mid_all.at[0], mid_all.at[1], base + 2, part)
            note(layer, 1, grad_second * unit)
            note(layer, 3, grad_second)
            note(layer, 4, grad_middle)
        load("hs", layer)
        point(layer, HEADS)
        loaded("wo")
        loaded("joined")
        loaded("mixed")
        grad_mixed[...] = dot(mid_all[0], wo[...], 1, 0)
        attend_back(joined.at[0], mixed.at[0], grad_mixed, grad_joined.at[0], seq)
        loaded("wq")
        own_part[...] = dot(grad_joined[0], wq[...], 1, 1)
        for part in range(2):
            span = slice(*parts[part])
            point(layer, MIDDLES + part)
            y_wait(base + 2, part)
            grad_mixed[span] = dot(mid_all[1, span], wo[...], 1, 0)
        attend_back(joined.at[1], mixed.at[1], grad_mixed, grad_joined.at[1], seq)
        y_departed(base + 1)
        for part in range(2):
            span = slice(*parts[part])
            sending[span] = dot(grad_joined[1, span], wq[...], 1, 1)
            y_start(sending, received.at[1], base + 3, part)
        if layer == 1:
            load("wd", 0)
            load("joined", 0)
        point(layer, PRODUCT_OUT)
        product(O, layer, mid_all, mixed)
        loaded("n1")
        product(Q, layer, normed, grad_joined)
        if layer == 1:
            load("mixed", 0)
            load("n2", 0)
        for image in range(2):
            for piece in (0, 2):
                lanes = slice(piece * width, (piece + 1) * width)
                spot = slice(piece // 2 * width, (piece // 2 + 1) * width)
                gvec[layer, 8:9, spot] = gvec[layer, 8:9, spot] + total(
                    grad_joined[image, :, lanes]
                )
        point(layer, REST)
        loaded("hs")
        if layer == 1:
            y_departed(0)
        for part in range(2):
            span = slice(*parts[part])
            point(layer, RESULT + part)
            unit, inverse = normalize(before[span])
            y_wait(base + 3, part)
            grad_first = own_part[span] + received[1, span]
            value = mid_all[0, span] + normalize_back(
                grad_first * vectors.gain(0), unit, inverse
            )
            gin[layer, span] = value
            if layer == 1:
                begin(0, part, value * live[span, 0:1])
            note(layer, 0, grad_first * unit)
            note(layer, 2, grad_first)
        if layer == 1:
            load("mid", 0)
            pl.when(s == 0)(gin_copy().start)
    for layer in range(2):

        def write(tensor, core, chip, upper, lower):
            step = (chip + chips - z) % chips
            cut[tensor, core, layer, step, 0:8] = upper
            cut[tensor, core, layer, step, 8:16] = lower

        cut_vectors(gvec.at[layer], depth // (4 * chips), chips, here.t, write)
    copy = launch(
        remote(cut.at[:, 1 - c], vc, v_send.at[0], v_recv.at[0], here.core_peer)
    )
    point(0, ENDING + 0)
    copy.wait_recv()
    point(0, ENDING + 1)
    cut[:, c] = cut[:, c] + vc[...]
    copy = launch(
        remote(cut.at[1 - here.t, c], vy, v_send.at[1], v_recv.at[1], here.y_peer)
    )
    point(0, ENDING + 2)
    copy.wait_recv()
    cut[here.t, c] = cut[here.t, c] + vy[...]
    copy = launch(
        remote(
            cut.at[here.t, c, 1 - s],
            vx,
            v_send.at[chips + 1],
            v_recv.at[chips + 1],
            here.x_peer,
        )
    )
    pl.when(s == 1)(gin_copy().start)
    point(0, ENDING + 3)
    copy.wait_recv()
    cut[here.t, c, s] = cut[here.t, c, s] + vx[...]
    copies = []
    for step in range(1, chips):
        copies.append(
            launch(
                remote(
                    cut.at[here.t, c, s, step],
                    vz.at[step - 1],
                    v_send.at[1 + step],
                    v_recv.at[1 + step],
                    here.z_peer(step),
                )
            )
        )
    point(0, ENDING + 4)
    for section in range(2):

        @pl.when(s == section)
        def _():
            for part in range(3):
                lanes = slice(part * width, (part + 1) * width)
                outq[part] = mine[Q][section, 0, :, lanes]
            for matrix in (O, U, D):
                outs[matrix][...] = mine[matrix][section, 0]

    total_vec = cut[here.t, c, s, 0]
    for step in range(1, chips):
        copies[step - 1].wait_recv()
        total_vec = total_vec + vz[step - 1]
    vec_out[...] = total_vec
    for slot in range(2):
        settle_all(slot)
    own_gin = pltpu.make_async_copy(gin.at[s], gin_both.at[s], g_own.at[1])
    own_gin.start()
    out_copy.wait_recv()
    gin_copy().wait()
    own_out.wait()
    own_gin.wait()
    for item in departing:
        item.wait_send()
    for item in exchanges.values():
        item.wait_send()

    def departures(section):
        for layer in range(2):
            own = section == layer
            for matrix in range(4):
                path = SUMS[layer][matrix]
                if path != (VIA_OTHER if own else VIA_OWN):
                    for step in here.departures()[:-1]:
                        z_grad(matrix, layer, step).wait_send()
                    if not own:
                        x_grad(matrix, layer, 0).wait_send()
                elif own:
                    for step in range(1, chips):
                        x_grad(matrix, layer, step).wait_send()
                else:
                    for step in range(chips):
                        x_grad(matrix, layer, step).wait_send()

    for section in range(2):
        pl.when(s == section)(functools.partial(departures, section))


def backward(chips, seq, cot, live, vec, out_all, hs, mid, whole, kept):
    rows, depth = cot.shape
    sent_rows = up_to(seq, 8)
    width, width_ff = whole[1].shape[2], whole[2].shape[2]
    widths = [w.shape[2] for w in whole]
    block = depth // (2 * chips)
    any_space = pl.BlockSpec(memory_space=pl.ANY)
    vmem = pl.BlockSpec(memory_space=pltpu.VMEM)
    outs = [
        ((16, 128), vmem),
        ((3, block, width), vmem),
        *[((block, w), vmem) for w in widths[1:]],
        ((2, rows, depth), any_space),
        ((2, rows, depth), any_space),
        *[((2, chips, block, w), any_space) for w in widths * 2],
    ]
    sems = pltpu.SemaphoreType.DMA
    scratch = [
        pltpu.VMEM((2, rows, depth), F32),
        pltpu.VMEM(vec.shape, F32),
        pltpu.VMEM((depth, width_ff), F32),
        pltpu.VMEM((depth, width_ff), F32),
        pltpu.VMEM((rows, depth), F32),
        pltpu.VMEM((2, rows, depth), F32),
        pltpu.VMEM((2, rows, 3 * width), F32),
        pltpu.VMEM((2, rows, width), F32),
        pltpu.VMEM((2, rows, width_ff), F32),
        pltpu.VMEM((2, rows, width_ff), F32),
        *[pltpu.VMEM((2, rows, depth), F32) for _ in range(3)],
        pltpu.VMEM((rows, depth), F32),
        pltpu.VMEM((rows, depth), F32),
        pltpu.VMEM((rows, width), F32),
        pltpu.VMEM((2, rows, 3 * width), F32),
        *[pltpu.VMEM((2, chips, block, w), F32) for w in widths],
        *[
            pltpu.VMEM((slots_of(matrix, chips)[1], block, w), F32)
            for matrix, w in enumerate(widths)
        ],
        pltpu.VMEM((2, depth, depth), F32),
        pltpu.VMEM((chips, block, width_ff), F32),
        pltpu.VMEM((3, block, width_ff), F32),
        pltpu.VMEM((2, 2, 2, chips, 16, 128), F32),
        pltpu.VMEM((2, 2, chips, 16, 128), F32),
        pltpu.VMEM((2, chips, 16, 128), F32),
        pltpu.VMEM((chips - 1, 16, 128), F32),
        pltpu.VMEM((chips, 16, 128), F32),
        sems((8, 2)),
        sems((8, 2)),
        sems((12,)),
        sems((2, chips)),
        sems((2, chips)),
        sems((2, 4, 3, chips)),
        *[sems((2, 4, chips)) for _ in range(4)],
        sems,
        sems((3,)),
        sems((chips + 2,)),
        sems((chips + 2,)),
        sems((2,)),
        sems((2,)),
        sems((2,)),
    ]
    results = pl.pallas_call(
        functools.partial(backward_kernel, chips, seq, sent_rows),
        out_shape=[jax.ShapeDtypeStruct(shape, F32) for shape, _ in outs],
        in_specs=[any_space] + [vmem] * 2 + [any_space] * 12,
        out_specs=[spec for _, spec in outs],
        scratch_shapes=scratch,
        compiler_params=pltpu.CompilerParams(
            collective_id=1, has_side_effects=True, vmem_limit_bytes=VMEM_BYTES
        ),
        name="backward_both",
    )(cot, live, vec, out_all, hs, mid, *whole, *kept)
    return results[:7]


def body(
    embedded,
    image_counts,
    cotangent,
    qkv_weight,
    qv_bias,
    out_weight,
    up_weight,
    up_bias,
    down_weight,
    norm_gains,
    shift_terms,
):
    groups = lax.axis_size("dp")
    chips = groups // 2
    tensors = lax.axis_size("tensor")
    s = lax.axis_index("section")
    t = lax.axis_index("tensor")
    seq = embedded.shape[3]
    rows = up_to(seq, 16)

    def padded(value):
        chosen = lax.dynamic_index_in_dim(value[:, 0, 0], s, 0, keepdims=False)
        return jnp.pad(chosen, ((0, rows - seq), (0, 0)))

    slot = s * tensors + t
    alive = (slot < image_counts[0]).astype(F32)
    inside = lax.broadcasted_iota(jnp.int32, (rows, 128), 0) < seq
    live = jnp.where(inside, alive, 0.0)

    pieces = [norm_gains[0], shift_terms[0], qv_bias[0], up_bias.reshape(4, -1)]
    packed = jnp.concatenate(pieces)
    packed = jnp.pad(packed, ((0, 16 - packed.shape[0]), (0, 128 - packed.shape[1])))

    shards = (
        qkv_weight[0].transpose(1, 0, 2),
        out_weight[0].T,
        up_weight[0],
        down_weight[0].T,
    )
    out_all, vec, hs, mid, gq, go, gu, gd, *kept = forward(
        chips, seq, padded(embedded), live, packed, *shards
    )
    vec_sum, sum_q, sum_o, sum_u, sum_d, gin_both, out_both = backward(
        chips,
        seq,
        padded(cotangent),
        live,
        vec,
        out_all,
        hs,
        mid,
        (gq, go, gu, gd),
        kept,
    )
    piece = norm_gains.shape[2]
    return (
        out_both[None, :, None, None, :seq],
        gin_both[None, :, None, None, :seq],
        sum_q.transpose(1, 0, 2)[None],
        vec_sum[None, 6:8, :piece],
        sum_o.T[None],
        sum_u[None],
        vec_sum[8:12, :piece].reshape(1, 4 * piece),
        sum_d.T[None],
        vec_sum[None, 0:2, :piece],
        vec_sum[None, 2:6, :piece],
    )


def solution(mesh):
    placed = (
        P(None, "dp", "tensor", None, None),
        P("dp"),
        P(None, "dp", "tensor", None, None),
        P("section", "dp", None, "tensor"),
        P("section", None, ("tensor", "dp")),
        P("section", "tensor", "dp"),
        P("section", "dp", "tensor"),
        P("section", ("tensor", "dp")),
        P("section", "tensor", "dp"),
        P("section", None, ("tensor", "dp")),
        P("section", None, ("tensor", "dp")),
    )
    return jax.shard_map(
        body,
        mesh=mesh,
        in_specs=placed,
        out_specs=(
            P("section", None, "dp", "tensor", None, None),
            P("section", None, "dp", "tensor", None, None),
            P("section", "dp", None, "tensor"),
            P("section", None, ("tensor", "dp")),
            P("section", "tensor", "dp"),
            P("section", "dp", "tensor"),
            P("section", ("tensor", "dp")),
            P("section", "tensor", "dp"),
            P("section", None, ("tensor", "dp")),
            P("section", None, ("tensor", "dp")),
        ),
        check_vma=False,
    )
```

```python
import functools

import jax
import jax.numpy as jnp
from jax import lax
from jax.experimental import pallas as pl
from jax.experimental.pallas import tpu as pltpu
from jax.sharding import PartitionSpec as P

HD = 64
SCALE = HD ** (-0.5)
EPS = 1e-06
HIGH = lax.Precision.HIGH
MESH = pl.DeviceIdType.MESH
VMEM_BYTES = 63 * 2**20
F32 = jnp.float32


def dot(left, right, left_dim, right_dim):
    return lax.dot_general(
        left,
        right,
        (((left_dim,), (right_dim,)), ((), ())),
        precision=HIGH,
        preferred_element_type=F32,
    )


def up_to(count, step):
    return -(-count // step) * step


def normalize(value):
    centred = value - jnp.mean(value, -1, keepdims=True)
    inverse = lax.rsqrt(jnp.mean(centred * centred, -1, keepdims=True) + EPS)
    return centred * inverse, inverse


def normalize_back(grad_unit, unit, inverse):
    return inverse * (
        grad_unit
        - jnp.mean(grad_unit, -1, keepdims=True)
        - unit * jnp.mean(grad_unit * unit, -1, keepdims=True)
    )


class Place:
    def __init__(self, chips):
        self.s = lax.axis_index("section")
        self.t = lax.axis_index("tensor")
        d = lax.axis_index("dp")
        self.chips = chips
        self.z = d // 2
        self.c = d % 2
        self.x_peer = (1 - self.s, self.t, d)
        self.y_peer = (self.s, 1 - self.t, d)
        self.core_peer = (self.s, self.t, self.z * 2 + 1 - self.c)

    def z_at(self, step):
        return (self.z + self.chips + step) % self.chips

    def z_peer(self, step):
        return (self.s, self.t, self.z_at(step) * 2 + self.c)

    def greet(self):
        barrier = pltpu.get_barrier_semaphore()
        peers = [self.x_peer, self.y_peer, self.core_peer]
        peers += [self.z_peer(step) for step in range(1, self.chips)]
        for peer in peers:
            pl.semaphore_signal(barrier, inc=1, device_id=peer, device_id_type=MESH)
        pl.semaphore_wait(barrier, len(peers))


    @property
    def relays(self):
        return self.chips == 4

    def arrivals(self):
        if not self.relays:
            return list(range(1, self.chips))
        near = jnp.where(self.z < 2, 3, 1)
        return [2, near, 4 - near]

    def departures(self):
        if not self.relays:
            return list(range(1, self.chips)) + [0]
        far = jnp.where(self.z < 2, 3, 1)
        return [far, 4 - far, 2, 0]

    @property
    def middle(self):
        return (self.z == 1) | (self.z == 2)

    def direct(self, step):
        if not self.relays or step == 2:
            return None
        return self.z <= 2 if step == 1 else self.z >= 1


def when(condition, action):
    if condition is None:
        action()
    else:
        pl.when(condition)(action)


def parts_of(rows):
    first = up_to(rows // 2, 8)
    return [(0, first), (first, rows)]


def remote(src, dst, send, recv, peer):
    return pltpu.make_async_remote_copy(
        src_ref=src,
        dst_ref=dst,
        send_sem=send,
        recv_sem=recv,
        device_id=peer,
        device_id_type=MESH,
    )


def key_mask(rows, seq):
    return lax.broadcasted_iota(jnp.int32, (rows, rows), 1) < seq


def head_lanes(which):
    return lax.broadcasted_iota(jnp.int32, (1, 2 * HD), 1) // HD == which


def attend(joined, mixed, seq):
    rows, width = mixed.shape
    keep = key_mask(rows, seq)
    for pair in range(width // (2 * HD)):
        lanes = slice(pair * 2 * HD, (pair + 1) * 2 * HD)
        query = joined[:, lanes] * SCALE
        keys = joined[:, width + lanes.start : width + lanes.stop]
        values = joined[:, 2 * width + lanes.start : 2 * width + lanes.stop]
        total = None
        for which in range(2):
            own = head_lanes(which)
            scores = dot(query, jnp.where(own, keys, 0.0), 1, 1)
            scores = jnp.where(keep, scores, -3e38)
            weights = jnp.exp(scores - jnp.max(scores, -1, keepdims=True))
            probs = weights / jnp.sum(weights, -1, keepdims=True)
            part = dot(probs, jnp.where(own, values, 0.0), 1, 0)
            total = part if total is None else total + part
        mixed[:, lanes] = total


def attend_back(joined, mixed, grad_mixed, grad_joined, seq):
    rows, width = mixed.shape
    keep = key_mask(rows, seq)
    for pair in range(width // (2 * HD)):
        lanes = slice(pair * 2 * HD, (pair + 1) * 2 * HD)
        query = joined[:, lanes] * SCALE
        keys = joined[:, width + lanes.start : width + lanes.stop]
        values = joined[:, 2 * width + lanes.start : 2 * width + lanes.stop]
        grad = grad_mixed[:, lanes]
        product = grad * mixed[:, lanes]
        grads = [None, None, None]
        for which in range(2):
            own = head_lanes(which)
            own_keys = jnp.where(own, keys, 0.0)
            scores = dot(query, own_keys, 1, 1)
            scores = jnp.where(keep, scores, -3e38)
            weights = jnp.exp(scores - jnp.max(scores, -1, keepdims=True))
            probs = weights / jnp.sum(weights, -1, keepdims=True)
            own_grad = jnp.where(own, grad, 0.0)
            row_dot = jnp.sum(jnp.where(own, product, 0.0), -1, keepdims=True)
            grad_probs = dot(grad, jnp.where(own, values, 0.0), 1, 1)
            grad_scores = probs * (grad_probs - row_dot)
            parts = (
                dot(grad_scores, own_keys, 1, 0) * SCALE,
                dot(grad_scores, jnp.where(own, query, 0.0), 0, 0),
                dot(probs, own_grad, 0, 0),
            )
            grads = [b if a is None else a + b for a, b in zip(grads, parts)]
        for number, part in enumerate(grads):
            start = number * width + lanes.start
            grad_joined[:, start : start + 2 * HD] = part


def phi_big(value):
    return 0.5 * (1.0 + lax.erf(value * 0.7071067811865476))


def phi_small(value):
    return jnp.exp(-0.5 * value * value) * 0.3989422804014327


class Vectors:
    def __init__(self, ref, width, hidden):
        self.ref, self.width, self.hidden = ref, width, hidden

    def gain(self, which):
        return self.ref[which : which + 1, :]

    def shift(self, which):
        return self.ref[2 + which : 3 + which, :]

    def query(self):
        return self.ref[8:9, 0 : self.width]

    def value(self):
        return self.ref[8:9, self.width : 2 * self.width]

    def up(self, row):
        return self.ref[9 + row : 10 + row, :]


def place(tile, start, piece, lanes):
    lane = lax.broadcasted_iota(jnp.int32, tile.shape, 1)
    tile = jnp.where(lane < piece, tile, 0.0)
    first, shift = divmod(start, 128)
    if shift == 0:
        return {first: tile}
    turned = pltpu.roll(tile, shift, 1)
    if shift + piece <= 128:
        return {first: turned}
    return {
        first: jnp.where(lane >= shift, turned, 0.0),
        first + 1: jnp.where(lane < shift, turned, 0.0),
    }


def take(read, start, piece):
    first, shift = divmod(start, 128)
    tile = read(first)
    lane = lax.broadcasted_iota(jnp.int32, tile.shape, 1)
    if shift:
        tile = pltpu.roll(tile, 128 - shift, 1)
        if shift + piece > 128:
            after = pltpu.roll(read(first + 1), 128 - shift, 1)
            tile = jnp.where(lane < 128 - shift, tile, after)
    return jnp.where(lane < piece, tile, 0.0)


def spread_vectors(target, pieces, piece, chips, own):
    depth = target.shape[1]
    width = depth // 2
    tiles = [{} for _ in range(3)]

    def gather(kind, found, rows):
        for index, value in found.items():
            value = jnp.where(rows, value, 0.0)
            old = tiles[kind].get(index)
            tiles[kind][index] = value if old is None else old + value

    row = lax.broadcasted_iota(jnp.int32, (8, 128), 0)
    for chip in range(chips):
        for core in range(2):
            number = chip * 2 + core
            for tensor in range(2):
                tile = pieces(tensor, core, chip)[0:8]
                start = (tensor * 2 * chips + number) * piece
                gather(0, place(tile, start, piece, depth), row < 6)
            tile = pieces(own, core, chip)
            for part in range(2):
                found = place(tile[0:8], part * width + number * piece, piece, depth)
                gather(1, found, row == 6 + part)
            for part in range(4):
                found = place(tile[8:16], (number * 4 + part) * piece, piece, depth)
                gather(2, found, row == part)
    for index in range(depth // 128):
        lanes = slice(index * 128, (index + 1) * 128)
        target[0:8, lanes] = tiles[0][index]
        target[8:9, lanes] = jnp.sum(tiles[1][index], 0, keepdims=True)
        for up in range(2):
            value = tiles[2][up * (depth // 128) + index]
            target[9 + up : 10 + up, lanes] = jnp.sum(value, 0, keepdims=True)


def cut_vectors(source, piece, chips, own, write):
    depth = source.shape[1]
    width = depth // 2
    row = lax.broadcasted_iota(jnp.int32, (8, 128), 0)
    for chip in range(chips):
        for core in range(2):
            number = chip * 2 + core
            upper = jnp.zeros((8, 128), F32)
            for part in range(2):
                start = part * width + number * piece
                found = take(lambda n: source[8:9, n * 128 : n * 128 + 128], start, piece)
                upper = jnp.where(row == 6 + part, found, upper)
            lower = jnp.zeros((8, 128), F32)
            for part in range(4):
                up, start = divmod((number * 4 + part) * piece, depth)
                found = take(
                    lambda n: source[9 + up : 10 + up, n * 128 : n * 128 + 128], start, piece
                )
                lower = jnp.where(row == part, found, lower)
            for tensor in range(2):
                start = (tensor * 2 * chips + number) * piece
                wide = take(lambda n: source[0:8, n * 128 : n * 128 + 128], start, piece)
                mine = jnp.where(own == tensor, 1.0, 0.0)
                write(
                    tensor,
                    core,
                    chip,
                    jnp.where(row < 6, wide, upper * mine),
                    lower * mine,
                )


def add_rows(target, sources, step):
    rows = target.shape[0]

    @pl.loop(0, rows // step)
    def _(index):
        here = pl.ds(pl.multiple_of(index * step, 8), step)
        total = target[here, :]
        for source in sources:
            total = total + source[here, :]
        target[here, :] = total


Q, O, U, D = range(4)

VIA_OWN, BOTH, VIA_OTHER = range(3)

(START, LAYER, MIXED, TOKENS, MIDDLE, SECOND, SECONDS, HIDDEN, RESULT) = range(0, 72, 8)
(GRADS, PRODUCTS, PRODUCT_UP, HEADS, MIDDLES, PRODUCT_OUT, REST, ENDING) = range(72, 136, 8)

OWN, SPREAD, OVER_Z, OVER_X = range(4)
CORE, SEND, ADD, RELAY, SUM, LAST = range(6)
GATHER = (
    (VIA_OWN, VIA_OWN, VIA_OTHER, VIA_OWN),
    (VIA_OWN, VIA_OWN, VIA_OTHER, VIA_OWN),
)

PASS_ON = (
    {
        (0, START): (
            (OWN, 0, U), (OWN, 0, D), (OWN, 0, O), (OWN, 0, Q), (SPREAD, 0, Q),
            (OVER_Z, 0, Q, 0), (SPREAD, 0, O), (OVER_Z, 0, O, 0), (OVER_Z, 0, Q, 2),
        ),
        (0, LAYER): (
            (OVER_Z, 0, Q, 1), (OVER_Z, 0, O, 1), (SPREAD, 0, D), (OVER_Z, 0, O, 2),
        ),
        (0, MIDDLE + 0): (
            (OVER_Z, 0, D, 0), (OVER_X, 1, Q, 1), (OVER_X, 0, U, 0), (OVER_X, 1, O, -1),
            (OVER_X, 1, Q, 0), (OVER_Z, 0, D, 1), (OVER_Z, 0, D, 2),
        ),
        (0, MIDDLE + 1): (
            (OVER_X, 1, Q, -1), (OVER_X, 0, U, 2), (OVER_X, 1, U, -1),
        ),
        (0, SECOND): (
            (OVER_X, 0, U, 1),
        ),
        (0, RESULT + 0): (
            (OVER_Z, 1, U, 0), (OVER_X, 1, O, 1), (OVER_X, 1, O, 0), (OVER_X, 1, O, 2),
        ),
        (1, LAYER): (
            (OVER_X, 1, Q, 2),
        ),
        (1, TOKENS + 0): (
            (OVER_Z, 1, U, 2),
        ),
        (1, TOKENS + 1): (
            (OVER_X, 1, D, -1),
        ),
        (1, MIDDLE + 0): (
            (OVER_Z, 1, U, 1), (OVER_X, 1, D, 2),
        ),
        (1, HIDDEN): (
            (OVER_X, 1, D, 1), (OVER_X, 1, D, 0),
        ),
    },
    {
        (0, START): (
            (SPREAD, 1, Q), (OWN, 1, D), (OWN, 1, U), (OVER_X, 0, U, -1),
            (OVER_Z, 1, Q, 0), (SPREAD, 1, O), (OVER_Z, 1, Q, 1), (OWN, 1, Q),
        ),
        (0, LAYER): (
            (OVER_Z, 0, U, 0), (OVER_X, 0, O, -1), (OVER_X, 0, Q, 2), (OVER_Z, 0, U, 2),
            (SPREAD, 1, D), (OVER_X, 0, Q, 1), (OWN, 1, O), (OVER_X, 0, Q, -1),
            (OVER_X, 0, Q, 0), (OVER_X, 0, O, 1), (OVER_X, 0, O, 0), (OVER_X, 0, D, -1),
            (OVER_Z, 0, U, 1), (OVER_X, 0, O, 2),
        ),
        (0, MIDDLE + 1): (
            (OVER_Z, 1, O, 1),
        ),
        (0, SECOND): (
            (OVER_Z, 1, O, 0), (OVER_Z, 1, Q, 2),
        ),
        (0, SECONDS + 1): (
            (OVER_X, 0, D, 1), (OVER_X, 0, D, 0), (OVER_Z, 1, O, 2), (OVER_Z, 1, D, 0),
            (OVER_X, 0, D, 2),
        ),
        (0, RESULT + 0): (
            (OVER_Z, 1, D, 2),
        ),
        (1, MIXED): (
            (OVER_X, 1, U, 0),
        ),
        (1, TOKENS + 0): (
            (OVER_Z, 1, D, 1),
        ),
        (1, MIDDLE + 0): (
            (OVER_X, 1, U, 1), (OVER_X, 1, U, 2),
        ),
    },
)


def forward_kernel(
    chips,
    seq,
    sent_rows,
    x_in,
    live,
    vec_in,
    wq,
    wo,
    wu,
    wd,
    out_all,
    vec,
    hs,
    mid,
    gq_out,
    go_out,
    gu_out,
    gd_out,
    n1_out,
    n2_out,
    joined_out,
    mixed_out,
    pre_out,
    gq,
    go,
    gu,
    gd,
    n1,
    n2,
    joined,
    mixed,
    pre,
    hidden,
    received,
    sending,
    pieces,
    y_send,
    y_recv,
    v_send,
    v_recv,
    zs,
    zr,
    xs,
    xr,
    cs,
    cr,
    local,
    save,
):
    here = Place(chips)
    s, c, z = here.s, here.c, here.z
    shards = (wq, wo, wu, wd)
    whole = (gq, go, gu, gd)
    block = wo.shape[0]
    rows, depth = x_in.shape
    width = go.shape[2]
    tail = rows - sent_rows
    parts = parts_of(rows)
    for buffer in (n1, n2):
        for layer in range(2):
            buffer[layer, 1, sent_rows:rows, :] = jnp.zeros((tail, depth), F32)
    for index in range(received.shape[0]):
        received[index, sent_rows:rows, :] = jnp.zeros((tail, depth), F32)
    here.greet()


    def spot(matrix, layer, back, core=None):
        start = (here.z_at(-back) * 2 + (c if core is None else core)) * block
        span = pl.ds(pl.multiple_of(start, 8), block)
        if matrix == Q:
            return whole[matrix].at[layer, :, span, :]
        return whole[matrix].at[layer, span, :]

    def z_copy(layer, matrix, step, src=None):
        place = spot(matrix, layer, 0)
        return remote(
            place if src is None else src,
            place,
            zs.at[layer, matrix, step],
            zr.at[layer, matrix, step],
            here.z_peer(step),
        )

    def z_relay(layer, matrix):
        place = spot(matrix, layer, 2)
        step = jnp.where(z == 1, 3, 1)
        return remote(
            place,
            place,
            zs.at[layer, matrix, 0],
            zr.at[layer, matrix, 4 - step],
            here.z_peer(step),
        )

    def x_copy(layer, matrix, back, src=None):
        place = spot(matrix, layer, back)
        return remote(
            place if src is None else src,
            place,
            xs.at[layer, matrix, back],
            xr.at[layer, matrix, back],
            here.x_peer,
        )

    def c_copy(layer, matrix, back, src=None):
        place = spot(matrix, layer, back)
        return remote(
            place if src is None else src,
            place,
            cs.at[layer, matrix, back],
            cr.at[layer, matrix, back],
            here.core_peer,
        )

    def landed(place, sem):
        pltpu.make_async_copy(place, place, sem).wait()

    def z_spread(layer, matrix, src=None):
        for step in [2, 1, 3] if here.relays else range(1, chips):
            when(here.direct(step), z_copy(layer, matrix, step, src).start)

    count = chips - 1

    def act(section, event):
        kind, layer, matrix, *third = event
        own = section == layer
        path = GATHER[layer][matrix]
        if kind == OWN:
            x_copy(layer, matrix, 0, shards[matrix]).start()
        elif kind == SPREAD:
            z_spread(layer, matrix, shards[matrix])
        elif third[0] < 0:
            landed(spot(matrix, layer, 0), xr.at[layer, matrix, 0])
            if path != VIA_OWN:
                z_spread(layer, matrix)
            c_copy(layer, matrix, 0).start()
        else:
            for number in range(count * third[0] // 3, count * (third[0] + 1) // 3):
                back = here.arrivals()[number]
                place = spot(matrix, layer, back)
                if kind == OVER_X:
                    landed(place, xr.at[layer, matrix, back])
                else:
                    landed(place, zr.at[layer, matrix, back])
                    if here.relays and number == 0:
                        pl.when(here.middle)(z_relay(layer, matrix).start)
                    if path == (VIA_OWN if own else VIA_OTHER):
                        x_copy(layer, matrix, back).start()
                c_copy(layer, matrix, back).start()

    def point(layer, name):
        for section in range(2):
            events = PASS_ON[section].get((layer, name))
            if events:

                @pl.when(s == section)
                def _():
                    for event in events:
                        act(section, event)

    piece = depth // (4 * chips)
    pieces[here.t, c, s, z] = vec_in[...]
    copy = remote(
        pieces.at[here.t, c, s, z],
        pieces.at[here.t, c, s, z],
        v_send.at[0],
        v_recv.at[0],
        here.x_peer,
    )
    copy.start()
    copy.wait_send()
    landed(pieces.at[here.t, c, 1 - s, z], v_recv.at[0])
    vector_copies = []
    for step in range(1, chips):
        place_ = pieces.at[here.t, c, :, z]
        copy = remote(
            place_, place_, v_send.at[step], v_recv.at[step], here.z_peer(step)
        )
        copy.start()
        vector_copies.append(copy)
    own_copies = []
    for matrix in range(4):
        c_copy(s, matrix, 0, shards[matrix]).start()
        copy = pltpu.make_async_copy(
            shards[matrix], spot(matrix, s, 0), local.at[matrix]
        )
        copy.start()
        own_copies.append(copy)
    point(0, START)
    for step in range(1, chips):
        vector_copies[step - 1].wait_send()
        landed(pieces.at[here.t, c, :, here.z_at(-step)], v_recv.at[step])
    place_ = pieces.at[here.t, c]
    copy = remote(place_, place_, v_send.at[chips], v_recv.at[chips], here.y_peer)
    copy.start()
    copy.wait_send()
    landed(pieces.at[1 - here.t, c], v_recv.at[chips])
    place_ = pieces.at[:, c]
    copy = remote(
        place_, place_, v_send.at[chips + 1], v_recv.at[chips + 1], here.core_peer
    )
    copy.start()
    copy.wait_send()
    landed(pieces.at[:, 1 - c], v_recv.at[chips + 1])
    for layer in range(2):
        spread_vectors(
            vec.at[layer],
            lambda tensor, core, chip: pieces[tensor, core, layer, chip],
            piece,
            chips,
            here.t,
        )

    saves = {}

    def keep(name, src, dst, sem):
        copy = pltpu.make_async_copy(src, dst, save.at[sem])
        copy.start()
        saves[name] = copy

    def before_write(name):
        if name in saves:
            saves.pop(name).wait()

    def finish(layer, matrix):
        pl.when(s == layer)(own_copies[matrix].wait)
        for back in range(chips):
            landed(spot(matrix, layer, back, 1 - c), cr.at[layer, matrix, back])
        if matrix == Q:
            for part in range(3):
                keep(
                    "whole%d%d%d" % (layer, matrix, part),
                    whole[matrix].at[layer, part],
                    gq_out.at[layer, :, pl.ds(part * width, width)],
                    22 + 3 * layer + part,
                )
        else:
            keep(
                "whole%d%d" % (layer, matrix),
                whole[matrix].at[layer],
                (None, go_out, gu_out, gd_out)[matrix].at[layer],
                14 + 4 * layer + matrix,
            )

    exchanges = {}

    def y_start(src, dst, index, part):
        start, stop = parts[part]
        span = pl.ds(start, min(stop, sent_rows) - start)
        copy = remote(
            src.at[span],
            dst.at[span],
            y_send.at[index, part],
            y_recv.at[index, part],
            here.y_peer,
        )
        copy.start()
        exchanges[index, part] = copy

    def y_wait(index, part):
        exchanges[index, part].wait_recv()

    def y_departed(index):
        for part in range(2):
            exchanges.pop((index, part)).wait_send()

    def begin(layer, part, value):
        span = slice(*parts[part])
        hs[layer, span] = value
        unit, _ = normalize(value)
        vectors = Vectors(vec.at[layer], width, None)
        n1[layer, 0, span] = unit * vectors.gain(0) + vectors.shift(0)
        y_start(n1.at[layer, 0], n1.at[layer, 1], 4 * layer, part)

    def project(layer, image, span):
        vectors = Vectors(vec.at[layer], width, None)
        for piece in range(3):
            lanes = slice(piece * width, (piece + 1) * width)
            value = dot(n1[layer, image, span], gq[layer, piece], 1, 0)
            if piece == 0:
                value = value + vectors.query()
            if piece == 2:
                value = value + vectors.value()
            joined[image, span, lanes] = value

    def expand(layer, image, span):
        vectors = Vectors(vec.at[layer], width, None)
        for piece in range(pre.shape[2] // depth):
            lanes = slice(piece * depth, (piece + 1) * depth)
            value = dot(n2[layer, image, span], gu[layer, :, lanes], 1, 0)
            value = value + vectors.up(piece)
            pre[image, span, lanes] = value
            hidden[image, span, lanes] = value * phi_big(value)

    everything = slice(0, rows)
    for part in range(2):
        begin(0, part, x_in[slice(*parts[part])])
    for layer in range(2):
        vectors = Vectors(vec.at[layer], width, None)
        point(layer, LAYER)
        before_write("joined")
        before_write("mixed")
        finish(layer, Q)
        project(layer, 0, everything)
        attend(joined.at[0], mixed.at[0], seq)
        point(layer, MIXED)
        finish(layer, O)
        mid[layer] = hs[layer] + dot(mixed[0], go[layer], 1, 1) + vectors.shift(2)
        for part in range(2):
            point(layer, TOKENS + part)
            y_wait(4 * layer, part)
            project(layer, 1, slice(*parts[part]))
        attend(joined.at[1], mixed.at[1], seq)
        if layer == 1:
            y_departed(1)
        for part in range(2):
            span = slice(*parts[part])
            sending[0, span] = dot(mixed[1, span], go[layer], 1, 1)
            y_start(sending.at[0], received.at[2 * layer], 4 * layer + 1, part)
        keep("n1%d" % layer, n1.at[layer], n1_out.at[layer], 4 + layer)
        keep("joined", joined, joined_out.at[layer], 6 + layer)
        keep("mixed", mixed, mixed_out.at[layer], 8 + layer)
        for part in range(2):
            span = slice(*parts[part])
            point(layer, MIDDLE + part)
            y_wait(4 * layer + 1, part)
            middle = mid[layer, span] + received[2 * layer, span]
            mid[layer, span] = middle
            unit, _ = normalize(middle)
            n2[layer, 0, span] = unit * vectors.gain(1) + vectors.shift(1)
            y_start(n2.at[layer, 0], n2.at[layer, 1], 4 * layer + 2, part)
        point(layer, SECOND)
        before_write("pre")
        finish(layer, U)
        expand(layer, 0, everything)
        if layer == 0:
            for part in range(2):
                point(0, SECONDS + part)
                y_wait(2, part)
                expand(0, 1, slice(*parts[part]))
        else:
            y_departed(3)
        point(layer, HIDDEN)
        finish(layer, D)
        if layer == 1:
            out_all[layer] = mid[layer] + dot(hidden[0], gd[layer], 1, 1)
        for part in range(2):
            span = slice(*parts[part])
            if layer == 1:
                point(1, SECONDS + part)
                y_wait(6, part)
                expand(1, 1, span)
            sending[1, span] = dot(hidden[1, span], gd[layer], 1, 1)
            y_start(sending.at[1], received.at[2 * layer + 1], 4 * layer + 3, part)
        if layer == 0:
            out_all[layer] = mid[layer] + dot(hidden[0], gd[layer], 1, 1)
        keep("n2%d" % layer, n2.at[layer], n2_out.at[layer], 10 + layer)
        keep("pre", pre, pre_out.at[layer], 12 + layer)
        for part in range(2):
            span = slice(*parts[part])
            point(layer, RESULT + part)
            y_wait(4 * layer + 3, part)
            result = out_all[layer, span] + received[2 * layer + 1, span]
            result = (result + vectors.shift(3)) * live[span, 0:1]
            out_all[layer, span] = result
            if layer == 0:
                begin(1, part, result)

    for copy in saves.values():
        copy.wait()
    for copy in exchanges.values():
        copy.wait_send()
    def z_departures(layer, matrix):
        for step in range(1, chips):
            when(here.direct(step), z_copy(layer, matrix, step).wait_send)
        if here.relays:
            pl.when(here.middle)(z_relay(layer, matrix).wait_send)

    def departures(section):
        for layer in range(2):
            for matrix in range(4):
                path = GATHER[layer][matrix]
                own = section == layer
                if own:
                    x_copy(layer, matrix, 0).wait_send()
                if path == (VIA_OWN if own else VIA_OTHER):
                    for back in range(1, chips):
                        x_copy(layer, matrix, back).wait_send()
                if path != (VIA_OTHER if own else VIA_OWN):
                    z_departures(layer, matrix)

    for section in range(2):
        pl.when(s == section)(functools.partial(departures, section))
    for layer in range(2):
        for matrix in range(4):
            for back in range(chips):
                c_copy(layer, matrix, back).wait_send()


def forward(chips, seq, x_in, live, vec_in, wq, wo, wu, wd):
    rows, depth = x_in.shape
    sent_rows = up_to(seq, 8)
    width = wo.shape[1]
    hidden = wu.shape[1]
    widths = (3 * width, width, hidden, hidden)
    whole = [(2, depth, w) for w in widths]
    any_space = pl.BlockSpec(memory_space=pl.ANY)
    vmem = pl.BlockSpec(memory_space=pltpu.VMEM)
    both = (2, 16, depth)
    outs = [
        ((2, rows, depth), vmem),
        (both, vmem),
        ((2, rows, depth), vmem),
        ((2, rows, depth), vmem),
        *[(w, any_space) for w in whole],
        ((2, 2, rows, depth), any_space),
        ((2, 2, rows, depth), any_space),
        ((2, 2, rows, 3 * width), any_space),
        ((2, 2, rows, width), any_space),
        ((2, 2, rows, hidden), any_space),
    ]
    sems = pltpu.SemaphoreType.DMA
    scratch = [
        pltpu.VMEM((2, 3, depth, width), F32),
        *[pltpu.VMEM(w, F32) for w in whole[1:]],
        pltpu.VMEM((2, 2, rows, depth), F32),
        pltpu.VMEM((2, 2, rows, depth), F32),
        pltpu.VMEM((2, rows, 3 * width), F32),
        pltpu.VMEM((2, rows, width), F32),
        pltpu.VMEM((2, rows, hidden), F32),
        pltpu.VMEM((2, rows, hidden), F32),
        pltpu.VMEM((4, rows, depth), F32),
        pltpu.VMEM((2, rows, depth), F32),
        pltpu.VMEM((2, 2, 2, chips) + vec_in.shape, F32),
        sems((8, 2)),
        sems((8, 2)),
        sems((chips + 2,)),
        sems((chips + 2,)),
        *[sems((2, 4, chips)) for _ in range(6)],
        sems((4,)),
        sems((28,)),
    ]
    return pl.pallas_call(
        functools.partial(forward_kernel, chips, seq, sent_rows),
        out_shape=[jax.ShapeDtypeStruct(shape, F32) for shape, _ in outs],
        in_specs=[vmem] * 3 + [any_space] * 4,
        out_specs=[spec for _, spec in outs],
        scratch_shapes=scratch,
        compiler_params=pltpu.CompilerParams(
            collective_id=0, has_side_effects=True, vmem_limit_bytes=VMEM_BYTES
        ),
        name="forward_both",
    )(x_in, live, vec_in, wq, wo, wu, wd)


SUMS = (
    (VIA_OTHER, VIA_OTHER, VIA_OWN, BOTH),
    (VIA_OTHER, VIA_OWN, VIA_OWN, VIA_OTHER),
)

SUM_UP = (
    {
        (1, MIDDLE + 0): (
            (CORE, 1, D),
        ),
        (1, MIDDLE + 1): (
            (SEND, 1, D), (CORE, 1, U),
        ),
        (1, HEADS): (
            (SEND, 1, U),
        ),
        (1, RESULT + 0): (
            (ADD, 1, D, 0), (CORE, 1, O), (ADD, 1, D, 1), (SEND, 1, O),
        ),
        (0, LAYER): (
            (CORE, 1, Q), (SEND, 1, Q), (ADD, 1, D, 2), (RELAY, 1, D),
        ),
        (0, MIDDLE + 0): (
            (CORE, 0, D),
        ),
        (0, MIDDLE + 1): (
            (SEND, 0, D), (ADD, 1, Q, 0), (CORE, 0, U),
        ),
        (0, HEADS): (
            (SEND, 0, U),
        ),
        (0, MIDDLES + 0): (
            (RELAY, 0, D),
        ),
        (0, REST): (
            (CORE, 0, O), (SEND, 0, O),
        ),
        (0, RESULT + 0): (
            (ADD, 1, Q, 2), (ADD, 0, U, 0), (ADD, 1, Q, 1), (CORE, 0, Q), (SEND, 0, Q),
            (ADD, 0, U, 1), (SUM, 1, D), (RELAY, 1, Q), (ADD, 0, U, 2), (RELAY, 0, U),
        ),
        (0, ENDING + 4): (
            (SUM, 0, D), (SUM, 1, Q), (ADD, 0, U, 3), (LAST, 0, D), (LAST, 0, Q),
            (LAST, 0, O), (SUM, 0, U),
        ),
    },
    {
        (1, MIDDLE + 1): (
            (CORE, 1, D), (SEND, 1, D),
        ),
        (1, MIDDLES + 0): (
            (CORE, 1, U),
        ),
        (1, REST): (
            (SEND, 1, U), (ADD, 1, U, 0),
        ),
        (0, LAYER): (
            (CORE, 1, O), (ADD, 1, U, 1), (SEND, 1, O),
        ),
        (0, GRADS + 0): (
            (CORE, 1, Q), (SEND, 1, Q),
        ),
        (0, GRADS + 1): (
            (ADD, 1, U, 2),
        ),
        (0, MIDDLE + 0): (
            (CORE, 0, D), (SEND, 0, D),
        ),
        (0, MIDDLE + 1): (
            (CORE, 0, U), (RELAY, 1, U), (SEND, 0, U),
        ),
        (0, RESULT + 0): (
            (CORE, 0, O), (ADD, 1, O, 2), (SEND, 0, O),
        ),
        (0, ENDING + 2): (
            (ADD, 1, O, 1), (ADD, 1, U, 3), (ADD, 0, O, 2), (RELAY, 0, D), (CORE, 0, Q),
            (ADD, 0, O, 0), (SEND, 0, Q), (ADD, 0, Q, 0),
        ),
        (0, ENDING + 3): (
            (ADD, 0, Q, 1), (ADD, 1, O, 3), (ADD, 1, O, 0), (ADD, 0, Q, 2), (RELAY, 0, Q),
            (SUM, 0, D), (SUM, 1, U), (RELAY, 0, O), (LAST, 1, D), (RELAY, 1, O),
            (SUM, 0, Q), (ADD, 0, O, 1),
        ),
        (0, ENDING + 4): (
            (LAST, 1, Q), (SUM, 1, O), (SUM, 0, O),
        ),
    },
)


def slots_of(matrix, chips):
    slots = {}
    counts = [0, 0]
    for layer in range(2):
        path = SUMS[layer][matrix]
        slots[layer, layer] = counts[layer]
        counts[layer] += chips if path == VIA_OWN else 1
        if path == VIA_OTHER:
            slots[1 - layer, layer] = counts[1 - layer] - 1
            counts[1 - layer] += chips - 1
    return slots, max(counts)


def backward_kernel(
    chips,
    seq,
    sent_rows,
    cot,
    live,
    vec,
    out_all,
    hs_in,
    mid_in,
    gq_in,
    go_in,
    gu_in,
    gd_in,
    n1_in,
    n2_in,
    joined_in,
    mixed_in,
    pre_in,
    vec_out,
    outq,
    outo,
    outu,
    outd,
    gin_both,
    out_both,
    rcq,
    rco,
    rcu,
    rcd,
    rzq,
    rzo,
    rzu,
    rzd,
    gin,
    gvec,
    wb,
    wu,
    before,
    normed,
    joined,
    mixed,
    pre,
    hidden,
    grad_all,
    mid_all,
    received,
    sending,
    own_part,
    grad_mixed,
    grad_joined,
    aq,
    ao,
    au,
    ad,
    rxq,
    rxo,
    rxu,
    rxd,
    tile,
    fetched,
    single,
    cut,
    vc,
    vy,
    vz,
    vx,
    y_send,
    y_recv,
    loads,
    cs,
    cl,
    cr,
    xs,
    xr,
    zs,
    zr,
    fetch_sem,
    single_sem,
    v_send,
    v_recv,
    g_send,
    g_recv,
    g_own,
):
    here = Place(chips)
    s, c, z = here.s, here.c, here.z
    rows, depth = cot.shape
    width = mixed.shape[2]
    width_ff = wu.shape[1]
    tail = rows - sent_rows
    parts = parts_of(rows)
    mine = (aq, ao, au, ad)
    from_core = (rcq, rco, rcu, rcd)
    from_x = (rxq, rxo, rxu, rxd)
    x_slots = [slots_of(matrix, chips)[0] for matrix in range(4)]
    from_z = (rzq, rzo, rzu, rzd)
    outs = (outq, outo, outu, outd)
    block = outo.shape[0]
    small = 24 if block % 24 == 0 else block
    for buffer in (grad_all, mid_all):
        buffer[1, sent_rows:rows, :] = jnp.zeros((tail, depth), F32)
    for index in range(received.shape[0]):
        received[index, sent_rows:rows, :] = jnp.zeros((tail, depth), F32)
    gvec[...] = jnp.zeros(gvec.shape, F32)

    wq, wo = wb.at[:, 0 : 3 * width], wb.at[:, 3 * width : 4 * width]
    sources = dict(
        wd=(gd_in, wb),
        pre=(pre_in, pre),
        wu=(gu_in, wu),
        n2=(n2_in, normed),
        mid=(mid_in, before),
        joined=(joined_in, joined),
        mixed=(mixed_in, mixed),
        n1=(n1_in, normed),
        hs=(hs_in, before),
        wo=(go_in, wo),
        wq=(gq_in, wq),
    )
    order = list(sources)
    loading = {}

    def load(name, layer):
        src, dst = sources[name]
        copy = pltpu.make_async_copy(src.at[layer], dst, loads.at[order.index(name)])
        copy.start()
        loading[name] = copy

    def loaded(name):
        loading.pop(name).wait()

    for name in order[:-2]:
        if name not in ("hs", "n1"):
            load(name, 1)
    cot_copy = pltpu.make_async_copy(cot, own_part, loads.at[len(order)])
    cot_copy.start()
    here.greet()
    departing = []

    def launch(copy):
        copy.start()
        departing.append(copy)
        return copy

    def departed(copy):
        copy.wait_send()
        departing[:] = [item for item in departing if item is not copy]

    exchanges = {}

    def y_start(src, dst, index, part):
        start, stop = parts[part]
        span = pl.ds(start, min(stop, sent_rows) - start)
        copy = remote(
            src.at[span],
            dst.at[span],
            y_send.at[index, part],
            y_recv.at[index, part],
            here.y_peer,
        )
        copy.start()
        exchanges[index, part] = copy

    def y_wait(index, part):
        exchanges[index, part].wait_recv()

    def y_departed(index):
        for part in range(2):
            exchanges.pop((index, part)).wait_send()

    def gin_copy():
        return remote(
            gin.at[1 - s], gin_both.at[s], g_send.at[1], g_recv.at[1], here.x_peer
        )

    out_copy = launch(
        remote(
            out_all.at[1 - s], out_both.at[s], g_send.at[0], g_recv.at[0], here.x_peer
        )
    )
    own_out = pltpu.make_async_copy(out_all.at[s], out_both.at[s], g_own.at[0])
    own_out.start()


    def tile_copies(slot, matrix, layer, number, start, size, step):
        lanes = pl.ds(start, size)
        spots = []
        for core in (1 - c, c):
            first = pl.multiple_of((here.z_at(step) * 2 + core) * block, 8)
            spots.append(tile.at[slot, pl.ds(first, block), pl.ds(0, size)])
        return (
            remote(
                spots[0],
                from_core[matrix].at[layer, step, :, lanes],
                cs.at[slot, step],
                cr.at[layer, matrix, number, step],
                here.core_peer,
            ),
            pltpu.make_async_copy(
                spots[1], mine[matrix].at[layer, step, :, lanes], cl.at[slot, step]
            ),
        )

    in_slot = [[None, None], [None, None]]
    next_slot = [0]

    def settle(section, slot):
        what = in_slot[section][slot]
        if what is not None:
            in_slot[section][slot] = None

            @pl.loop(0, chips)
            def _(step):
                away, kept = tile_copies(slot, *what, step)
                away.wait_send()
                kept.wait()

    def settle_all(slot):
        if in_slot[0][slot] == in_slot[1][slot]:
            settle(0, slot)
            in_slot[1][slot] = None
        for section in range(2):
            if in_slot[section][slot] is not None:
                pl.when(s == section)(functools.partial(settle, section, slot))

    def tiles_of(matrix):
        size = width if matrix < 2 else depth
        return [(n, n * size, size) for n in range(mine[matrix].shape[3] // size)]

    def flat(ref):
        return ref[...].reshape(2 * rows, ref.shape[-1])

    def product(matrix, layer, left, right):
        both = flat(left)
        for number, start, size in tiles_of(matrix):
            slot = next_slot[0]
            next_slot[0] = 1 - slot
            settle_all(slot)
            piece = right[:, :, start : start + size].reshape(2 * rows, size)
            tile[slot, :, 0:size] = dot(both, piece, 0, 0)
            what = (matrix, layer, number, start, size)

            @pl.loop(0, chips)
            def _(step):
                away, kept = tile_copies(slot, *what, step)
                away.start()
                kept.start()

            in_slot[0][slot] = in_slot[1][slot] = what

    def fetch(slot, src):
        spot = single.at[slot, :, pl.ds(0, src.shape[1])]
        copy = pltpu.make_async_copy(src, spot, single_sem.at[slot])
        copy.start()
        return copy, spot

    def add_from(src, target):
        copy, spot = fetch(0, src)
        copy.wait()
        add_rows(target, [spot], small)

    def x_slot(matrix, layer, step):
        to_own = SUMS[layer][matrix] == VIA_OWN or (isinstance(step, int) and step == 0)
        section = layer if to_own else 1 - layer
        return x_slots[matrix][section, layer] + step

    def x_grad(matrix, layer, step):
        return remote(
            mine[matrix].at[layer, step],
            from_x[matrix].at[x_slot(matrix, layer, step)],
            xs.at[layer, matrix, step],
            xr.at[layer, matrix, step],
            here.x_peer,
        )

    def z_grad(matrix, layer, step):
        return remote(
            mine[matrix].at[layer, step],
            from_z[matrix].at[layer, step],
            zs.at[layer, matrix, step],
            zr.at[layer, matrix, step],
            here.z_peer(step),
        )

    def z_left(matrix, layer):
        far = here.departures()[0]
        return remote(
            mine[matrix].at[layer, far],
            from_z[matrix].at[layer, 0],
            zs.at[layer, matrix, far],
            zr.at[layer, matrix, 0],
            here.z_peer(4 - far),
        )

    def z_out(matrix, layer, number):
        step = here.departures()[number]
        if not here.relays:
            if step:
                z_grad(matrix, layer, step).start()
        elif number == 0:
            pl.when(here.middle)(z_grad(matrix, layer, step).start)
            pl.when(~here.middle)(z_left(matrix, layer).start)
        elif number == 1:
            z_grad(matrix, layer, step).start()
        elif number == 2:
            pl.when(~here.middle)(z_grad(matrix, layer, step).start)

    def core(section, layer, matrix):
        for slot in range(2):
            what = in_slot[section][slot]
            if what is not None and what[:2] == (matrix, layer):
                settle(section, slot)
        for what in tiles_of(matrix):

            @pl.loop(0, chips)
            def _(step):
                tile_copies(0, matrix, layer, *what, step)[0].wait_recv()

        lanes = pl.ds(0, mine[matrix].shape[3])
        pltpu.make_async_copy(
            from_core[matrix].at[layer], fetched.at[:, :, lanes], fetch_sem
        ).start()

    def send(section, layer, matrix):
        lanes = pl.ds(0, mine[matrix].shape[3])
        pltpu.make_async_copy(
            from_core[matrix].at[layer], fetched.at[:, :, lanes], fetch_sem
        ).wait()
        path = SUMS[layer][matrix]
        for number, step in enumerate(here.departures()):
            add_rows(mine[matrix].at[layer, step], [fetched.at[step, :, lanes]], small)
            if path == BOTH:
                z_out(matrix, layer, number)
            elif path == VIA_OWN and section != layer:
                x_grad(matrix, layer, step).start()
            elif path == VIA_OTHER and section == layer and number < chips - 1:
                x_grad(matrix, layer, step).start()

    def add(section, layer, matrix, group):
        steps = here.departures()
        count, groups = (chips, 4) if section == layer else (chips - 1, 3)
        for number in range(count * group // groups, count * (group + 1) // groups):
            step = steps[number]
            x_grad(matrix, layer, step).wait_recv()
            block_in = from_x[matrix].at[x_slot(matrix, layer, step)]
            add_rows(mine[matrix].at[layer, step], [block_in], small)
            z_out(matrix, layer, number)

    def relay(section, layer, matrix):
        if here.relays:

            @pl.when(here.middle)
            def _():
                z_left(matrix, layer).wait_recv()
                add_from(from_z[matrix].at[layer, 0], mine[matrix].at[layer, 2])
                z_grad(matrix, layer, 2).start()

    def sum_z(section, layer, matrix):
        target = mine[matrix].at[layer, 0]

        def several(steps):
            fetched_now = []
            for slot, step in enumerate(steps):
                z_grad(matrix, layer, step).wait_recv()
                fetched_now.append(fetch(slot, from_z[matrix].at[layer, step]))
            for copy, _ in fetched_now:
                copy.wait()
            add_rows(target, [spot for _, spot in fetched_now], small)

        steps = here.departures()[:-1]
        if here.relays:
            pl.when(here.middle)(lambda: several([steps[0], 2, steps[1]]))
            pl.when(~here.middle)(lambda: several([steps[0], 2]))
        else:
            for step in steps:
                several([step])
        if section != layer:
            x_grad(matrix, layer, 0).start()

    def last(section, layer, matrix):
        x_grad(matrix, layer, 0).wait_recv()
        block_in = from_x[matrix].at[x_slot(matrix, layer, 0)]
        add_rows(mine[matrix].at[layer, 0], [block_in], small)

    actions = (core, send, add, relay, sum_z, last)

    def act(section, events):
        for name, layer, matrix, *more in events:
            actions[name](section, layer, matrix, *more)

    def point(layer, name):
        for section in range(2):
            events = SUM_UP[section].get((layer, name))
            if events:
                pl.when(s == section)(functools.partial(act, section, events))

    def total(value):
        return jnp.sum(value, 0, keepdims=True)

    def note(layer, row, value):
        gvec[layer, row : row + 1, :] = gvec[layer, row : row + 1, :] + total(value)

    def begin(layer, part, value):
        span = slice(*parts[part])
        grad_all[0, span] = value
        y_start(grad_all.at[0], grad_all.at[1], 4 * (1 - layer), part)
        note(layer, 5, value)

    def contract(layer, image, span):
        for piece in range(width_ff // depth):
            lanes = slice(piece * depth, (piece + 1) * depth)
            grad_hidden = dot(grad_all[image, span], wb[:, lanes], 1, 0)
            value = pre[image, span, lanes]
            upper = phi_big(value)
            hidden[image, span, lanes] = value * upper
            pre[image, span, lanes] = grad_hidden * (upper + value * phi_small(value))

    everything = slice(0, rows)
    cot_copy.wait()
    for part in range(2):
        span = slice(*parts[part])
        begin(1, part, own_part[span] * live[span, 0:1])
    for layer in (1, 0):
        vectors = Vectors(vec.at[layer], width, None)
        base = 4 * (1 - layer)
        point(layer, LAYER)
        loaded("wd")
        loaded("pre")
        contract(layer, 0, everything)
        loaded("wu")
        own_part[...] = dot(pre[0], wu[...], 1, 1)
        if layer == 0:
            y_departed(3)
        for part in range(2):
            span = slice(*parts[part])
            point(layer, GRADS + part)
            y_wait(base, part)
            contract(layer, 1, span)
            sending[span] = dot(pre[1, span], wu[...], 1, 1)
            y_start(sending, received.at[0], base + 1, part)
        load("wo", layer)
        load("wq", layer)
        if layer == 1:
            load("wu", 0)
        point(layer, PRODUCTS)
        product(D, layer, grad_all, hidden)
        point(layer, PRODUCT_UP)
        loaded("n2")
        product(U, layer, normed, pre)
        load("n1", layer)
        for piece in range(width_ff // depth):
            lanes = slice(piece * depth, (piece + 1) * depth)
            note(layer, 9 + piece, pre[0, :, lanes])
            note(layer, 9 + piece, pre[1, :, lanes])
        if layer == 1:
            load("pre", 0)
        loaded("mid")
        if layer == 0:
            y_departed(2)
        for part in range(2):
            span = slice(*parts[part])
            point(layer, MIDDLE + part)
            unit, inverse = normalize(before[span])
            y_wait(base + 1, part)
            grad_second = own_part[span] + received[0, span]
            grad_middle = grad_all[0, span] + normalize_back(
                grad_second * vectors.gain(1), unit, inverse
            )
            mid_all[0, span] = grad_middle
            y_start(mid_all.at[0], mid_all.at[1], base + 2, part)
            note(layer, 1, grad_second * unit)
            note(layer, 3, grad_second)
            note(layer, 4, grad_middle)
        load("hs", layer)
        point(layer, HEADS)
        loaded("wo")
        loaded("joined")
        loaded("mixed")
        grad_mixed[...] = dot(mid_all[0], wo[...], 1, 0)
        attend_back(joined.at[0], mixed.at[0], grad_mixed, grad_joined.at[0], seq)
        loaded("wq")
        own_part[...] = dot(grad_joined[0], wq[...], 1, 1)
        for part in range(2):
            span = slice(*parts[part])
            point(layer, MIDDLES + part)
            y_wait(base + 2, part)
            grad_mixed[span] = dot(mid_all[1, span], wo[...], 1, 0)
        attend_back(joined.at[1], mixed.at[1], grad_mixed, grad_joined.at[1], seq)
        y_departed(base + 1)
        for part in range(2):
            span = slice(*parts[part])
            sending[span] = dot(grad_joined[1, span], wq[...], 1, 1)
            y_start(sending, received.at[1], base + 3, part)
        if layer == 1:
            load("wd", 0)
            load("joined", 0)
        point(layer, PRODUCT_OUT)
        product(O, layer, mid_all, mixed)
        loaded("n1")
        product(Q, layer, normed, grad_joined)
        if layer == 1:
            load("mixed", 0)
            load("n2", 0)
        for image in range(2):
            for piece in (0, 2):
                lanes = slice(piece * width, (piece + 1) * width)
                spot = slice(piece // 2 * width, (piece // 2 + 1) * width)
                gvec[layer, 8:9, spot] = gvec[layer, 8:9, spot] + total(
                    grad_joined[image, :, lanes]
                )
        point(layer, REST)
        loaded("hs")
        if layer == 1:
            y_departed(0)
        for part in range(2):
            span = slice(*parts[part])
            point(layer, RESULT + part)
            unit, inverse = normalize(before[span])
            y_wait(base + 3, part)
            grad_first = own_part[span] + received[1, span]
            value = mid_all[0, span] + normalize_back(
                grad_first * vectors.gain(0), unit, inverse
            )
            gin[layer, span] = value
            if layer == 1:
                begin(0, part, value * live[span, 0:1])
            note(layer, 0, grad_first * unit)
            note(layer, 2, grad_first)
        if layer == 1:
            load("mid", 0)
            pl.when(s == 0)(gin_copy().start)
    for layer in range(2):

        def write(tensor, core, chip, upper, lower):
            step = (chip + chips - z) % chips
            cut[tensor, core, layer, step, 0:8] = upper
            cut[tensor, core, layer, step, 8:16] = lower

        cut_vectors(gvec.at[layer], depth // (4 * chips), chips, here.t, write)
    copy = launch(
        remote(cut.at[:, 1 - c], vc, v_send.at[0], v_recv.at[0], here.core_peer)
    )
    point(0, ENDING + 0)
    copy.wait_recv()
    point(0, ENDING + 1)
    cut[:, c] = cut[:, c] + vc[...]
    copy = launch(
        remote(cut.at[1 - here.t, c], vy, v_send.at[1], v_recv.at[1], here.y_peer)
    )
    point(0, ENDING + 2)
    copy.wait_recv()
    cut[here.t, c] = cut[here.t, c] + vy[...]
    copy = launch(
        remote(
            cut.at[here.t, c, 1 - s],
            vx,
            v_send.at[chips + 1],
            v_recv.at[chips + 1],
            here.x_peer,
        )
    )
    pl.when(s == 1)(gin_copy().start)
    point(0, ENDING + 3)
    copy.wait_recv()
    cut[here.t, c, s] = cut[here.t, c, s] + vx[...]
    copies = []
    for step in range(1, chips):
        copies.append(
            launch(
                remote(
                    cut.at[here.t, c, s, step],
                    vz.at[step - 1],
                    v_send.at[1 + step],
                    v_recv.at[1 + step],
                    here.z_peer(step),
                )
            )
        )
    point(0, ENDING + 4)
    for section in range(2):

        @pl.when(s == section)
        def _():
            for part in range(3):
                lanes = slice(part * width, (part + 1) * width)
                outq[part] = mine[Q][section, 0, :, lanes]
            for matrix in (O, U, D):
                outs[matrix][...] = mine[matrix][section, 0]

    total_vec = cut[here.t, c, s, 0]
    for step in range(1, chips):
        copies[step - 1].wait_recv()
        total_vec = total_vec + vz[step - 1]
    vec_out[...] = total_vec
    for slot in range(2):
        settle_all(slot)
    own_gin = pltpu.make_async_copy(gin.at[s], gin_both.at[s], g_own.at[1])
    own_gin.start()
    out_copy.wait_recv()
    gin_copy().wait()
    own_out.wait()
    own_gin.wait()
    for item in departing:
        item.wait_send()
    for item in exchanges.values():
        item.wait_send()

    def departures(section):
        for layer in range(2):
            own = section == layer
            for matrix in range(4):
                path = SUMS[layer][matrix]
                if path != (VIA_OTHER if own else VIA_OWN):
                    for step in here.departures()[:-1]:
                        z_grad(matrix, layer, step).wait_send()
                    if not own:
                        x_grad(matrix, layer, 0).wait_send()
                elif own:
                    for step in range(1, chips):
                        x_grad(matrix, layer, step).wait_send()
                else:
                    for step in range(chips):
                        x_grad(matrix, layer, step).wait_send()

    for section in range(2):
        pl.when(s == section)(functools.partial(departures, section))


def backward(chips, seq, cot, live, vec, out_all, hs, mid, whole, kept):
    rows, depth = cot.shape
    sent_rows = up_to(seq, 8)
    width, width_ff = whole[1].shape[2], whole[2].shape[2]
    widths = [w.shape[2] for w in whole]
    block = depth // (2 * chips)
    any_space = pl.BlockSpec(memory_space=pl.ANY)
    vmem = pl.BlockSpec(memory_space=pltpu.VMEM)
    outs = [
        ((16, 128), vmem),
        ((3, block, width), vmem),
        *[((block, w), vmem) for w in widths[1:]],
        ((2, rows, depth), any_space),
        ((2, rows, depth), any_space),
        *[((2, chips, block, w), any_space) for w in widths * 2],
    ]
    sems = pltpu.SemaphoreType.DMA
    scratch = [
        pltpu.VMEM((2, rows, depth), F32),
        pltpu.VMEM(vec.shape, F32),
        pltpu.VMEM((depth, width_ff), F32),
        pltpu.VMEM((depth, width_ff), F32),
        pltpu.VMEM((rows, depth), F32),
        pltpu.VMEM((2, rows, depth), F32),
        pltpu.VMEM((2, rows, 3 * width), F32),
        pltpu.VMEM((2, rows, width), F32),
        pltpu.VMEM((2, rows, width_ff), F32),
        pltpu.VMEM((2, rows, width_ff), F32),
        *[pltpu.VMEM((2, rows, depth), F32) for _ in range(3)],
        pltpu.VMEM((rows, depth), F32),
        pltpu.VMEM((rows, depth), F32),
        pltpu.VMEM((rows, width), F32),
        pltpu.VMEM((2, rows, 3 * width), F32),
        *[pltpu.VMEM((2, chips, block, w), F32) for w in widths],
        *[
            pltpu.VMEM((slots_of(matrix, chips)[1], block, w), F32)
            for matrix, w in enumerate(widths)
        ],
        pltpu.VMEM((2, depth, depth), F32),
        pltpu.VMEM((chips, block, width_ff), F32),
        pltpu.VMEM((3, block, width_ff), F32),
        pltpu.VMEM((2, 2, 2, chips, 16, 128), F32),
        pltpu.VMEM((2, 2, chips, 16, 128), F32),
        pltpu.VMEM((2, chips, 16, 128), F32),
        pltpu.VMEM((chips - 1, 16, 128), F32),
        pltpu.VMEM((chips, 16, 128), F32),
        sems((8, 2)),
        sems((8, 2)),
        sems((12,)),
        sems((2, chips)),
        sems((2, chips)),
        sems((2, 4, 3, chips)),
        *[sems((2, 4, chips)) for _ in range(4)],
        sems,
        sems((3,)),
        sems((chips + 2,)),
        sems((chips + 2,)),
        sems((2,)),
        sems((2,)),
        sems((2,)),
    ]
    results = pl.pallas_call(
        functools.partial(backward_kernel, chips, seq, sent_rows),
        out_shape=[jax.ShapeDtypeStruct(shape, F32) for shape, _ in outs],
        in_specs=[any_space] + [vmem] * 2 + [any_space] * 12,
        out_specs=[spec for _, spec in outs],
        scratch_shapes=scratch,
        compiler_params=pltpu.CompilerParams(
            collective_id=1, has_side_effects=True, vmem_limit_bytes=VMEM_BYTES
        ),
        name="backward_both",
    )(cot, live, vec, out_all, hs, mid, *whole, *kept)
    return results[:7]


def body(
    embedded,
    image_counts,
    cotangent,
    qkv_weight,
    qv_bias,
    out_weight,
    up_weight,
    up_bias,
    down_weight,
    norm_gains,
    shift_terms,
):
    groups = lax.axis_size("dp")
    chips = groups // 2
    tensors = lax.axis_size("tensor")
    s = lax.axis_index("section")
    t = lax.axis_index("tensor")
    seq = embedded.shape[3]
    rows = up_to(seq, 16)

    def padded(value):
        chosen = lax.dynamic_index_in_dim(value[:, 0, 0], s, 0, keepdims=False)
        return jnp.pad(chosen, ((0, rows - seq), (0, 0)))

    slot = s * tensors + t
    alive = (slot < image_counts[0]).astype(F32)
    inside = lax.broadcasted_iota(jnp.int32, (rows, 128), 0) < seq
    live = jnp.where(inside, alive, 0.0)

    pieces = [norm_gains[0], shift_terms[0], qv_bias[0], up_bias.reshape(4, -1)]
    packed = jnp.concatenate(pieces)
    packed = jnp.pad(packed, ((0, 16 - packed.shape[0]), (0, 128 - packed.shape[1])))

    shards = (
        qkv_weight[0].transpose(1, 0, 2),
        out_weight[0].T,
        up_weight[0],
        down_weight[0].T,
    )
    out_all, vec, hs, mid, gq, go, gu, gd, *kept = forward(
        chips, seq, padded(embedded), live, packed, *shards
    )
    vec_sum, sum_q, sum_o, sum_u, sum_d, gin_both, out_both = backward(
        chips,
        seq,
        padded(cotangent),
        live,
        vec,
        out_all,
        hs,
        mid,
        (gq, go, gu, gd),
        kept,
    )
    piece = norm_gains.shape[2]
    return (
        out_both[None, :, None, None, :seq],
        gin_both[None, :, None, None, :seq],
        sum_q.transpose(1, 0, 2)[None],
        vec_sum[None, 6:8, :piece],
        sum_o.T[None],
        sum_u[None],
        vec_sum[8:12, :piece].reshape(1, 4 * piece),
        sum_d.T[None],
        vec_sum[None, 0:2, :piece],
        vec_sum[None, 2:6, :piece],
    )


def solution(mesh):
    placed = (
        P(None, "dp", "tensor", None, None),
        P("dp"),
        P(None, "dp", "tensor", None, None),
        P("section", "dp", None, "tensor"),
        P("section", None, ("tensor", "dp")),
        P("section", "tensor", "dp"),
        P("section", "dp", "tensor"),
        P("section", ("tensor", "dp")),
        P("section", "tensor", "dp"),
        P("section", None, ("tensor", "dp")),
        P("section", None, ("tensor", "dp")),
    )
    return jax.shard_map(
        body,
        mesh=mesh,
        in_specs=placed,
        out_specs=(
            P("section", None, "dp", "tensor", None, None),
            P("section", None, "dp", "tensor", None, None),
            P("section", "dp", None, "tensor"),
            P("section", None, ("tensor", "dp")),
            P("section", "tensor", "dp"),
            P("section", "dp", "tensor"),
            P("section", ("tensor", "dp")),
            P("section", "tensor", "dp"),
            P("section", None, ("tensor", "dp")),
            P("section", None, ("tensor", "dp")),
        ),
        check_vma=False,
    )
```

```python
import functools

import jax
import jax.numpy as jnp
from jax import lax
from jax.experimental import pallas as pl
from jax.experimental.pallas import tpu as pltpu
from jax.sharding import PartitionSpec as P

HD = 64
SCALE = HD ** (-0.5)
EPS = 1e-06
HIGH = lax.Precision.HIGH
MESH = pl.DeviceIdType.MESH
VMEM_BYTES = 63 * 2**20
F32 = jnp.float32


def dot(left, right, left_dim, right_dim):
    return lax.dot_general(
        left,
        right,
        (((left_dim,), (right_dim,)), ((), ())),
        precision=HIGH,
        preferred_element_type=F32,
    )


def up_to(count, step):
    return -(-count // step) * step


def normalize(value):
    centred = value - jnp.mean(value, -1, keepdims=True)
    inverse = lax.rsqrt(jnp.mean(centred * centred, -1, keepdims=True) + EPS)
    return centred * inverse, inverse


def normalize_back(grad_unit, unit, inverse):
    return inverse * (
        grad_unit
        - jnp.mean(grad_unit, -1, keepdims=True)
        - unit * jnp.mean(grad_unit * unit, -1, keepdims=True)
    )


class Place:
    def __init__(self, chips):
        self.s = lax.axis_index("section")
        self.t = lax.axis_index("tensor")
        d = lax.axis_index("dp")
        self.chips = chips
        self.z = d // 2
        self.c = d % 2
        self.x_peer = (1 - self.s, self.t, d)
        self.y_peer = (self.s, 1 - self.t, d)
        self.core_peer = (self.s, self.t, self.z * 2 + 1 - self.c)

    def z_at(self, step):
        return (self.z + self.chips + step) % self.chips

    def z_peer(self, step):
        return (self.s, self.t, self.z_at(step) * 2 + self.c)

    def greet(self):
        barrier = pltpu.get_barrier_semaphore()
        peers = [self.x_peer, self.y_peer, self.core_peer]
        peers += [self.z_peer(step) for step in range(1, self.chips)]
        for peer in peers:
            pl.semaphore_signal(barrier, inc=1, device_id=peer, device_id_type=MESH)
        pl.semaphore_wait(barrier, len(peers))


    @property
    def relays(self):
        return self.chips == 4

    def arrivals(self):
        if not self.relays:
            return list(range(1, self.chips))
        near = jnp.where(self.z < 2, 3, 1)
        return [2, near, 4 - near]

    def departures(self):
        if not self.relays:
            return list(range(1, self.chips)) + [0]
        far = jnp.where(self.z < 2, 3, 1)
        return [far, 4 - far, 2, 0]

    @property
    def middle(self):
        return (self.z == 1) | (self.z == 2)

    def direct(self, step):
        if not self.relays or step == 2:
            return None
        return self.z <= 2 if step == 1 else self.z >= 1


def when(condition, action):
    if condition is None:
        action()
    else:
        pl.when(condition)(action)


def parts_of(rows):
    first = up_to(rows // 2, 8)
    return [(0, first), (first, rows)]


def remote(src, dst, send, recv, peer):
    return pltpu.make_async_remote_copy(
        src_ref=src,
        dst_ref=dst,
        send_sem=send,
        recv_sem=recv,
        device_id=peer,
        device_id_type=MESH,
    )


def key_mask(rows, seq):
    return lax.broadcasted_iota(jnp.int32, (rows, rows), 1) < seq


def head_lanes(which):
    return lax.broadcasted_iota(jnp.int32, (1, 2 * HD), 1) // HD == which


def attend(joined, mixed, seq):
    rows, width = mixed.shape
    keep = key_mask(rows, seq)
    for pair in range(width // (2 * HD)):
        lanes = slice(pair * 2 * HD, (pair + 1) * 2 * HD)
        query = joined[:, lanes] * SCALE
        keys = joined[:, width + lanes.start : width + lanes.stop]
        values = joined[:, 2 * width + lanes.start : 2 * width + lanes.stop]
        total = None
        for which in range(2):
            own = head_lanes(which)
            scores = dot(query, jnp.where(own, keys, 0.0), 1, 1)
            scores = jnp.where(keep, scores, -3e38)
            weights = jnp.exp(scores - jnp.max(scores, -1, keepdims=True))
            probs = weights / jnp.sum(weights, -1, keepdims=True)
            part = dot(probs, jnp.where(own, values, 0.0), 1, 0)
            total = part if total is None else total + part
        mixed[:, lanes] = total


def attend_back(joined, mixed, grad_mixed, grad_joined, seq):
    rows, width = mixed.shape
    keep = key_mask(rows, seq)
    for pair in range(width // (2 * HD)):
        lanes = slice(pair * 2 * HD, (pair + 1) * 2 * HD)
        query = joined[:, lanes] * SCALE
        keys = joined[:, width + lanes.start : width + lanes.stop]
        values = joined[:, 2 * width + lanes.start : 2 * width + lanes.stop]
        grad = grad_mixed[:, lanes]
        product = grad * mixed[:, lanes]
        grads = [None, None, None]
        for which in range(2):
            own = head_lanes(which)
            own_keys = jnp.where(own, keys, 0.0)
            scores = dot(query, own_keys, 1, 1)
            scores = jnp.where(keep, scores, -3e38)
            weights = jnp.exp(scores - jnp.max(scores, -1, keepdims=True))
            probs = weights / jnp.sum(weights, -1, keepdims=True)
            own_grad = jnp.where(own, grad, 0.0)
            row_dot = jnp.sum(jnp.where(own, product, 0.0), -1, keepdims=True)
            grad_probs = dot(grad, jnp.where(own, values, 0.0), 1, 1)
            grad_scores = probs * (grad_probs - row_dot)
            parts = (
                dot(grad_scores, own_keys, 1, 0) * SCALE,
                dot(grad_scores, jnp.where(own, query, 0.0), 0, 0),
                dot(probs, own_grad, 0, 0),
            )
            grads = [b if a is None else a + b for a, b in zip(grads, parts)]
        for number, part in enumerate(grads):
            start = number * width + lanes.start
            grad_joined[:, start : start + 2 * HD] = part


def phi_big(value):
    return 0.5 * (1.0 + lax.erf(value * 0.7071067811865476))


def phi_small(value):
    return jnp.exp(-0.5 * value * value) * 0.3989422804014327


class Vectors:
    def __init__(self, ref, width, hidden):
        self.ref, self.width, self.hidden = ref, width, hidden

    def gain(self, which):
        return self.ref[which : which + 1, :]

    def shift(self, which):
        return self.ref[2 + which : 3 + which, :]

    def query(self):
        return self.ref[8:9, 0 : self.width]

    def value(self):
        return self.ref[8:9, self.width : 2 * self.width]

    def up(self, row):
        return self.ref[9 + row : 10 + row, :]


def place(tile, start, piece, lanes):
    lane = lax.broadcasted_iota(jnp.int32, tile.shape, 1)
    tile = jnp.where(lane < piece, tile, 0.0)
    first, shift = divmod(start, 128)
    if shift == 0:
        return {first: tile}
    turned = pltpu.roll(tile, shift, 1)
    if shift + piece <= 128:
        return {first: turned}
    return {
        first: jnp.where(lane >= shift, turned, 0.0),
        first + 1: jnp.where(lane < shift, turned, 0.0),
    }


def take(read, start, piece):
    first, shift = divmod(start, 128)
    tile = read(first)
    lane = lax.broadcasted_iota(jnp.int32, tile.shape, 1)
    if shift:
        tile = pltpu.roll(tile, 128 - shift, 1)
        if shift + piece > 128:
            after = pltpu.roll(read(first + 1), 128 - shift, 1)
            tile = jnp.where(lane < 128 - shift, tile, after)
    return jnp.where(lane < piece, tile, 0.0)


def spread_vectors(target, pieces, piece, chips, own):
    depth = target.shape[1]
    width = depth // 2
    tiles = [{} for _ in range(3)]

    def gather(kind, found, rows):
        for index, value in found.items():
            value = jnp.where(rows, value, 0.0)
            old = tiles[kind].get(index)
            tiles[kind][index] = value if old is None else old + value

    row = lax.broadcasted_iota(jnp.int32, (8, 128), 0)
    for chip in range(chips):
        for core in range(2):
            number = chip * 2 + core
            for tensor in range(2):
                tile = pieces(tensor, core, chip)[0:8]
                start = (tensor * 2 * chips + number) * piece
                gather(0, place(tile, start, piece, depth), row < 6)
            tile = pieces(own, core, chip)
            for part in range(2):
                found = place(tile[0:8], part * width + number * piece, piece, depth)
                gather(1, found, row == 6 + part)
            for part in range(4):
                found = place(tile[8:16], (number * 4 + part) * piece, piece, depth)
                gather(2, found, row == part)
    for index in range(depth // 128):
        lanes = slice(index * 128, (index + 1) * 128)
        target[0:8, lanes] = tiles[0][index]
        target[8:9, lanes] = jnp.sum(tiles[1][index], 0, keepdims=True)
        for up in range(2):
            value = tiles[2][up * (depth // 128) + index]
            target[9 + up : 10 + up, lanes] = jnp.sum(value, 0, keepdims=True)


def cut_vectors(source, piece, chips, own, write):
    depth = source.shape[1]
    width = depth // 2
    row = lax.broadcasted_iota(jnp.int32, (8, 128), 0)
    for chip in range(chips):
        for core in range(2):
            number = chip * 2 + core
            upper = jnp.zeros((8, 128), F32)
            for part in range(2):
                start = part * width + number * piece
                found = take(lambda n: source[8:9, n * 128 : n * 128 + 128], start, piece)
                upper = jnp.where(row == 6 + part, found, upper)
            lower = jnp.zeros((8, 128), F32)
            for part in range(4):
                up, start = divmod((number * 4 + part) * piece, depth)
                found = take(
                    lambda n: source[9 + up : 10 + up, n * 128 : n * 128 + 128], start, piece
                )
                lower = jnp.where(row == part, found, lower)
            for tensor in range(2):
                start = (tensor * 2 * chips + number) * piece
                wide = take(lambda n: source[0:8, n * 128 : n * 128 + 128], start, piece)
                mine = jnp.where(own == tensor, 1.0, 0.0)
                write(
                    tensor,
                    core,
                    chip,
                    jnp.where(row < 6, wide, upper * mine),
                    lower * mine,
                )


def add_rows(target, sources, step):
    rows = target.shape[0]

    @pl.loop(0, rows // step)
    def _(index):
        here = pl.ds(pl.multiple_of(index * step, 8), step)
        total = target[here, :]
        for source in sources:
            total = total + source[here, :]
        target[here, :] = total


Q, O, U, D = range(4)

VIA_OWN, BOTH, VIA_OTHER = range(3)

(START, LAYER, MIXED, TOKENS, MIDDLE, SECOND, SECONDS, HIDDEN, RESULT) = range(0, 72, 8)
(GRADS, PRODUCTS, PRODUCT_UP, HEADS, MIDDLES, PRODUCT_OUT, REST, ENDING) = range(72, 136, 8)

OWN, SPREAD, OVER_Z, OVER_X = range(4)
CORE, SEND, ADD, RELAY, SUM, LAST = range(6)
GATHER = (
    (VIA_OWN, VIA_OWN, VIA_OTHER, VIA_OWN),
    (VIA_OWN, VIA_OWN, VIA_OTHER, VIA_OWN),
)

PASS_ON = (
    {
        (0, START): (
            (OWN, 0, U), (OWN, 0, D), (OWN, 0, O), (OWN, 0, Q), (SPREAD, 0, Q),
            (OVER_Z, 0, Q, 0), (SPREAD, 0, O), (OVER_Z, 0, O, 0), (OVER_Z, 0, Q, 2),
        ),
        (0, LAYER): (
            (OVER_Z, 0, Q, 1), (OVER_Z, 0, O, 1), (SPREAD, 0, D), (OVER_Z, 0, O, 2),
        ),
        (0, MIDDLE + 0): (
            (OVER_Z, 0, D, 0), (OVER_X, 1, Q, 1), (OVER_X, 0, U, 0), (OVER_X, 1, O, -1),
            (OVER_X, 1, Q, 0), (OVER_Z, 0, D, 1), (OVER_Z, 0, D, 2),
        ),
        (0, MIDDLE + 1): (
            (OVER_X, 1, Q, -1), (OVER_X, 0, U, 2), (OVER_X, 1, U, -1),
        ),
        (0, SECOND): (
            (OVER_X, 0, U, 1),
        ),
        (0, RESULT + 0): (
            (OVER_Z, 1, U, 0), (OVER_X, 1, O, 1), (OVER_X, 1, O, 0), (OVER_X, 1, O, 2),
        ),
        (1, LAYER): (
            (OVER_X, 1, Q, 2),
        ),
        (1, TOKENS + 0): (
            (OVER_Z, 1, U, 2),
        ),
        (1, TOKENS + 1): (
            (OVER_X, 1, D, -1),
        ),
        (1, MIDDLE + 0): (
            (OVER_Z, 1, U, 1), (OVER_X, 1, D, 2),
        ),
        (1, HIDDEN): (
            (OVER_X, 1, D, 1), (OVER_X, 1, D, 0),
        ),
    },
    {
        (0, START): (
            (SPREAD, 1, Q), (OWN, 1, D), (OWN, 1, U), (OVER_X, 0, U, -1),
            (OVER_Z, 1, Q, 0), (SPREAD, 1, O), (OVER_Z, 1, Q, 1), (OWN, 1, Q),
        ),
        (0, LAYER): (
            (OVER_Z, 0, U, 0), (OVER_X, 0, O, -1), (OVER_X, 0, Q, 2), (OVER_Z, 0, U, 2),
            (SPREAD, 1, D), (OVER_X, 0, Q, 1), (OWN, 1, O), (OVER_X, 0, Q, -1),
            (OVER_X, 0, Q, 0), (OVER_X, 0, O, 1), (OVER_X, 0, O, 0), (OVER_X, 0, D, -1),
            (OVER_Z, 0, U, 1), (OVER_X, 0, O, 2),
        ),
        (0, MIDDLE + 1): (
            (OVER_Z, 1, O, 1),
        ),
        (0, SECOND): (
            (OVER_Z, 1, O, 0), (OVER_Z, 1, Q, 2),
        ),
        (0, SECONDS + 1): (
            (OVER_X, 0, D, 1), (OVER_X, 0, D, 0), (OVER_Z, 1, O, 2), (OVER_Z, 1, D, 0),
            (OVER_X, 0, D, 2),
        ),
        (0, RESULT + 0): (
            (OVER_Z, 1, D, 2),
        ),
        (1, MIXED): (
            (OVER_X, 1, U, 0),
        ),
        (1, TOKENS + 0): (
            (OVER_Z, 1, D, 1),
        ),
        (1, MIDDLE + 0): (
            (OVER_X, 1, U, 1), (OVER_X, 1, U, 2),
        ),
    },
)


def forward_kernel(
    chips,
    seq,
    sent_rows,
    x_in,
    live,
    vec_in,
    wq,
    wo,
    wu,
    wd,
    out_all,
    vec,
    hs,
    mid,
    gq_out,
    go_out,
    gu_out,
    gd_out,
    n1_out,
    n2_out,
    joined_out,
    mixed_out,
    pre_out,
    gq,
    go,
    gu,
    gd,
    n1,
    n2,
    joined,
    mixed,
    pre,
    hidden,
    received,
    sending,
    pieces,
    y_send,
    y_recv,
    v_send,
    v_recv,
    zs,
    zr,
    xs,
    xr,
    cs,
    cr,
    local,
    save,
):
    here = Place(chips)
    s, c, z = here.s, here.c, here.z
    shards = (wq, wo, wu, wd)
    whole = (gq, go, gu, gd)
    block = wo.shape[0]
    rows, depth = hs.shape[1:]
    width = go.shape[2]
    tail = rows - sent_rows
    parts = parts_of(rows)
    for buffer in (n1, n2):
        for layer in range(2):
            buffer[layer, 1, sent_rows:rows, :] = jnp.zeros((tail, depth), F32)
    for index in range(received.shape[0]):
        received[index, sent_rows:rows, :] = jnp.zeros((tail, depth), F32)
    here.greet()


    def spot(matrix, layer, back, core=None):
        start = (here.z_at(-back) * 2 + (c if core is None else core)) * block
        span = pl.ds(pl.multiple_of(start, 8), block)
        if matrix == Q:
            return whole[matrix].at[layer, :, span, :]
        return whole[matrix].at[layer, span, :]

    def z_copy(layer, matrix, step, src=None):
        place = spot(matrix, layer, 0)
        return remote(
            place if src is None else src,
            place,
            zs.at[layer, matrix, step],
            zr.at[layer, matrix, step],
            here.z_peer(step),
        )

    def z_relay(layer, matrix):
        place = spot(matrix, layer, 2)
        step = jnp.where(z == 1, 3, 1)
        return remote(
            place,
            place,
            zs.at[layer, matrix, 0],
            zr.at[layer, matrix, 4 - step],
            here.z_peer(step),
        )

    def x_copy(layer, matrix, back, src=None):
        place = spot(matrix, layer, back)
        return remote(
            place if src is None else src,
            place,
            xs.at[layer, matrix, back],
            xr.at[layer, matrix, back],
            here.x_peer,
        )

    def c_copy(layer, matrix, back, src=None):
        place = spot(matrix, layer, back)
        return remote(
            place if src is None else src,
            place,
            cs.at[layer, matrix, back],
            cr.at[layer, matrix, back],
            here.core_peer,
        )

    def landed(place, sem):
        pltpu.make_async_copy(place, place, sem).wait()

    def z_spread(layer, matrix, src=None):
        for step in [2, 1, 3] if here.relays else range(1, chips):
            when(here.direct(step), z_copy(layer, matrix, step, src).start)

    count = chips - 1

    def act(section, event):
        kind, layer, matrix, *third = event
        own = section == layer
        path = GATHER[layer][matrix]
        if kind == OWN:
            x_copy(layer, matrix, 0, shards[matrix]).start()
        elif kind == SPREAD:
            z_spread(layer, matrix, shards[matrix])
        elif third[0] < 0:
            landed(spot(matrix, layer, 0), xr.at[layer, matrix, 0])
            if path != VIA_OWN:
                z_spread(layer, matrix)
            c_copy(layer, matrix, 0).start()
        else:
            for number in range(count * third[0] // 3, count * (third[0] + 1) // 3):
                back = here.arrivals()[number]
                place = spot(matrix, layer, back)
                if kind == OVER_X:
                    landed(place, xr.at[layer, matrix, back])
                else:
                    landed(place, zr.at[layer, matrix, back])
                    if here.relays and number == 0:
                        pl.when(here.middle)(z_relay(layer, matrix).start)
                    if path == (VIA_OWN if own else VIA_OTHER):
                        x_copy(layer, matrix, back).start()
                c_copy(layer, matrix, back).start()

    def point(layer, name):
        for section in range(2):
            events = PASS_ON[section].get((layer, name))
            if events:

                @pl.when(s == section)
                def _():
                    for event in events:
                        act(section, event)

    piece = depth // (4 * chips)
    pieces[here.t, c, s, z] = vec_in[...]
    copy = remote(
        pieces.at[here.t, c, s, z],
        pieces.at[here.t, c, s, z],
        v_send.at[0],
        v_recv.at[0],
        here.x_peer,
    )
    copy.start()
    copy.wait_send()
    landed(pieces.at[here.t, c, 1 - s, z], v_recv.at[0])
    vector_copies = []
    for step in range(1, chips):
        place_ = pieces.at[here.t, c, :, z]
        copy = remote(
            place_, place_, v_send.at[step], v_recv.at[step], here.z_peer(step)
        )
        copy.start()
        vector_copies.append(copy)
    own_copies = []
    for matrix in range(4):
        c_copy(s, matrix, 0, shards[matrix]).start()
        copy = pltpu.make_async_copy(
            shards[matrix], spot(matrix, s, 0), local.at[matrix]
        )
        copy.start()
        own_copies.append(copy)
    point(0, START)
    for step in range(1, chips):
        vector_copies[step - 1].wait_send()
        landed(pieces.at[here.t, c, :, here.z_at(-step)], v_recv.at[step])
    place_ = pieces.at[here.t, c]
    copy = remote(place_, place_, v_send.at[chips], v_recv.at[chips], here.y_peer)
    copy.start()
    copy.wait_send()
    landed(pieces.at[1 - here.t, c], v_recv.at[chips])
    place_ = pieces.at[:, c]
    copy = remote(
        place_, place_, v_send.at[chips + 1], v_recv.at[chips + 1], here.core_peer
    )
    copy.start()
    copy.wait_send()
    landed(pieces.at[:, 1 - c], v_recv.at[chips + 1])
    for layer in range(2):
        spread_vectors(
            vec.at[layer],
            lambda tensor, core, chip: pieces[tensor, core, layer, chip],
            piece,
            chips,
            here.t,
        )

    saves = {}

    def keep(name, src, dst, sem):
        copy = pltpu.make_async_copy(src, dst, save.at[sem])
        copy.start()
        saves[name] = copy

    def before_write(name):
        if name in saves:
            saves.pop(name).wait()

    def finish(layer, matrix):
        pl.when(s == layer)(own_copies[matrix].wait)
        for back in range(chips):
            landed(spot(matrix, layer, back, 1 - c), cr.at[layer, matrix, back])
        if matrix == Q:
            for part in range(3):
                keep(
                    "whole%d%d%d" % (layer, matrix, part),
                    whole[matrix].at[layer, part],
                    gq_out.at[layer, :, pl.ds(part * width, width)],
                    22 + 3 * layer + part,
                )
        else:
            keep(
                "whole%d%d" % (layer, matrix),
                whole[matrix].at[layer],
                (None, go_out, gu_out, gd_out)[matrix].at[layer],
                14 + 4 * layer + matrix,
            )

    exchanges = {}

    def y_start(src, dst, index, part):
        start, stop = parts[part]
        span = pl.ds(start, min(stop, sent_rows) - start)
        copy = remote(
            src.at[span],
            dst.at[span],
            y_send.at[index, part],
            y_recv.at[index, part],
            here.y_peer,
        )
        copy.start()
        exchanges[index, part] = copy

    def y_wait(index, part):
        exchanges[index, part].wait_recv()

    def y_departed(index):
        for part in range(2):
            exchanges.pop((index, part)).wait_send()

    def begin(layer, part, value):
        span = slice(*parts[part])
        hs[layer, span] = value
        unit, _ = normalize(value)
        vectors = Vectors(vec.at[layer], width, None)
        n1[layer, 0, span] = unit * vectors.gain(0) + vectors.shift(0)
        y_start(n1.at[layer, 0], n1.at[layer, 1], 4 * layer, part)

    def project(layer, image, span):
        vectors = Vectors(vec.at[layer], width, None)
        for piece in range(3):
            lanes = slice(piece * width, (piece + 1) * width)
            value = dot(n1[layer, image, span], gq[layer, piece], 1, 0)
            if piece == 0:
                value = value + vectors.query()
            if piece == 2:
                value = value + vectors.value()
            joined[image, span, lanes] = value

    def expand(layer, image, span):
        vectors = Vectors(vec.at[layer], width, None)
        for piece in range(pre.shape[2] // depth):
            lanes = slice(piece * depth, (piece + 1) * depth)
            value = dot(n2[layer, image, span], gu[layer, :, lanes], 1, 0)
            value = value + vectors.up(piece)
            pre[image, span, lanes] = value
            hidden[image, span, lanes] = value * phi_big(value)

    everything = slice(0, rows)
    for part in range(2):
        start, stop = parts[part]
        if stop > seq:
            hs[0, seq // 8 * 8 : rows] = jnp.zeros((rows - seq // 8 * 8, depth), F32)
            hs[0, start:seq] = x_in[start:seq]
            begin(0, part, hs[0, start:stop])
        else:
            begin(0, part, x_in[start:stop])
    for layer in range(2):
        vectors = Vectors(vec.at[layer], width, None)
        point(layer, LAYER)
        before_write("joined")
        before_write("mixed")
        finish(layer, Q)
        project(layer, 0, everything)
        attend(joined.at[0], mixed.at[0], seq)
        point(layer, MIXED)
        finish(layer, O)
        mid[layer] = hs[layer] + dot(mixed[0], go[layer], 1, 1) + vectors.shift(2)
        for part in range(2):
            point(layer, TOKENS + part)
            y_wait(4 * layer, part)
            project(layer, 1, slice(*parts[part]))
        attend(joined.at[1], mixed.at[1], seq)
        if layer == 1:
            y_departed(1)
        for part in range(2):
            span = slice(*parts[part])
            sending[0, span] = dot(mixed[1, span], go[layer], 1, 1)
            y_start(sending.at[0], received.at[2 * layer], 4 * layer + 1, part)
        keep("n1%d" % layer, n1.at[layer], n1_out.at[layer], 4 + layer)
        keep("joined", joined, joined_out.at[layer], 6 + layer)
        keep("mixed", mixed, mixed_out.at[layer], 8 + layer)
        for part in range(2):
            span = slice(*parts[part])
            point(layer, MIDDLE + part)
            y_wait(4 * layer + 1, part)
            middle = mid[layer, span] + received[2 * layer, span]
            mid[layer, span] = middle
            unit, _ = normalize(middle)
            n2[layer, 0, span] = unit * vectors.gain(1) + vectors.shift(1)
            y_start(n2.at[layer, 0], n2.at[layer, 1], 4 * layer + 2, part)
        point(layer, SECOND)
        before_write("pre")
        finish(layer, U)
        expand(layer, 0, everything)
        if layer == 0:
            for part in range(2):
                point(0, SECONDS + part)
                y_wait(2, part)
                expand(0, 1, slice(*parts[part]))
        else:
            y_departed(3)
        point(layer, HIDDEN)
        finish(layer, D)
        if layer == 1:
            out_all[layer] = mid[layer] + dot(hidden[0], gd[layer], 1, 1)
        for part in range(2):
            span = slice(*parts[part])
            if layer == 1:
                point(1, SECONDS + part)
                y_wait(6, part)
                expand(1, 1, span)
            sending[1, span] = dot(hidden[1, span], gd[layer], 1, 1)
            y_start(sending.at[1], received.at[2 * layer + 1], 4 * layer + 3, part)
        if layer == 0:
            out_all[layer] = mid[layer] + dot(hidden[0], gd[layer], 1, 1)
        keep("n2%d" % layer, n2.at[layer], n2_out.at[layer], 10 + layer)
        keep("pre", pre, pre_out.at[layer], 12 + layer)
        for part in range(2):
            span = slice(*parts[part])
            point(layer, RESULT + part)
            y_wait(4 * layer + 3, part)
            result = out_all[layer, span] + received[2 * layer + 1, span]
            result = (result + vectors.shift(3)) * live[span, 0:1]
            out_all[layer, span] = result
            if layer == 0:
                begin(1, part, result)

    for copy in saves.values():
        copy.wait()
    for copy in exchanges.values():
        copy.wait_send()
    def z_departures(layer, matrix):
        for step in range(1, chips):
            when(here.direct(step), z_copy(layer, matrix, step).wait_send)
        if here.relays:
            pl.when(here.middle)(z_relay(layer, matrix).wait_send)

    def departures(section):
        for layer in range(2):
            for matrix in range(4):
                path = GATHER[layer][matrix]
                own = section == layer
                if own:
                    x_copy(layer, matrix, 0).wait_send()
                if path == (VIA_OWN if own else VIA_OTHER):
                    for back in range(1, chips):
                        x_copy(layer, matrix, back).wait_send()
                if path != (VIA_OTHER if own else VIA_OWN):
                    z_departures(layer, matrix)

    for section in range(2):
        pl.when(s == section)(functools.partial(departures, section))
    for layer in range(2):
        for matrix in range(4):
            for back in range(chips):
                c_copy(layer, matrix, back).wait_send()


def forward(chips, rows, x_in, live, vec_in, wq, wo, wu, wd):
    seq, depth = x_in.shape
    sent_rows = up_to(seq, 8)
    width = wo.shape[1]
    hidden = wu.shape[1]
    widths = (3 * width, width, hidden, hidden)
    whole = [(2, depth, w) for w in widths]
    any_space = pl.BlockSpec(memory_space=pl.ANY)
    vmem = pl.BlockSpec(memory_space=pltpu.VMEM)
    both = (2, 16, depth)
    outs = [
        ((2, rows, depth), vmem),
        (both, vmem),
        ((2, rows, depth), vmem),
        ((2, rows, depth), vmem),
        *[(w, any_space) for w in whole],
        ((2, 2, rows, depth), any_space),
        ((2, 2, rows, depth), any_space),
        ((2, 2, rows, 3 * width), any_space),
        ((2, 2, rows, width), any_space),
        ((2, 2, rows, hidden), any_space),
    ]
    sems = pltpu.SemaphoreType.DMA
    scratch = [
        pltpu.VMEM((2, 3, depth, width), F32),
        *[pltpu.VMEM(w, F32) for w in whole[1:]],
        pltpu.VMEM((2, 2, rows, depth), F32),
        pltpu.VMEM((2, 2, rows, depth), F32),
        pltpu.VMEM((2, rows, 3 * width), F32),
        pltpu.VMEM((2, rows, width), F32),
        pltpu.VMEM((2, rows, hidden), F32),
        pltpu.VMEM((2, rows, hidden), F32),
        pltpu.VMEM((4, rows, depth), F32),
        pltpu.VMEM((2, rows, depth), F32),
        pltpu.VMEM((2, 2, 2, chips) + vec_in.shape, F32),
        sems((8, 2)),
        sems((8, 2)),
        sems((chips + 2,)),
        sems((chips + 2,)),
        *[sems((2, 4, chips)) for _ in range(6)],
        sems((4,)),
        sems((28,)),
    ]
    return pl.pallas_call(
        functools.partial(forward_kernel, chips, seq, sent_rows),
        out_shape=[jax.ShapeDtypeStruct(shape, F32) for shape, _ in outs],
        in_specs=[vmem] * 3 + [any_space] * 4,
        out_specs=[spec for _, spec in outs],
        scratch_shapes=scratch,
        compiler_params=pltpu.CompilerParams(
            collective_id=0, has_side_effects=True, vmem_limit_bytes=VMEM_BYTES
        ),
        name="forward_both",
    )(x_in, live, vec_in, wq, wo, wu, wd)


SUMS = (
    (VIA_OTHER, VIA_OWN, BOTH, VIA_OWN),
    (VIA_OTHER, VIA_OWN, VIA_OWN, BOTH),
)

SUM_UP = (
    {
        (1, MIDDLE + 0): (
            (CORE, 1, D),
        ),
        (1, MIDDLE + 1): (
            (SEND, 1, D), (CORE, 1, U), (SEND, 1, U),
        ),
        (1, RESULT + 0): (
            (CORE, 1, O), (SEND, 1, O), (RELAY, 1, D), (CORE, 1, Q),
        ),
        (0, GRADS + 0): (
            (SEND, 1, Q), (ADD, 1, Q, 0),
        ),
        (0, PRODUCTS): (
            (ADD, 1, Q, 1),
        ),
        (0, MIDDLE + 0): (
            (ADD, 1, Q, 2), (RELAY, 1, Q),
        ),
        (0, MIDDLE + 1): (
            (CORE, 0, D),
        ),
        (0, HEADS): (
            (SEND, 0, D), (CORE, 0, U),
        ),
        (0, MIDDLES + 0): (
            (SEND, 0, U),
        ),
        (0, MIDDLES + 1): (
            (SUM, 1, D),
        ),
        (0, REST): (
            (RELAY, 0, U), (CORE, 0, O),
        ),
        (0, RESULT + 0): (
            (ADD, 0, D, 0),
        ),
        (0, RESULT + 1): (
            (SEND, 0, O), (CORE, 0, Q), (SEND, 0, Q), (SUM, 1, Q), (ADD, 0, D, 3),
            (ADD, 0, D, 1), (ADD, 0, O, 0),
        ),
        (0, ENDING + 2): (
            (SUM, 0, U), (ADD, 0, D, 2), (RELAY, 0, D),
        ),
        (0, ENDING + 4): (
            (ADD, 0, O, 2), (LAST, 0, U), (RELAY, 0, O), (SUM, 0, D), (ADD, 0, O, 1),
            (ADD, 0, O, 3), (SUM, 0, O), (LAST, 0, Q),
        ),
    },
    {
        (1, MIDDLE + 0): (
            (CORE, 1, D),
        ),
        (1, HEADS): (
            (SEND, 1, D),
        ),
        (1, MIDDLES + 1): (
            (CORE, 1, U), (SEND, 1, U),
        ),
        (1, REST): (
            (CORE, 1, O),
        ),
        (1, RESULT + 0): (
            (SEND, 1, O), (ADD, 1, U, 0), (CORE, 1, Q), (SEND, 1, Q),
        ),
        (0, LAYER): (
            (RELAY, 1, D), (ADD, 1, U, 1),
        ),
        (0, MIDDLE + 0): (
            (CORE, 0, D), (ADD, 1, U, 2), (RELAY, 1, U), (SEND, 0, D), (SUM, 1, D),
        ),
        (0, MIDDLE + 1): (
            (ADD, 1, U, 3),
        ),
        (0, MIDDLES + 1): (
            (CORE, 0, U), (SEND, 0, U), (ADD, 1, O, 0),
        ),
        (0, REST): (
            (CORE, 0, O), (SEND, 0, O), (CORE, 0, Q), (RELAY, 0, U), (ADD, 1, O, 3),
            (LAST, 1, D),
        ),
        (0, RESULT + 0): (
            (SEND, 0, Q), (ADD, 0, Q, 0), (ADD, 0, Q, 1),
        ),
        (0, ENDING + 1): (
            (SUM, 0, U), (ADD, 0, Q, 2), (RELAY, 0, Q),
        ),
        (0, ENDING + 2): (
            (LAST, 1, Q), (SUM, 1, U), (ADD, 1, O, 2), (RELAY, 1, O),
        ),
        (0, ENDING + 3): (
            (SUM, 0, Q),
        ),
        (0, ENDING + 4): (
            (ADD, 1, O, 1), (SUM, 1, O),
        ),
    },
)


def slots_of(matrix, chips):
    slots = {}
    counts = [0, 0]
    for layer in range(2):
        path = SUMS[layer][matrix]
        slots[layer, layer] = counts[layer]
        counts[layer] += chips if path == VIA_OWN else 1
        if path == VIA_OTHER:
            slots[1 - layer, layer] = counts[1 - layer] - 1
            counts[1 - layer] += chips - 1
    return slots, max(counts)


def backward_kernel(
    chips,
    seq,
    sent_rows,
    cot,
    live,
    vec,
    out_all,
    hs_in,
    mid_in,
    gq_in,
    go_in,
    gu_in,
    gd_in,
    n1_in,
    n2_in,
    joined_in,
    mixed_in,
    pre_in,
    vec_out,
    outq,
    outo,
    outu,
    outd,
    gin_both,
    out_both,
    rcq,
    rco,
    rcu,
    rcd,
    rzq,
    rzo,
    rzu,
    rzd,
    gin,
    gvec,
    wb,
    wu,
    before,
    normed,
    joined,
    mixed,
    pre,
    hidden,
    grad_all,
    mid_all,
    received,
    sending,
    own_part,
    grad_mixed,
    grad_joined,
    aq,
    ao,
    au,
    ad,
    rxq,
    rxo,
    rxu,
    rxd,
    tile,
    fetched,
    single,
    cut,
    vc,
    vy,
    vz,
    vx,
    y_send,
    y_recv,
    loads,
    cs,
    cl,
    cr,
    xs,
    xr,
    zs,
    zr,
    fetch_sem,
    single_sem,
    v_send,
    v_recv,
    g_send,
    g_recv,
    g_own,
):
    here = Place(chips)
    s, c, z = here.s, here.c, here.z
    rows, depth = cot.shape
    width = mixed.shape[2]
    width_ff = wu.shape[1]
    tail = rows - sent_rows
    parts = parts_of(rows)
    mine = (aq, ao, au, ad)
    from_core = (rcq, rco, rcu, rcd)
    from_x = (rxq, rxo, rxu, rxd)
    x_slots = [slots_of(matrix, chips)[0] for matrix in range(4)]
    from_z = (rzq, rzo, rzu, rzd)
    outs = (outq, outo, outu, outd)
    block = outo.shape[0]
    small = 24 if block % 24 == 0 else block
    for buffer in (grad_all, mid_all):
        buffer[1, sent_rows:rows, :] = jnp.zeros((tail, depth), F32)
    for index in range(received.shape[0]):
        received[index, sent_rows:rows, :] = jnp.zeros((tail, depth), F32)
    gvec[...] = jnp.zeros(gvec.shape, F32)

    wq, wo = wb.at[:, 0 : 3 * width], wb.at[:, 3 * width : 4 * width]
    sources = dict(
        wd=(gd_in, wb),
        pre=(pre_in, pre),
        wu=(gu_in, wu),
        n2=(n2_in, normed),
        mid=(mid_in, before),
        joined=(joined_in, joined),
        mixed=(mixed_in, mixed),
        n1=(n1_in, normed),
        hs=(hs_in, before),
        wo=(go_in, wo),
        wq=(gq_in, wq),
    )
    order = list(sources)
    loading = {}

    def load(name, layer):
        src, dst = sources[name]
        copy = pltpu.make_async_copy(src.at[layer], dst, loads.at[order.index(name)])
        copy.start()
        loading[name] = copy

    def loaded(name):
        loading.pop(name).wait()

    for name in order[:-2]:
        if name not in ("hs", "n1"):
            load(name, 1)
    cot_copy = pltpu.make_async_copy(cot, own_part, loads.at[len(order)])
    cot_copy.start()
    here.greet()
    departing = []

    def launch(copy):
        copy.start()
        departing.append(copy)
        return copy

    def departed(copy):
        copy.wait_send()
        departing[:] = [item for item in departing if item is not copy]

    exchanges = {}

    def y_start(src, dst, index, part):
        start, stop = parts[part]
        span = pl.ds(start, min(stop, sent_rows) - start)
        copy = remote(
            src.at[span],
            dst.at[span],
            y_send.at[index, part],
            y_recv.at[index, part],
            here.y_peer,
        )
        copy.start()
        exchanges[index, part] = copy

    def y_wait(index, part):
        exchanges[index, part].wait_recv()

    def y_departed(index):
        for part in range(2):
            exchanges.pop((index, part)).wait_send()

    def gin_copy():
        return remote(
            gin.at[1 - s], gin_both.at[s], g_send.at[1], g_recv.at[1], here.x_peer
        )

    out_copy = launch(
        remote(
            out_all.at[1 - s], out_both.at[s], g_send.at[0], g_recv.at[0], here.x_peer
        )
    )
    own_out = pltpu.make_async_copy(out_all.at[s], out_both.at[s], g_own.at[0])
    own_out.start()


    def tile_copies(slot, matrix, layer, number, start, size, step):
        lanes = pl.ds(start, size)
        spots = []
        for core in (1 - c, c):
            first = pl.multiple_of((here.z_at(step) * 2 + core) * block, 8)
            spots.append(tile.at[slot, pl.ds(first, block), pl.ds(0, size)])
        return (
            remote(
                spots[0],
                from_core[matrix].at[layer, step, :, lanes],
                cs.at[slot, step],
                cr.at[layer, matrix, number, step],
                here.core_peer,
            ),
            pltpu.make_async_copy(
                spots[1], mine[matrix].at[layer, step, :, lanes], cl.at[slot, step]
            ),
        )

    in_slot = [[None, None], [None, None]]
    next_slot = [0]

    def settle(section, slot):
        what = in_slot[section][slot]
        if what is not None:
            in_slot[section][slot] = None

            @pl.loop(0, chips)
            def _(step):
                away, kept = tile_copies(slot, *what, step)
                away.wait_send()
                kept.wait()

    def settle_all(slot):
        if in_slot[0][slot] == in_slot[1][slot]:
            settle(0, slot)
            in_slot[1][slot] = None
        for section in range(2):
            if in_slot[section][slot] is not None:
                pl.when(s == section)(functools.partial(settle, section, slot))

    def tiles_of(matrix):
        size = width if matrix < 2 else depth
        return [(n, n * size, size) for n in range(mine[matrix].shape[3] // size)]

    def flat(ref):
        return ref[...].reshape(2 * rows, ref.shape[-1])

    def product(matrix, layer, left, right):
        both = flat(left)
        for number, start, size in tiles_of(matrix):
            slot = next_slot[0]
            next_slot[0] = 1 - slot
            settle_all(slot)
            piece = right[:, :, start : start + size].reshape(2 * rows, size)
            tile[slot, :, 0:size] = dot(both, piece, 0, 0)
            what = (matrix, layer, number, start, size)

            @pl.loop(0, chips)
            def _(step):
                away, kept = tile_copies(slot, *what, step)
                away.start()
                kept.start()

            in_slot[0][slot] = in_slot[1][slot] = what

    def fetch(slot, src):
        spot = single.at[slot, :, pl.ds(0, src.shape[1])]
        copy = pltpu.make_async_copy(src, spot, single_sem.at[slot])
        copy.start()
        return copy, spot

    def add_from(src, target):
        copy, spot = fetch(0, src)
        copy.wait()
        add_rows(target, [spot], small)

    def x_slot(matrix, layer, step):
        to_own = SUMS[layer][matrix] == VIA_OWN or (isinstance(step, int) and step == 0)
        section = layer if to_own else 1 - layer
        return x_slots[matrix][section, layer] + step

    def x_grad(matrix, layer, step):
        return remote(
            mine[matrix].at[layer, step],
            from_x[matrix].at[x_slot(matrix, layer, step)],
            xs.at[layer, matrix, step],
            xr.at[layer, matrix, step],
            here.x_peer,
        )

    def z_grad(matrix, layer, step):
        return remote(
            mine[matrix].at[layer, step],
            from_z[matrix].at[layer, step],
            zs.at[layer, matrix, step],
            zr.at[layer, matrix, step],
            here.z_peer(step),
        )

    def z_left(matrix, layer):
        far = here.departures()[0]
        return remote(
            mine[matrix].at[layer, far],
            from_z[matrix].at[layer, 0],
            zs.at[layer, matrix, far],
            zr.at[layer, matrix, 0],
            here.z_peer(4 - far),
        )

    def z_out(matrix, layer, number):
        step = here.departures()[number]
        if not here.relays:
            if step:
                z_grad(matrix, layer, step).start()
        elif number == 0:
            pl.when(here.middle)(z_grad(matrix, layer, step).start)
            pl.when(~here.middle)(z_left(matrix, layer).start)
        elif number == 1:
            z_grad(matrix, layer, step).start()
        elif number == 2:
            pl.when(~here.middle)(z_grad(matrix, layer, step).start)

    def core(section, layer, matrix):
        for slot in range(2):
            what = in_slot[section][slot]
            if what is not None and what[:2] == (matrix, layer):
                settle(section, slot)
        for what in tiles_of(matrix):

            @pl.loop(0, chips)
            def _(step):
                tile_copies(0, matrix, layer, *what, step)[0].wait_recv()

        lanes = pl.ds(0, mine[matrix].shape[3])
        pltpu.make_async_copy(
            from_core[matrix].at[layer], fetched.at[:, :, lanes], fetch_sem
        ).start()

    def send(section, layer, matrix):
        lanes = pl.ds(0, mine[matrix].shape[3])
        pltpu.make_async_copy(
            from_core[matrix].at[layer], fetched.at[:, :, lanes], fetch_sem
        ).wait()
        path = SUMS[layer][matrix]
        for number, step in enumerate(here.departures()):
            add_rows(mine[matrix].at[layer, step], [fetched.at[step, :, lanes]], small)
            if path == BOTH:
                z_out(matrix, layer, number)
            elif path == VIA_OWN and section != layer:
                x_grad(matrix, layer, step).start()
            elif path == VIA_OTHER and section == layer and number < chips - 1:
                x_grad(matrix, layer, step).start()

    def add(section, layer, matrix, group):
        steps = here.departures()
        count, groups = (chips, 4) if section == layer else (chips - 1, 3)
        for number in range(count * group // groups, count * (group + 1) // groups):
            step = steps[number]
            x_grad(matrix, layer, step).wait_recv()
            block_in = from_x[matrix].at[x_slot(matrix, layer, step)]
            add_rows(mine[matrix].at[layer, step], [block_in], small)
            z_out(matrix, layer, number)

    def relay(section, layer, matrix):
        if here.relays:

            @pl.when(here.middle)
            def _():
                z_left(matrix, layer).wait_recv()
                add_from(from_z[matrix].at[layer, 0], mine[matrix].at[layer, 2])
                z_grad(matrix, layer, 2).start()

    def sum_z(section, layer, matrix):
        target = mine[matrix].at[layer, 0]

        def several(steps):
            fetched_now = []
            for slot, step in enumerate(steps):
                z_grad(matrix, layer, step).wait_recv()
                fetched_now.append(fetch(slot, from_z[matrix].at[layer, step]))
            for copy, _ in fetched_now:
                copy.wait()
            add_rows(target, [spot for _, spot in fetched_now], small)

        steps = here.departures()[:-1]
        if here.relays:
            pl.when(here.middle)(lambda: several([steps[0], 2, steps[1]]))
            pl.when(~here.middle)(lambda: several([steps[0], 2]))
        else:
            for step in steps:
                several([step])
        if section != layer:
            x_grad(matrix, layer, 0).start()

    def last(section, layer, matrix):
        x_grad(matrix, layer, 0).wait_recv()
        block_in = from_x[matrix].at[x_slot(matrix, layer, 0)]
        add_rows(mine[matrix].at[layer, 0], [block_in], small)

    actions = (core, send, add, relay, sum_z, last)

    def act(section, events):
        for name, layer, matrix, *more in events:
            actions[name](section, layer, matrix, *more)

    def point(layer, name):
        for section in range(2):
            events = SUM_UP[section].get((layer, name))
            if events:
                pl.when(s == section)(functools.partial(act, section, events))

    def total(value):
        return jnp.sum(value, 0, keepdims=True)

    def note(layer, row, value):
        gvec[layer, row : row + 1, :] = gvec[layer, row : row + 1, :] + total(value)

    def begin(layer, part, value):
        span = slice(*parts[part])
        grad_all[0, span] = value
        y_start(grad_all.at[0], grad_all.at[1], 4 * (1 - layer), part)
        note(layer, 5, value)

    def contract(layer, image, span):
        for piece in range(width_ff // depth):
            lanes = slice(piece * depth, (piece + 1) * depth)
            grad_hidden = dot(grad_all[image, span], wb[:, lanes], 1, 0)
            value = pre[image, span, lanes]
            upper = phi_big(value)
            hidden[image, span, lanes] = value * upper
            pre[image, span, lanes] = grad_hidden * (upper + value * phi_small(value))

    everything = slice(0, rows)
    cot_copy.wait()
    for part in range(2):
        span = slice(*parts[part])
        begin(1, part, own_part[span] * live[span, 0:1])
    for layer in (1, 0):
        vectors = Vectors(vec.at[layer], width, None)
        base = 4 * (1 - layer)
        point(layer, LAYER)
        loaded("wd")
        loaded("pre")
        contract(layer, 0, everything)
        loaded("wu")
        own_part[...] = dot(pre[0], wu[...], 1, 1)
        if layer == 0:
            y_departed(3)
        for part in range(2):
            span = slice(*parts[part])
            point(layer, GRADS + part)
            y_wait(base, part)
            contract(layer, 1, span)
            sending[span] = dot(pre[1, span], wu[...], 1, 1)
            y_start(sending, received.at[0], base + 1, part)
        load("wo", layer)
        load("wq", layer)
        if layer == 1:
            load("wu", 0)
        point(layer, PRODUCTS)
        product(D, layer, grad_all, hidden)
        point(layer, PRODUCT_UP)
        loaded("n2")
        product(U, layer, normed, pre)
        load("n1", layer)
        for piece in range(width_ff // depth):
            lanes = slice(piece * depth, (piece + 1) * depth)
            note(layer, 9 + piece, pre[0, :, lanes])
            note(layer, 9 + piece, pre[1, :, lanes])
        if layer == 1:
            load("pre", 0)
        loaded("mid")
        if layer == 0:
            y_departed(2)
        for part in range(2):
            span = slice(*parts[part])
            point(layer, MIDDLE + part)
            unit, inverse = normalize(before[span])
            y_wait(base + 1, part)
            grad_second = own_part[span] + received[0, span]
            grad_middle = grad_all[0, span] + normalize_back(
                grad_second * vectors.gain(1), unit, inverse
            )
            mid_all[0, span] = grad_middle
            y_start(mid_all.at[0], mid_all.at[1], base + 2, part)
            note(layer, 1, grad_second * unit)
            note(layer, 3, grad_second)
            note(layer, 4, grad_middle)
        load("hs", layer)
        point(layer, HEADS)
        loaded("wo")
        loaded("joined")
        loaded("mixed")
        grad_mixed[...] = dot(mid_all[0], wo[...], 1, 0)
        attend_back(joined.at[0], mixed.at[0], grad_mixed, grad_joined.at[0], seq)
        loaded("wq")
        own_part[...] = dot(grad_joined[0], wq[...], 1, 1)
        for part in range(2):
            span = slice(*parts[part])
            point(layer, MIDDLES + part)
            y_wait(base + 2, part)
            grad_mixed[span] = dot(mid_all[1, span], wo[...], 1, 0)
        attend_back(joined.at[1], mixed.at[1], grad_mixed, grad_joined.at[1], seq)
        y_departed(base + 1)
        for part in range(2):
            span = slice(*parts[part])
            sending[span] = dot(grad_joined[1, span], wq[...], 1, 1)
            y_start(sending, received.at[1], base + 3, part)
        if layer == 1:
            load("wd", 0)
            load("joined", 0)
        point(layer, PRODUCT_OUT)
        product(O, layer, mid_all, mixed)
        loaded("n1")
        product(Q, layer, normed, grad_joined)
        if layer == 1:
            load("mixed", 0)
            load("n2", 0)
        for image in range(2):
            for piece in (0, 2):
                lanes = slice(piece * width, (piece + 1) * width)
                spot = slice(piece // 2 * width, (piece // 2 + 1) * width)
                gvec[layer, 8:9, spot] = gvec[layer, 8:9, spot] + total(
                    grad_joined[image, :, lanes]
                )
        point(layer, REST)
        loaded("hs")
        if layer == 1:
            y_departed(0)
        for part in range(2):
            span = slice(*parts[part])
            point(layer, RESULT + part)
            unit, inverse = normalize(before[span])
            y_wait(base + 3, part)
            grad_first = own_part[span] + received[1, span]
            value = mid_all[0, span] + normalize_back(
                grad_first * vectors.gain(0), unit, inverse
            )
            gin[layer, span] = value
            if layer == 1:
                begin(0, part, value * live[span, 0:1])
            note(layer, 0, grad_first * unit)
            note(layer, 2, grad_first)
        if layer == 1:
            load("mid", 0)
            pl.when(s == 0)(gin_copy().start)
    for layer in range(2):

        def write(tensor, core, chip, upper, lower):
            step = (chip + chips - z) % chips
            cut[tensor, core, layer, step, 0:8] = upper
            cut[tensor, core, layer, step, 8:16] = lower

        cut_vectors(gvec.at[layer], depth // (4 * chips), chips, here.t, write)
    copy = launch(
        remote(cut.at[:, 1 - c], vc, v_send.at[0], v_recv.at[0], here.core_peer)
    )
    point(0, ENDING + 0)
    copy.wait_recv()
    point(0, ENDING + 1)
    cut[:, c] = cut[:, c] + vc[...]
    copy = launch(
        remote(cut.at[1 - here.t, c], vy, v_send.at[1], v_recv.at[1], here.y_peer)
    )
    point(0, ENDING + 2)
    copy.wait_recv()
    cut[here.t, c] = cut[here.t, c] + vy[...]
    copy = launch(
        remote(
            cut.at[here.t, c, 1 - s],
            vx,
            v_send.at[chips + 1],
            v_recv.at[chips + 1],
            here.x_peer,
        )
    )
    pl.when(s == 1)(gin_copy().start)
    point(0, ENDING + 3)
    copy.wait_recv()
    cut[here.t, c, s] = cut[here.t, c, s] + vx[...]
    copies = []
    for step in range(1, chips):
        copies.append(
            launch(
                remote(
                    cut.at[here.t, c, s, step],
                    vz.at[step - 1],
                    v_send.at[1 + step],
                    v_recv.at[1 + step],
                    here.z_peer(step),
                )
            )
        )
    point(0, ENDING + 4)
    for section in range(2):

        @pl.when(s == section)
        def _():
            for part in range(3):
                lanes = slice(part * width, (part + 1) * width)
                outq[part] = mine[Q][section, 0, :, lanes]
            for matrix in (O, U, D):
                outs[matrix][...] = mine[matrix][section, 0]

    total_vec = cut[here.t, c, s, 0]
    for step in range(1, chips):
        copies[step - 1].wait_recv()
        total_vec = total_vec + vz[step - 1]
    vec_out[...] = total_vec
    for slot in range(2):
        settle_all(slot)
    own_gin = pltpu.make_async_copy(gin.at[s], gin_both.at[s], g_own.at[1])
    own_gin.start()
    out_copy.wait_recv()
    gin_copy().wait()
    own_out.wait()
    own_gin.wait()
    for item in departing:
        item.wait_send()
    for item in exchanges.values():
        item.wait_send()

    def departures(section):
        for layer in range(2):
            own = section == layer
            for matrix in range(4):
                path = SUMS[layer][matrix]
                if path != (VIA_OTHER if own else VIA_OWN):
                    for step in here.departures()[:-1]:
                        z_grad(matrix, layer, step).wait_send()
                    if not own:
                        x_grad(matrix, layer, 0).wait_send()
                elif own:
                    for step in range(1, chips):
                        x_grad(matrix, layer, step).wait_send()
                else:
                    for step in range(chips):
                        x_grad(matrix, layer, step).wait_send()

    for section in range(2):
        pl.when(s == section)(functools.partial(departures, section))


def backward(chips, seq, cot, live, vec, out_all, hs, mid, whole, kept):
    rows, depth = cot.shape
    sent_rows = up_to(seq, 8)
    width, width_ff = whole[1].shape[2], whole[2].shape[2]
    widths = [w.shape[2] for w in whole]
    block = depth // (2 * chips)
    any_space = pl.BlockSpec(memory_space=pl.ANY)
    vmem = pl.BlockSpec(memory_space=pltpu.VMEM)
    outs = [
        ((16, 128), vmem),
        ((3, block, width), vmem),
        *[((block, w), vmem) for w in widths[1:]],
        ((2, rows, depth), any_space),
        ((2, rows, depth), any_space),
        *[((2, chips, block, w), any_space) for w in widths * 2],
    ]
    sems = pltpu.SemaphoreType.DMA
    scratch = [
        pltpu.VMEM((2, rows, depth), F32),
        pltpu.VMEM(vec.shape, F32),
        pltpu.VMEM((depth, width_ff), F32),
        pltpu.VMEM((depth, width_ff), F32),
        pltpu.VMEM((rows, depth), F32),
        pltpu.VMEM((2, rows, depth), F32),
        pltpu.VMEM((2, rows, 3 * width), F32),
        pltpu.VMEM((2, rows, width), F32),
        pltpu.VMEM((2, rows, width_ff), F32),
        pltpu.VMEM((2, rows, width_ff), F32),
        *[pltpu.VMEM((2, rows, depth), F32) for _ in range(3)],
        pltpu.VMEM((rows, depth), F32),
        pltpu.VMEM((rows, depth), F32),
        pltpu.VMEM((rows, width), F32),
        pltpu.VMEM((2, rows, 3 * width), F32),
        *[pltpu.VMEM((2, chips, block, w), F32) for w in widths],
        *[
            pltpu.VMEM((slots_of(matrix, chips)[1], block, w), F32)
            for matrix, w in enumerate(widths)
        ],
        pltpu.VMEM((2, depth, depth), F32),
        pltpu.VMEM((chips, block, width_ff), F32),
        pltpu.VMEM((3, block, width_ff), F32),
        pltpu.VMEM((2, 2, 2, chips, 16, 128), F32),
        pltpu.VMEM((2, 2, chips, 16, 128), F32),
        pltpu.VMEM((2, chips, 16, 128), F32),
        pltpu.VMEM((chips - 1, 16, 128), F32),
        pltpu.VMEM((chips, 16, 128), F32),
        sems((8, 2)),
        sems((8, 2)),
        sems((12,)),
        sems((2, chips)),
        sems((2, chips)),
        sems((2, 4, 3, chips)),
        *[sems((2, 4, chips)) for _ in range(4)],
        sems,
        sems((3,)),
        sems((chips + 2,)),
        sems((chips + 2,)),
        sems((2,)),
        sems((2,)),
        sems((2,)),
    ]
    results = pl.pallas_call(
        functools.partial(backward_kernel, chips, seq, sent_rows),
        out_shape=[jax.ShapeDtypeStruct(shape, F32) for shape, _ in outs],
        in_specs=[any_space] + [vmem] * 2 + [any_space] * 12,
        out_specs=[spec for _, spec in outs],
        scratch_shapes=scratch,
        compiler_params=pltpu.CompilerParams(
            collective_id=1, has_side_effects=True, vmem_limit_bytes=VMEM_BYTES
        ),
        name="backward_both",
    )(cot, live, vec, out_all, hs, mid, *whole, *kept)
    return results[:7]


def body(
    embedded,
    image_counts,
    cotangent,
    qkv_weight,
    qv_bias,
    out_weight,
    up_weight,
    up_bias,
    down_weight,
    norm_gains,
    shift_terms,
):
    groups = lax.axis_size("dp")
    chips = groups // 2
    tensors = lax.axis_size("tensor")
    s = lax.axis_index("section")
    t = lax.axis_index("tensor")
    seq = embedded.shape[3]
    rows = up_to(seq, 16)

    def of_section(value):
        return lax.dynamic_index_in_dim(value[:, 0, 0], s, 0, keepdims=False)

    slot = s * tensors + t
    inside = lax.broadcasted_iota(jnp.int32, (rows, 128), 0) < seq
    live = jnp.where(inside & (slot < image_counts[:, None]), 1.0, 0.0).astype(F32)

    piece = norm_gains.shape[2]
    ups = [up_bias[:, start : start + piece] for start in range(0, 4 * piece, piece)]
    packed = jnp.concatenate([norm_gains[0], shift_terms[0], qv_bias[0], *ups])
    packed = jnp.pad(packed, ((0, 16 - packed.shape[0]), (0, 128 - packed.shape[1])))

    shards = (
        qkv_weight[0].transpose(1, 0, 2),
        out_weight[0].T,
        up_weight[0],
        down_weight[0].T,
    )
    out_all, vec, hs, mid, gq, go, gu, gd, *kept = forward(
        chips, rows, of_section(embedded), live, packed, *shards
    )
    vec_sum, sum_q, sum_o, sum_u, sum_d, gin_both, out_both = backward(
        chips,
        seq,
        jnp.pad(of_section(cotangent), ((0, rows - seq), (0, 0))),
        live,
        vec,
        out_all,
        hs,
        mid,
        (gq, go, gu, gd),
        kept,
    )
    return (
        out_both[None, :, None, None, :seq],
        gin_both[None, :, None, None, :seq],
        sum_q.transpose(1, 0, 2)[None],
        vec_sum[None, 6:8, :piece],
        sum_o.T[None],
        sum_u[None],
        vec_sum[8:12, :piece].reshape(1, 4 * piece),
        sum_d.T[None],
        vec_sum[None, 0:2, :piece],
        vec_sum[None, 2:6, :piece],
    )


def solution(mesh):
    placed = (
        P(None, "dp", "tensor", None, None),
        P("dp"),
        P(None, "dp", "tensor", None, None),
        P("section", "dp", None, "tensor"),
        P("section", None, ("tensor", "dp")),
        P("section", "tensor", "dp"),
        P("section", "dp", "tensor"),
        P("section", ("tensor", "dp")),
        P("section", "tensor", "dp"),
        P("section", None, ("tensor", "dp")),
        P("section", None, ("tensor", "dp")),
    )
    return jax.shard_map(
        body,
        mesh=mesh,
        in_specs=placed,
        out_specs=(
            P("section", None, "dp", "tensor", None, None),
            P("section", None, "dp", "tensor", None, None),
            P("section", "dp", None, "tensor"),
            P("section", None, ("tensor", "dp")),
            P("section", "tensor", "dp"),
            P("section", "dp", "tensor"),
            P("section", ("tensor", "dp")),
            P("section", "tensor", "dp"),
            P("section", None, ("tensor", "dp")),
            P("section", None, ("tensor", "dp")),
        ),
        check_vma=False,
    )
```
